128 devices in a mesh: seq: 16 (over z, y), grp: 8 (over x, core).
Axes of the slice: x: 4, y: 4, z: 4, core: 2. Of those that a mesh axis runs over, the one named last changes fastest.
Arguments:
- x_group: bfloat16 [4096, 2304], P('seq'), may hold values from -6 to 6
- decode_input: bfloat16 [3, 128, 2304], P(None, 'seq'), may hold values from -6 to 6
- prompt_len: int32 [128], P('seq'), may hold values from 1 to 768, as said below
- latent_pages: bfloat16 [16, 16, 6, 64, 576], P('seq'), may hold values from -6 to 6
- slot_target: int32 [16, 16, 6], P(None, 'seq'), may hold values from 0 to 95, as said below
- page_counts: int32 [16, 16], P(None, 'seq'), may hold values from 0 to 6, as said below
- kda_state: float32 [128, 32, 128, 128], P(None, 'grp', 'seq'), may hold values from -4 to 4
- query_proj: bfloat16 [2304, 6144], P(None, 'grp'), may hold values from -1 to 1
- latent_proj: bfloat16 [2304, 576], replicated, may hold values from -1 to 1
- key_expand: bfloat16 [512, 4096], P(None, 'grp'), may hold values from -1 to 1
- value_expand: bfloat16 [512, 4096], P(None, 'grp'), may hold values from -0.25 to 0.25
- mla_output: bfloat16 [4096, 2304], P('grp'), may hold values from -0.09375 to 0.09375
- kda_inputs: bfloat16 [2304, 3, 4096], P(None, None, 'grp'), may hold values from -0.125 to 0.125
- kda_beta: bfloat16 [2304, 32], P(None, 'grp'), may hold values from -0.125 to 0.125
- decay_down: bfloat16 [2304, 128], replicated, may hold values from -0.125 to 0.125
- decay_up: bfloat16 [128, 4096], P(None, 'grp'), may hold values from -0.5 to 0.5
- gate_down: bfloat16 [2304, 128], replicated, may hold values from -0.125 to 0.125
- gate_up: bfloat16 [128, 4096], P(None, 'grp'), may hold values from -0.5 to 0.5
- decay_log: float32 [32], P('grp'), may hold values from -2.5 to 0.5
- kda_output: bfloat16 [4096, 2304], P('grp'), may hold values from -0.09375 to 0.09375
Outputs:
- prefill_out: bfloat16 [4096, 2304], P('seq', 'grp')
- decode_out: bfloat16 [3, 128, 2304], P(None, 'seq', 'grp')
The draws below stay inside these ranges and needn't reach their ends.
Inputs may be any that keep to these rules, and one draw needn't show every extreme that they name: A request has ceil(prompt_len / 64) pages, at most 12; on one owner drawn from the seed all 8 requests have 12 pages. `slot_target`: entry k < page_counts[s, d] holds local request * 12 + page of owner d; every page of every request is held in exactly one slot; entries past the count are 0. `page_counts`: slots are filled from slot 0; the count 6 is reached on some pair in every draw.
All inputs are finite; a program needn't handle non-finite values.
Results may differ from the reference program's by a relative error of at most 0.02.
Values may be sent and summed in bfloat16 or wider, within the bound.
No kernel may reach another device: no remote copies, remote signals or barrier semaphores. Data moves between devices by JAX's collectives and lax.ppermute only.
A program may use at most 192 MiB of HBM per device.

```python
import jax
import jax.numpy as jnp
from jax import lax

D = 2304
HEADS = 32
LAT = 512
ROPE = 64
NOPE = 128
VH = 128
KH = 32
DK = 128
DV = 128
REQ_DEV = 8
PAGE = 64
MAXP = 12
STEPS = 3
GROUP = 4096
REQUESTS = 128
CAP = 6
N_SEQ = 16


def handoff_plan(key):
    subkeys = jax.random.split(key, 4)
    owner_of = jnp.arange(REQUESTS) // REQ_DEV
    page_number = jax.random.randint(subkeys[0], (REQUESTS,), 1, MAXP + 1)
    fullest = jax.random.randint(subkeys[1], (), 0, N_SEQ)
    page_number = jnp.where(owner_of == fullest, MAXP, page_number)
    tails = jax.random.randint(subkeys[2], (REQUESTS,), 1, PAGE + 1)
    lengths = (page_number - 1) * PAGE + tails
    grid_pages = page_number.reshape(N_SEQ, REQ_DEV)
    starts = jnp.cumsum(grid_pages, axis=1) - grid_pages
    page_index = jnp.arange(MAXP)
    ordinal = starts[:, :, None] + page_index[None, None, :]
    valid = page_index[None, None, :] < grid_pages[:, :, None]
    orders = jax.vmap(lambda single: jax.random.permutation(single, N_SEQ))(jax.random.split(subkeys[3], N_SEQ))
    source = jnp.take_along_axis(orders, (ordinal % N_SEQ).reshape(N_SEQ, -1), axis=1).reshape(ordinal.shape)
    source = jnp.where(valid, source, N_SEQ)
    slot = ordinal // N_SEQ
    target = jnp.broadcast_to(jnp.arange(REQ_DEV)[None, :, None] * MAXP + page_index[None, None, :], ordinal.shape)
    owner = jnp.broadcast_to(jnp.arange(N_SEQ)[:, None, None], ordinal.shape)
    slot_target = jnp.zeros((N_SEQ, N_SEQ, CAP), jnp.int32).at[source, owner, slot].set(target.astype(jnp.int32), mode='drop')
    page_counts = jnp.zeros((N_SEQ, N_SEQ), jnp.int32).at[source, owner].add(jnp.ones(ordinal.shape, jnp.int32), mode='drop')
    return (lengths.astype(jnp.int32), slot_target, page_counts)


def draw_prompt_len(key, part):
    return handoff_plan(key)[0]


def draw_slot_target(key, part):
    return handoff_plan(key)[1]


def draw_page_counts(key, part):
    return handoff_plan(key)[2]


def draw_x_group(key, part):
    key = jax.random.fold_in(key, 21)
    shape = (GROUP, D)
    values = jnp.clip(jax.random.normal(key, shape), -6.0, 6.0)
    return values.astype(jnp.bfloat16)


def draw_decode_input(key, part):
    key = jax.random.fold_in(key, 22)
    shape = (STEPS, REQUESTS, D)
    values = jnp.clip(jax.random.normal(key, shape), -6.0, 6.0)
    return values.astype(jnp.bfloat16)


def draw_latent_pages(key, part):
    key = jax.random.fold_in(key, 23)
    shape = (N_SEQ, N_SEQ, CAP, PAGE, LAT + ROPE)
    values = jnp.clip(jax.random.normal(key, shape), -6.0, 6.0)
    return values.astype(jnp.bfloat16)


def draw_query_proj(key, part):
    key = jax.random.fold_in(key, 24)
    head_width = NOPE + ROPE
    values = jnp.clip(jax.random.normal(key, (D, HEADS, head_width)), -4.0, 4.0) * D ** (-0.5)
    return values.reshape(D, HEADS * head_width).astype(jnp.bfloat16)


def draw_latent_proj(key, part):
    key = jax.random.fold_in(key, 25)
    values = jnp.clip(jax.random.normal(key, (D, LAT + ROPE)), -4.0, 4.0) * D ** (-0.5)
    return values.astype(jnp.bfloat16)


def draw_key_expand(key, part):
    key = jax.random.fold_in(key, 26)
    values = jnp.clip(jax.random.normal(key, (LAT, HEADS, NOPE)), -4.0, 4.0) * LAT ** (-0.5)
    return values.reshape(LAT, HEADS * NOPE).astype(jnp.bfloat16)


def steps_of(rng, shape, cuts, smallest, largest):
    def one(axis_at, shards_of):
        steps = jax.random.uniform(jax.random.fold_in(jax.random.fold_in(rng, 6), axis_at), (shards_of,), jnp.float32, smallest / len(cuts), largest / len(cuts))
        return jnp.repeat(jnp.exp(steps), shape[axis_at] // shards_of).reshape((-1,) + (1,) * (len(shape) - axis_at - 1))

    loudness = one(*cuts[0])
    for cut in cuts[1:]:
        loudness = loudness * one(*cut)
    return loudness


def noise(own_key, extent, spread, limit, cuts=(), held_as=jnp.bfloat16):
    factor_of = steps_of(own_key, extent, cuts, -0.22, 0.18) if cuts else 1.0
    drawn = jax.random.normal(own_key, extent, jnp.float32) * spread * factor_of
    return jnp.minimum(jnp.maximum(drawn, -limit), limit).astype(held_as)


def setup_inputs(seed: int = 0) -> dict:
    key_of = jax.random.split(jax.random.key(seed), 21)
    return {
        "x_group": draw_x_group(jax.random.fold_in(key_of[20], 71), 0),
        "decode_input": draw_decode_input(jax.random.fold_in(key_of[20], 71), 0),
        "prompt_len": draw_prompt_len(jax.random.fold_in(key_of[20], 71), 0),
        "latent_pages": draw_latent_pages(jax.random.fold_in(key_of[20], 71), 0),
        "slot_target": draw_slot_target(jax.random.fold_in(key_of[20], 71), 0),
        "page_counts": draw_page_counts(jax.random.fold_in(key_of[20], 71), 0),
        "kda_state": noise(key_of[6], (REQUESTS, KH, DV, DK), 0.5, 4.0, ((1, 8), (2, 16)), jnp.float32),
        "query_proj": draw_query_proj(jax.random.fold_in(key_of[20], 71), 0),
        "latent_proj": draw_latent_proj(jax.random.fold_in(key_of[20], 71), 0),
        "key_expand": draw_key_expand(jax.random.fold_in(key_of[20], 71), 0),
        "value_expand": noise(key_of[10], (LAT, HEADS * VH), LAT ** -0.5, 0.25, ((1, 8),)),
        "mla_output": noise(key_of[11], (HEADS * VH, D), (HEADS * VH) ** -0.5, 0.09375, ((0, 8),)),
        "kda_inputs": noise(key_of[12], (D, 3, KH * DK), D ** -0.5, 0.125, ((2, 8),)),
        "kda_beta": noise(key_of[13], (D, KH), D ** -0.5, 0.125, ((1, 8),)),
        "decay_down": noise(key_of[14], (D, DK), D ** -0.5, 0.125),
        "decay_up": noise(key_of[15], (DK, KH * DK), DK ** -0.5, 0.5, ((1, 8),)),
        "gate_down": noise(key_of[16], (D, DK), D ** -0.5, 0.125),
        "gate_up": noise(key_of[17], (DK, KH * DV), DK ** -0.5, 0.5, ((1, 8),)),
        "decay_log": jnp.clip(-2.5 + 3.0 * jax.random.uniform(key_of[18], (KH,), jnp.float32) ** steps_of(key_of[18], (KH,), ((0, 8),), -0.2, 0.2), -2.5, 0.5),
        "kda_output": noise(key_of[19], (KH * DV, D), (KH * DV) ** -0.5, 0.09375, ((0, 8),)),
    }


epsilon = 1e-06
masked_score = -1e+30

def norm_rows(values):
    return values * lax.rsqrt(lax.optimization_barrier(jnp.mean(values * values, axis=-1, keepdims=True)) + epsilon)

def unit_rows(values):
    return values * lax.rsqrt(lax.optimization_barrier(jnp.sum(values * values, axis=-1, keepdims=True)) + epsilon)

def rotate(values, position):
    halfway = values.shape[-1] // 2
    frequency = jnp.exp(-jnp.log(10000.0) * jnp.arange(halfway, dtype=jnp.float32) / halfway)
    angles = position.astype(jnp.float32)[..., None] * frequency
    leading = values[..., :halfway]
    trailing = values[..., halfway:]
    return jnp.concatenate([leading * jnp.cos(angles) - trailing * jnp.sin(angles), leading * jnp.sin(angles) + trailing * jnp.cos(angles)], axis=-1)

def make_latent(normed, latent_proj, position):
    projected = jnp.dot(normed, latent_proj, preferred_element_type=jnp.float32)
    return jnp.concatenate([norm_rows(projected[:, :LAT]), rotate(projected[:, LAT:], position)], axis=-1).astype(jnp.bfloat16)

def make_query(normed, query_proj, position):
    head_count = query_proj.shape[1] // (NOPE + ROPE)
    projected = jnp.dot(normed, query_proj, preferred_element_type=jnp.float32).reshape(normed.shape[0], head_count, NOPE + ROPE)
    return (projected[..., :NOPE].astype(jnp.bfloat16), rotate(projected[..., NOPE:], position[:, None]).astype(jnp.bfloat16))

def absorb(q_nope, q_rope, key_expand):
    head_count = q_nope.shape[1]
    latent_query = jnp.einsum('rhn,chn->rhc', q_nope.astype(jnp.float32), key_expand.reshape(LAT, head_count, NOPE).astype(jnp.float32))
    return jnp.concatenate([latent_query.astype(jnp.bfloat16), q_rope], axis=-1)

def partial_attend(queries, key_rows, live_mask):
    scores = jnp.einsum('rhc,kc->rhk', queries.astype(jnp.float32), key_rows.astype(jnp.float32)) * (NOPE + ROPE) ** (-0.5)
    scores = jnp.where(live_mask[:, None, :], scores, masked_score)
    highest = lax.optimization_barrier(jnp.max(scores, axis=-1))
    weights = jnp.where(live_mask[:, None, :], jnp.exp(scores - highest[..., None]), 0.0)
    totals = lax.optimization_barrier(jnp.sum(weights, axis=-1))
    summed = jnp.einsum('rhk,kc->rhc', weights.astype(jnp.bfloat16).astype(jnp.float32), key_rows[:, :LAT].astype(jnp.float32))
    return (highest, totals, summed)

def cache_mask(target, counts, lengths, offset, width):
    slot_live = jnp.arange(target.shape[1])[None, :] < counts[:, None]
    request = target // MAXP
    token_pos = (target % MAXP)[..., None] * PAGE + offset + jnp.arange(width)[None, None, :]
    owners = jnp.arange(lengths.shape[0])[:, None, None, None]
    live = slot_live[None, :, :, None] & (request[None, :, :, None] == owners) & (token_pos[None] < lengths[:, None, None, None])
    return live.reshape(lengths.shape[0], -1)

def prefill(x_group, query_proj, latent_proj, key_expand, value_expand, mla_output):
    rows_in = x_group.astype(jnp.float32)
    normed = norm_rows(rows_in).astype(jnp.bfloat16)
    group_rows = x_group.shape[0]
    position = jnp.arange(group_rows)
    q_nope, q_rope = make_query(normed, query_proj, position)
    latent = make_latent(normed, latent_proj, position)
    k_nope = jnp.dot(latent[:, :LAT], key_expand, preferred_element_type=jnp.float32).astype(jnp.bfloat16).reshape(group_rows, HEADS, NOPE)
    values = jnp.dot(latent[:, :LAT], value_expand, preferred_element_type=jnp.float32).astype(jnp.bfloat16).reshape(group_rows, HEADS, VH)
    causal = position[None, :] <= position[:, None]
    rope_keys = latent[:, LAT:]

    def one_head(inputs):
        head_nope, head_rope, head_keys, head_values = inputs
        scores = (jnp.dot(head_nope, head_keys.T, preferred_element_type=jnp.float32) + jnp.dot(head_rope, rope_keys.T, preferred_element_type=jnp.float32)) * (NOPE + ROPE) ** (-0.5)
        scores = jnp.where(causal, scores, masked_score)
        highest = lax.optimization_barrier(jnp.max(scores, axis=-1))
        weights = jnp.where(causal, jnp.exp(scores - highest[:, None]), 0.0)
        totals = lax.optimization_barrier(jnp.sum(weights, axis=-1))
        summed = jnp.dot(weights.astype(jnp.bfloat16), head_values, preferred_element_type=jnp.float32)
        return (summed / totals[:, None]).astype(jnp.bfloat16)
    heads_out = lax.map(one_head, (q_nope.transpose(1, 0, 2), q_rope.transpose(1, 0, 2), k_nope.transpose(1, 0, 2), values.transpose(1, 0, 2)))
    flat = heads_out.transpose(1, 0, 2).reshape(group_rows, HEADS * VH)
    return (rows_in + jnp.dot(flat, mla_output, preferred_element_type=jnp.float32)).astype(jnp.bfloat16)

def reference(x_group, decode_input, prompt_len, latent_pages, slot_target, page_counts, kda_state, query_proj, latent_proj, key_expand, value_expand, mla_output, kda_inputs, kda_beta, decay_down, decay_up, gate_down, gate_up, decay_log, kda_output):
    prefill_out = prefill(x_group, query_proj, latent_proj, key_expand, value_expand, mla_output)
    rows_in = decode_input.astype(jnp.float32)
    dec_normed = norm_rows(rows_in).astype(jnp.bfloat16)
    query_list = []
    fresh_list = []
    for step_index in range(STEPS):
        place = prompt_len + step_index
        q_nope, q_rope = make_query(dec_normed[step_index], query_proj, place)
        query_list.append(absorb(q_nope, q_rope, key_expand))
        fresh_list.append(make_latent(dec_normed[step_index], latent_proj, place))
    queries = jnp.stack(query_list).reshape(STEPS, N_SEQ, REQ_DEV, HEADS, LAT + ROPE).transpose(1, 0, 2, 3, 4)
    fresh_all = jnp.stack(fresh_list).reshape(STEPS, N_SEQ, REQ_DEV, LAT + ROPE).transpose(1, 0, 2, 3)
    cache_all = latent_pages.transpose(1, 0, 2, 3, 4).reshape(N_SEQ, N_SEQ * CAP * PAGE, LAT + ROPE)

    def owner_attend(inputs):
        key_rows, target, counts, lengths, owner_queries, fresh_keys = inputs
        live = cache_mask(target, counts, lengths, 0, PAGE)
        results = []
        for step_index in range(STEPS):
            new_keys = fresh_keys[:step_index + 1].reshape(-1, LAT + ROPE)
            new_live = (jnp.arange(new_keys.shape[0]) % REQ_DEV)[None, :] == jnp.arange(REQ_DEV)[:, None]
            highest, totals, summed = partial_attend(owner_queries[step_index], jnp.concatenate([key_rows, new_keys], axis=0), jnp.concatenate([live, new_live], axis=1))
            results.append((summed / totals[..., None]).astype(jnp.bfloat16))
        return jnp.stack(results)
    latent_outs = lax.map(owner_attend, (cache_all, slot_target.transpose(1, 0, 2), page_counts.T, prompt_len.reshape(N_SEQ, REQ_DEV), queries, fresh_all))
    latent_outs = latent_outs.transpose(1, 0, 2, 3, 4).reshape(STEPS, REQUESTS, HEADS, LAT)
    states = kda_state.astype(jnp.float32)
    outputs = []
    for step_index in range(STEPS):
        head_values = jnp.einsum('rhc,chv->rhv', latent_outs[step_index].astype(jnp.float32), value_expand.reshape(LAT, HEADS, VH).astype(jnp.float32)).astype(jnp.bfloat16)
        hidden = rows_in[step_index] + jnp.dot(head_values.reshape(REQUESTS, HEADS * VH), mla_output, preferred_element_type=jnp.float32)
        kda_in = norm_rows(hidden).astype(jnp.bfloat16)
        projected = jnp.dot(kda_in, kda_inputs.reshape(D, 3 * KH * DK), preferred_element_type=jnp.float32).reshape(REQUESTS, 3, KH, DK)
        queries_kda = unit_rows(projected[:, 0]) * DK ** (-0.5)
        keys_kda = unit_rows(projected[:, 1])
        values_kda = projected[:, 2]
        write_rate = jax.nn.sigmoid(jnp.dot(kda_in, kda_beta, preferred_element_type=jnp.float32))
        decay_low = jnp.dot(kda_in, decay_down, preferred_element_type=jnp.float32).astype(jnp.bfloat16)
        decays = jnp.exp(-jnp.exp(decay_log)[None, :, None] * jax.nn.softplus(jnp.dot(decay_low, decay_up, preferred_element_type=jnp.float32).reshape(REQUESTS, KH, DK)))
        gate_low = jnp.dot(kda_in, gate_down, preferred_element_type=jnp.float32).astype(jnp.bfloat16)
        out_gate = jax.nn.sigmoid(jnp.dot(gate_low, gate_up, preferred_element_type=jnp.float32).reshape(REQUESTS, KH, DV))
        states = states * decays[:, :, None, :]
        errors = values_kda - lax.optimization_barrier(jnp.sum(states * keys_kda[:, :, None, :], axis=-1))
        states = states + write_rate[..., None, None] * errors[..., None] * keys_kda[:, :, None, :]
        readout = lax.optimization_barrier(jnp.sum(states * queries_kda[:, :, None, :], axis=-1))
        blended = (norm_rows(readout) * out_gate).astype(jnp.bfloat16).reshape(REQUESTS, KH * DV)
        outputs.append((hidden + jnp.dot(blended, kda_output, preferred_element_type=jnp.float32)).astype(jnp.bfloat16))
    return (prefill_out, jnp.stack(outputs))
```

```python
import functools

import jax
import jax.numpy as jnp
from jax import lax
from jax.experimental import pallas as pl
from jax.experimental.pallas import tpu as pltpu
from jax.sharding import PartitionSpec as P

LAT = 512
ROPE = 64
NOPE = 128
VH = 128
DK = 128
DV = 128
PAGE = 64
MAXP = 12
WIDE = LAT + ROPE
SENT = LAT + 128

epsilon = 1e-06
masked_score = -1e30
scale = (NOPE + ROPE) ** (-0.5)
log2e = 1.4426950408889634

f32 = jnp.float32
bf16 = jnp.bfloat16
MIB = 1024 * 1024


def params(mib):
    return pltpu.CompilerParams(vmem_limit_bytes=mib * MIB)


def dot_nt(a, b):
    return lax.dot_general(a, b, (((1,), (1,)), ((), ())), preferred_element_type=f32)


def dot_nn(a, b):
    return lax.dot_general(a, b, (((1,), (0,)), ((), ())), preferred_element_type=f32)


def norm_rows(values):
    return values * lax.rsqrt(jnp.mean(values * values, axis=-1, keepdims=True) + epsilon)


def unit_rows(values):
    return values * lax.rsqrt(jnp.sum(values * values, axis=-1, keepdims=True) + epsilon)


def turn(values, cos, sin):
    half = ROPE // 2
    swapped = jnp.concatenate([values[:, half:], values[:, :half]], axis=-1)
    return values * cos + swapped * sin


def rope_tables(position):
    half = ROPE // 2
    frequency = jnp.exp(-jnp.log(10000.0) * jnp.arange(half, dtype=f32) / half)
    angles = position.astype(f32)[:, None] * frequency
    cos, sin = jnp.cos(angles), jnp.sin(angles)
    return jnp.concatenate([cos, cos], axis=-1), jnp.concatenate([-sin, sin], axis=-1)


def latent_kernel(x_ref, dec_ref, proj_ref, cos_ref, sin_ref, normed_ref, lat_ref, fresh_ref):
    rows = x_ref.shape[0]
    normed = jnp.concatenate(
        [norm_rows(x_ref[...].astype(f32)), norm_rows(dec_ref[...].astype(f32))], axis=0
    ).astype(bf16)
    normed_ref[...] = normed
    projected = dot_nt(normed, proj_ref[...])
    latent = jnp.concatenate(
        [norm_rows(projected[:, :LAT]), turn(projected[:, LAT:], cos_ref[...], sin_ref[...])],
        axis=-1,
    )
    lat_ref[...] = latent[:rows].astype(bf16)
    fresh = latent[rows:]
    extra = jnp.zeros((fresh_ref.shape[0] - fresh.shape[0], WIDE), f32)
    fresh_ref[...] = jnp.concatenate([fresh, extra], axis=0).astype(bf16)


def make_latents(x, dec, proj_t, cos, sin):
    rows, width = x.shape
    total = rows + dec.shape[0]
    return pl.pallas_call(
        latent_kernel,
        out_shape=(
            jax.ShapeDtypeStruct((total, width), bf16),
            jax.ShapeDtypeStruct((rows, WIDE), bf16),
            jax.ShapeDtypeStruct((32, WIDE), bf16),
        ),
        compiler_params=params(40),
    )(x, dec, proj_t, cos, sin)


def query_kernel(heads, rows, normed_ref, proj_ref, cos_ref, sin_ref, expand_ref, qp_ref, qd_ref, acc):
    step = pl.program_id(0)

    @pl.when(step == 0)
    def _():
        acc[...] = jnp.zeros_like(acc)

    acc[...] += dot_nn(normed_ref[...], proj_ref[...])

    @pl.when(step == pl.num_programs(0) - 1)
    def _():
        cos, sin = cos_ref[...], sin_ref[...]
        decode = []
        for head in range(heads):
            at = head * (NOPE + ROPE)
            nope = acc[:, at : at + NOPE]
            turned = turn(acc[:, at + NOPE : at + NOPE + ROPE], cos, sin)
            qp_ref[head] = jnp.concatenate([nope[:rows], turned[:rows]], axis=-1).astype(bf16)
            absorbed = dot_nt(
                nope[rows:].astype(bf16), expand_ref[:, head * NOPE : (head + 1) * NOPE]
            )
            decode.append(jnp.concatenate([absorbed, turned[rows:]], axis=-1))
        qd_ref[...] = jnp.concatenate(decode, axis=0).astype(bf16)


def make_queries(normed, rows, query_proj, cos, sin, key_expand):
    total, width = normed.shape
    heads = key_expand.shape[1] // NOPE
    parts = 3
    depth = width // parts
    columns = query_proj.shape[1]
    whole = lambda shape: pl.BlockSpec(shape, lambda i: (0,) * len(shape))
    return pl.pallas_call(
        functools.partial(query_kernel, heads, rows),
        grid=(parts,),
        in_specs=[
            pl.BlockSpec((total, depth), lambda i: (0, i)),
            pl.BlockSpec((depth, columns), lambda i: (i, 0)),
            whole(cos.shape),
            whole(sin.shape),
            whole(key_expand.shape),
        ],
        out_specs=(
            whole((heads, rows, NOPE + ROPE)),
            whole((heads * (total - rows), WIDE)),
        ),
        out_shape=(
            jax.ShapeDtypeStruct((heads, rows, NOPE + ROPE), bf16),
            jax.ShapeDtypeStruct((heads * (total - rows), WIDE), bf16),
        ),
        scratch_shapes=[pltpu.VMEM((total, columns), f32)],
        compiler_params=params(40),
    )(normed, query_proj, cos, sin, key_expand)


def flash_kernel(
    heads,
    block,
    place_ref,
    q_ref,
    lat_ref,
    ke_ref,
    vet_ref,
    out_ref,
    sum_ref,
    peak,
    total,
    acc,
):
    step = pl.program_id(0)
    rows = q_ref.shape[1]
    first = place_ref[0]

    @pl.when(step == 0)
    def _():
        peak[...] = jnp.full_like(peak, masked_score)
        total[...] = jnp.zeros_like(total)
        acc[...] = jnp.zeros_like(acc)

    def work(masked):
        lat = lat_ref[...]
        keys = dot_nn(lat[:, :LAT], ke_ref[...]).astype(bf16)
        values = dot_nt(vet_ref[...], lat[:, :LAT]).astype(bf16)
        if masked:
            key_pos = step * block + lax.broadcasted_iota(jnp.int32, (block, rows), 0)
            live = key_pos <= first + lax.broadcasted_iota(jnp.int32, (block, rows), 1)
        for head in range(heads):
            whole_keys = jnp.concatenate(
                [keys[:, head * NOPE : (head + 1) * NOPE], lat[:, LAT:]], axis=-1
            )
            scores = dot_nt(whole_keys, q_ref[head]) * (scale * log2e)
            if masked:
                scores = jnp.where(live, scores, masked_score)
            old = peak[head]
            new = jnp.maximum(old, jnp.max(scores, axis=0, keepdims=True))
            fade = jnp.exp2(old - new)
            weights = jnp.exp2(scores - new)
            peak[head] = new
            total[head] = total[head] * fade + jnp.sum(weights, axis=0, keepdims=True)
            acc[head] = acc[head] * fade + dot_nn(
                values[head * VH : (head + 1) * VH], weights.astype(bf16)
            )

    @pl.when((step + 1) * block <= first + 1)
    def _():
        work(False)

    @pl.when(((step + 1) * block > first + 1) & (step * block < first + rows))
    def _():
        work(True)

    @pl.when(step == pl.num_programs(0) - 1)
    def _():
        mixed = jnp.concatenate([(acc[h] / total[h]).T for h in range(heads)], axis=-1)
        summed = dot_nn(mixed.astype(bf16), out_ref[...])
        sum_ref[...] = summed.T.astype(bf16)


def prefill_attend(place, q, lat_all, key_expand, value_expand_t, mla_output):
    heads, rows, _ = q.shape
    keys = lat_all.shape[0]
    block = min(512, keys)
    width = mla_output.shape[1]
    whole = lambda shape: pl.BlockSpec(shape, lambda i, s: (0,) * len(shape))
    return pl.pallas_call(
        functools.partial(flash_kernel, heads, block),
        grid_spec=pltpu.PrefetchScalarGridSpec(
            num_scalar_prefetch=1,
            grid=(keys // block,),
            in_specs=[
                whole(q.shape),
                pl.BlockSpec((block, WIDE), lambda i, s: (i, 0)),
                whole(key_expand.shape),
                whole(value_expand_t.shape),
                whole(mla_output.shape),
            ],
            out_specs=whole((width, rows)),
            scratch_shapes=[
                pltpu.VMEM((heads, 1, rows), f32),
                pltpu.VMEM((heads, 1, rows), f32),
                pltpu.VMEM((heads, VH, rows), f32),
            ],
        ),
        out_shape=jax.ShapeDtypeStruct((width, rows), bf16),
        compiler_params=params(56),
    )(place, q, lat_all, key_expand, value_expand_t, mla_output)


def pages_kernel(group, requests, first_ref, q_ref, keys_ref, fresh_ref, owner_ref, sent_ref):
    rows = q_ref.shape[0]
    q = q_ref[...]
    keys = keys_ref[...]
    fresh = fresh_ref[...]
    within = lax.rem(lax.broadcasted_iota(jnp.int32, (rows, 1), 0), group)
    request = lax.rem(within, requests)
    step = within // requests
    live_old = owner_ref[...] == request
    column = lax.broadcasted_iota(jnp.int32, (1, fresh.shape[0]), 1)
    fresh_request = lax.rem(column, requests)
    fresh_step = column // requests + first_ref[0] * group
    live_new = (fresh_request == request) & (fresh_step <= step)
    old = jnp.where(live_old, dot_nt(q, keys) * scale, masked_score)
    new = jnp.where(live_new, dot_nt(q, fresh) * scale, masked_score)
    highest = jnp.maximum(
        jnp.max(old, axis=-1, keepdims=True), jnp.max(new, axis=-1, keepdims=True)
    )
    w_old = jnp.where(live_old, jnp.exp(old - highest), 0.0)
    w_new = jnp.where(live_new, jnp.exp(new - highest), 0.0)
    total = jnp.sum(w_old, axis=-1, keepdims=True) + jnp.sum(w_new, axis=-1, keepdims=True)
    some = total > 0.0
    safe = jnp.where(some, total, 1.0)
    mixed = dot_nn(w_old.astype(bf16), keys[:, :LAT]) + dot_nn(w_new.astype(bf16), fresh[:, :LAT])
    mixed = mixed / safe
    level = jnp.where(some, highest + jnp.log(safe), masked_score)
    high = level.astype(bf16).astype(f32)
    middle = (level - high).astype(bf16).astype(f32)
    low = level - high - middle
    lane = lax.broadcasted_iota(jnp.int32, (rows, SENT - LAT), 1)
    tail = jnp.where(lane == 0, high, jnp.where(lane == 1, middle, jnp.where(lane == 2, low, 0.0)))
    sent_ref[...] = jnp.concatenate([mixed, tail], axis=-1).astype(bf16)


def pages_attend(first, q_all, keys, fresh, owner, group, requests):
    rows = q_all.shape[0]
    parts = 4
    block = rows // parts
    whole = lambda shape: pl.BlockSpec(shape, lambda i, s: (0,) * len(shape))
    return pl.pallas_call(
        functools.partial(pages_kernel, group, requests),
        grid_spec=pltpu.PrefetchScalarGridSpec(
            num_scalar_prefetch=1,
            grid=(parts,),
            in_specs=[
                pl.BlockSpec((block, WIDE), lambda i, s: (i, 0)),
                whole(keys.shape),
                whole(fresh.shape),
                whole(owner.shape),
            ],
            out_specs=pl.BlockSpec((block, SENT), lambda i, s: (i, 0)),
        ),
        out_shape=jax.ShapeDtypeStruct((rows, SENT), bf16),
        compiler_params=params(40),
    )(first, q_all, keys, fresh, owner)


def combine_kernel(heads, parts_ref, ve_ref, out_ref, sum_ref):
    tails = parts_ref[:, :, LAT:].astype(f32)
    lane = lax.broadcasted_iota(jnp.int32, tails.shape, 2)
    level = jnp.sum(jnp.where(lane < 3, tails, 0.0), axis=-1, keepdims=True)
    weights = jnp.exp(level - jnp.max(level, axis=0, keepdims=True))
    total = jnp.sum(weights, axis=0)
    mixed = jnp.sum(parts_ref[:, :, :LAT].astype(f32) * weights, axis=0) / total
    count = mixed.shape[0] // heads
    head_values = [
        dot_nn(
            mixed[h * count : (h + 1) * count].astype(bf16), ve_ref[:, h * VH : (h + 1) * VH]
        )
        for h in range(heads)
    ]
    joined = jnp.concatenate(head_values, axis=-1).astype(bf16)
    sum_ref[...] = dot_nn(joined, out_ref[...]).astype(bf16)


def combine(parts, value_expand, mla_output):
    heads = value_expand.shape[1] // VH
    return pl.pallas_call(
        functools.partial(combine_kernel, heads),
        out_shape=jax.ShapeDtypeStruct((parts.shape[1] // heads, mla_output.shape[1]), bf16),
        compiler_params=params(40),
    )(parts, value_expand, mla_output)


def kda_kernel(
    heads,
    requests,
    parts_ref,
    dec_ref,
    inputs_ref,
    beta_ref,
    decay_down_ref,
    decay_up_ref,
    gate_down_ref,
    gate_up_ref,
    rate_ref,
    states_ref,
    output_ref,
    hidden_ref,
    sum_ref,
    kin,
    projected,
):
    part = pl.program_id(0)
    shares, rows, share = hidden_ref.shape

    @pl.when(part == 0)
    def _():
        hidden = dec_ref[...].astype(f32) + jnp.sum(parts_ref[...].astype(f32), axis=0)
        for g in range(shares):
            hidden_ref[g] = hidden[:, g * share : (g + 1) * share]
        kin[...] = norm_rows(hidden).astype(bf16)

    projected[part] = dot_nn(kin[...], inputs_ref[0])

    @pl.when(part == pl.num_programs(0) - 1)
    def _():
        read_in = kin[...]
        beta = jax.nn.sigmoid(dot_nt(read_in, beta_ref[...]))
        decay_low = dot_nn(read_in, decay_down_ref[...]).astype(bf16)
        decays = jnp.exp(
            -rate_ref[...] * jax.nn.softplus(dot_nn(decay_low, decay_up_ref[...]))
        )
        gate_low = dot_nn(read_in, gate_down_ref[...]).astype(bf16)
        gates = jax.nn.sigmoid(dot_nn(gate_low, gate_up_ref[...]))
        steps = rows // requests
        at = lambda values, t: values[t * requests : (t + 1) * requests]
        along = lambda a, b: jnp.sum(a * b, axis=-1, keepdims=True)
        blended = []
        for head in range(heads):
            lanes = slice(head * DK, (head + 1) * DK)
            q = unit_rows(projected[0, :, lanes]) * DK ** (-0.5)
            k = unit_rows(projected[1, :, lanes])
            v = projected[2, :, lanes]
            a = decays[:, lanes]
            b = beta[:, head : head + 1]
            vectors = []
            held = None
            for t in range(steps):
                held = at(a, t) if held is None else held * at(a, t)
                vectors += [held * at(k, t), held * at(q, t)]
            vectors = jnp.concatenate(vectors, axis=0)
            high = vectors.astype(bf16)
            both = jnp.concatenate([high.astype(f32), vectors - high.astype(f32)], axis=0)
            owner = lax.rem(lax.broadcasted_iota(jnp.int32, (both.shape[0], 1), 0), requests)
            spread = jnp.concatenate(
                [jnp.where(owner == r, both, 0.0) for r in range(requests)], axis=-1
            ).astype(bf16)
            held_states = jnp.concatenate(
                [
                    states_ref[:, r, head].astype(f32).reshape(DV, DK)
                    for r in range(requests)
                ],
                axis=-1,
            ).astype(bf16)
            met = dot_nt(spread, held_states)
            met = met[: vectors.shape[0]] + met[vectors.shape[0] :]
            carried = []
            reads = []
            for t in range(steps):
                seen = at(met, 2 * t)
                read = at(met, 2 * t + 1)
                carried = [(u, w * at(a, t)) for u, w in carried]
                for u, w in carried:
                    seen = seen + u * along(w, at(k, t))
                u = at(b, t) * (at(v, t) - seen)
                carried.append((u, at(k, t)))
                for u, w in carried:
                    read = read + u * along(w, at(q, t))
                reads.append(read)
            read = jnp.concatenate(reads, axis=0)
            blended.append(norm_rows(read) * gates[:, lanes])
        mixed = jnp.concatenate(blended, axis=-1).astype(bf16)
        summed = dot_nn(mixed, output_ref[...])
        for g in range(shares):
            sum_ref[g] = summed[:, g * share : (g + 1) * share].astype(bf16)


def kda(parts, dec, inputs, beta_t, decay_down, decay_up, gate_down, gate_up, rate, states, output):
    shares, rows, width = parts.shape
    heads = beta_t.shape[0]
    requests = states.shape[1]
    columns = inputs.shape[2]
    whole = lambda a: pl.BlockSpec(a.shape, lambda i: (0,) * len(a.shape))
    share_spec = pl.BlockSpec((shares, rows, width // shares), lambda i: (0, 0, 0))
    return pl.pallas_call(
        functools.partial(kda_kernel, heads, requests),
        grid=(3,),
        in_specs=[
            whole(parts),
            whole(dec),
            pl.BlockSpec((1, width, columns), lambda i: (i, 0, 0)),
            whole(beta_t),
            whole(decay_down),
            whole(decay_up),
            whole(gate_down),
            whole(gate_up),
            whole(rate),
            whole(states),
            whole(output),
        ],
        out_specs=(share_spec, share_spec),
        out_shape=(
            jax.ShapeDtypeStruct((shares, rows, width // shares), f32),
            jax.ShapeDtypeStruct((shares, rows, width // shares), bf16),
        ),
        scratch_shapes=[pltpu.VMEM((rows, width), bf16), pltpu.VMEM((3, rows, columns), f32)],
        compiler_params=params(48),
    )(parts, dec, inputs, beta_t, decay_down, decay_up, gate_down, gate_up, rate, states, output)


def shards(
    x_group,
    decode_input,
    prompt_len,
    latent_pages,
    slot_target,
    page_counts,
    kda_state,
    query_proj,
    latent_proj,
    key_expand,
    value_expand,
    mla_output,
    kda_inputs,
    kda_beta,
    decay_down,
    decay_up,
    gate_down,
    gate_up,
    decay_log,
    kda_output,
):
    seq_index = lax.axis_index("seq")
    grp_index = lax.axis_index("grp")
    seq_size = lax.axis_size("seq")
    grp_size = lax.axis_size("grp")
    rows, width = x_group.shape
    steps, requests, _ = decode_input.shape
    decode_rows = steps * requests
    share = width // grp_size
    first_row = seq_index * rows
    place = jnp.concatenate(
        [first_row + jnp.arange(rows)]
        + [prompt_len + t for t in range(steps)]
    )
    cos, sin = rope_tables(place)
    dec = decode_input.reshape(decode_rows, width)

    normed, own_latent, fresh = make_latents(x_group, dec, latent_proj.T, cos, sin)
    lat_all = lax.all_gather(own_latent, "seq", axis=0, tiled=True)

    tokens = PAGE // grp_size
    own_tokens = lax.dynamic_slice_in_dim(latent_pages[0], grp_index * tokens, tokens, 2)
    arrived = lax.all_to_all(own_tokens, "seq", split_axis=0, concat_axis=0, tiled=True)
    slots = arrived.shape[1]
    page_keys = arrived.reshape(seq_size * slots * tokens, WIDE)
    target = slot_target[:, 0, :]
    owner = target // MAXP
    lengths = jnp.sum(
        jnp.where(owner[..., None] == jnp.arange(requests), prompt_len, 0), axis=-1
    )
    held = jnp.arange(slots)[None, :] < page_counts
    token_pos = (
        ((target % MAXP) * PAGE + grp_index * tokens)[..., None] + jnp.arange(tokens)
    )
    key_owner = jnp.where(
        held[..., None] & (token_pos < lengths[..., None]), owner[..., None], -1
    ).reshape(1, -1)

    states = lax.all_to_all(
        kda_state.astype(bf16), "seq", split_axis=0, concat_axis=0, tiled=True
    ).reshape((seq_size, requests) + kda_state.shape[1:])

    q_prefill, q_decode = make_queries(normed, rows, query_proj, cos, sin, key_expand)
    q_all = lax.all_gather(q_decode, "grp", axis=0, tiled=True)
    partial = pages_attend(
        grp_index.astype(jnp.int32).reshape(1), q_all, page_keys, fresh, key_owner, decode_rows, requests
    )
    partial = lax.all_to_all(
        partial.reshape(grp_size, -1, SENT), "grp", split_axis=0, concat_axis=0, tiled=True
    )
    mla_part = combine(partial, value_expand, mla_output)
    mla_parts = lax.all_gather(mla_part, "grp", axis=0, tiled=False)
    hidden, kda_part = kda(
        mla_parts,
        dec,
        kda_inputs.transpose(1, 0, 2),
        kda_beta.T,
        decay_down,
        decay_up,
        gate_down,
        gate_up,
        jnp.repeat(jnp.exp(decay_log), DK)[None, :],
        states,
        kda_output,
    )
    kda_parts = lax.all_to_all(kda_part, "grp", split_axis=0, concat_axis=0, tiled=True)
    hidden_share = lax.dynamic_index_in_dim(hidden, grp_index, 0, keepdims=False)
    decode_out = (hidden_share + jnp.sum(kda_parts.astype(f32), axis=0)).astype(bf16)

    prefill_part = prefill_attend(
        first_row.astype(jnp.int32).reshape(1),
        q_prefill,
        lat_all,
        key_expand,
        value_expand.T,
        mla_output,
    )
    prefill_parts = lax.all_to_all(
        prefill_part.reshape(grp_size, share, rows), "grp", split_axis=0, concat_axis=0, tiled=True
    )
    own_columns = lax.dynamic_slice_in_dim(x_group, grp_index * share, share, 1).T
    prefill_out = (
        own_columns.astype(f32) + jnp.sum(prefill_parts.astype(f32), axis=0)
    ).astype(bf16).T
    return (prefill_out, decode_out.reshape(steps, requests, share))


def solution(mesh):
    in_specs = (
        P("seq", None),
        P(None, "seq", None),
        P("seq"),
        P("seq", None, None, None, None),
        P(None, "seq", None),
        P(None, "seq"),
        P(None, "grp", "seq", None),
        P(None, "grp"),
        P(),
        P(None, "grp"),
        P(None, "grp"),
        P("grp", None),
        P(None, None, "grp"),
        P(None, "grp"),
        P(),
        P(None, "grp"),
        P(),
        P(None, "grp"),
        P("grp"),
        P("grp", None),
    )
    out_specs = (P("seq", "grp"), P(None, "seq", "grp"))
    return jax.shard_map(shards, mesh=mesh, in_specs=in_specs, out_specs=out_specs, check_vma=False)
```

```python
import functools

import jax
import jax.numpy as jnp
import numpy as np
from jax import lax
from jax.experimental import pallas as pl
from jax.experimental.pallas import tpu as pltpu
from jax.sharding import PartitionSpec as P

LAT = 512
ROPE = 64
NOPE = 128
VH = 128
DK = 128
DV = 128
PAGE = 64
MAXP = 12
WIDE = LAT + ROPE
SENT = LAT + 128

epsilon = 1e-06
masked_score = -1e30
scale = (NOPE + ROPE) ** (-0.5)
log2e = 1.4426950408889634

f32 = jnp.float32
bf16 = jnp.bfloat16
MIB = 1024 * 1024


def params(mib):
    return pltpu.CompilerParams(vmem_limit_bytes=mib * MIB)


def dot_nt(a, b):
    return lax.dot_general(a, b, (((1,), (1,)), ((), ())), preferred_element_type=f32)


def dot_nn(a, b):
    return lax.dot_general(a, b, (((1,), (0,)), ((), ())), preferred_element_type=f32)


def norm_rows(values):
    return values * lax.rsqrt(jnp.mean(values * values, axis=-1, keepdims=True) + epsilon)


def unit_rows(values):
    return values * lax.rsqrt(jnp.sum(values * values, axis=-1, keepdims=True) + epsilon)


def turn(values, cos, sin):
    half = ROPE // 2
    swapped = jnp.concatenate([values[:, half:], values[:, :half]], axis=-1)
    return values * cos + swapped * sin


def rope_tables(positions):
    half = ROPE // 2
    frequency = np.exp(-np.log(10000.0) * np.arange(half) / half)
    angles = np.asarray(positions, np.float64)[:, None] * frequency
    cos, sin = np.cos(angles), np.sin(angles)
    both = np.stack([np.concatenate([cos, cos], -1), np.concatenate([-sin, sin], -1)])
    return jnp.asarray(both, f32)


def front_kernel(
    place_ref,
    lengths_ref,
    fine_ref,
    coarse_ref,
    x_hbm,
    dec_hbm,
    lat_proj_hbm,
    query_proj_hbm,
    expand_hbm,
    pages_hbm,
    lat_ref,
    fresh_ref,
    qp_ref,
    qd_ref,
    own_hbm,
    x_ref,
    dec_ref,
    lat_proj_ref,
    query_proj_ref,
    expand_ref,
    normed,
    turns,
    sems,
):
    seq, grp = place_ref[0], place_ref[1]
    rows, width = x_ref.shape
    count = dec_ref.shape[0]
    half_rows = lat_ref.shape[0]
    core = lax.rem(grp, 2)
    _, slots, tokens, _ = own_hbm.shape
    heads = qp_ref.shape[0]
    requests = lengths_ref.shape[0]
    chunks = 3
    depth = width // chunks
    loads = [
        pltpu.make_async_copy(x_hbm, x_ref, sems.at[0]),
        pltpu.make_async_copy(dec_hbm, dec_ref, sems.at[1]),
        pltpu.make_async_copy(lat_proj_hbm, lat_proj_ref, sems.at[2]),
        pltpu.make_async_copy(expand_hbm, expand_ref, sems.at[3]),
    ]
    loads += [
        pltpu.make_async_copy(
            query_proj_hbm.at[pl.ds(i * depth, depth)],
            query_proj_ref.at[pl.ds(i * depth, depth)],
            sems.at[4 + i],
        )
        for i in range(chunks)
    ]
    pages = pltpu.make_async_copy(
        pages_hbm.at[:, pl.ds(core * slots, slots), pl.ds((grp // 2) * tokens, tokens), :],
        own_hbm,
        sems.at[4 + chunks],
    )
    for load in loads:
        load.start()
    pages.start()
    for r in range(requests):
        for t in range(count // requests):
            at = rows + t * requests + r
            row = lengths_ref[r] + t
            turns[0, at : at + 1] = fine_ref[0, pl.ds(row, 1)]
            turns[1, at : at + 1] = fine_ref[1, pl.ds(row, 1)]
    turns[:, rows + count :] = jnp.zeros((2, turns.shape[1] - rows - count, ROPE), f32)
    base_cos, base_sin = coarse_ref[0, pl.ds(seq, 1)], coarse_ref[1, pl.ds(seq, 1)]
    fine_cos, fine_sin = fine_ref[0, :rows], fine_ref[1, :rows]
    turns[0, :rows] = base_cos * fine_cos - base_sin * fine_sin
    turns[1, :rows] = base_sin * fine_cos + base_cos * fine_sin
    loads[0].wait()
    normed[:rows] = norm_rows(x_ref[...].astype(f32)).astype(bf16)
    loads[1].wait()
    tail = normed.shape[0] - rows - count
    normed[rows:] = jnp.concatenate(
        [norm_rows(dec_ref[...].astype(f32)), jnp.zeros((tail, width), f32)], axis=0
    ).astype(bf16)
    loads[2].wait()

    def latents(inputs, cos, sin):
        projected = dot_nt(inputs, lat_proj_ref[...])
        return jnp.concatenate(
            [norm_rows(projected[:, :LAT]), turn(projected[:, LAT:], cos, sin)], axis=-1
        ).astype(bf16)

    own = pl.ds(pl.multiple_of(core * half_rows, half_rows), half_rows)
    lat_ref[...] = latents(normed[own], turns[0, own], turns[1, own])
    fresh_ref[...] = latents(normed[rows:], turns[0, rows:], turns[1, rows:])
    total = None
    for i in range(chunks):
        loads[4 + i].wait()
        lanes = slice(i * depth, (i + 1) * depth)
        term = dot_nn(normed[:, lanes], query_proj_ref[lanes])
        total = term if total is None else total + term
    loads[3].wait()
    fold = scale * log2e
    decode = []
    cos, sin = turns[0], turns[1]
    for head in range(heads):
        at = head * (NOPE + ROPE)
        nope = total[:, at : at + NOPE]
        turned = turn(total[:, at + NOPE : at + NOPE + ROPE], cos, sin)
        qp_ref[head] = (
            jnp.concatenate([nope[:rows], turned[:rows]], axis=-1) * fold
        ).astype(bf16)
        absorbed = dot_nt(
            nope[rows:].astype(bf16), expand_ref[:, head * NOPE : (head + 1) * NOPE]
        )
        decode.append(jnp.concatenate([absorbed, turned[rows:]], axis=-1)[:count])
    qd_ref[...] = (jnp.concatenate(decode, axis=0) * fold).astype(bf16)
    pages.wait()


def front(place, lengths, x, dec, lat_proj_t, query_proj, key_expand, pages, seq_size, grp_size):
    rows, width = x.shape
    count = dec.shape[0]
    heads = key_expand.shape[1] // NOPE
    padded = count + 8
    requests = lengths.shape[0]
    fine = rope_tables(range(max(rows, MAXP * PAGE + count // requests)))
    coarse = rope_tables([rows * i for i in range(seq_size)])
    slots, tokens = pages.shape[1] // 2, PAGE // (grp_size // 2)
    smem = pl.BlockSpec(memory_space=pltpu.SMEM)
    vmem = pl.BlockSpec(memory_space=pltpu.VMEM)
    hbm = pl.BlockSpec(memory_space=pltpu.HBM)
    return pl.pallas_call(
        front_kernel,
        in_specs=[smem, smem, vmem, vmem] + [hbm] * 6,
        out_specs=(vmem, vmem, vmem, vmem, hbm),
        out_shape=(
            jax.ShapeDtypeStruct((rows // 2, WIDE), bf16),
            jax.ShapeDtypeStruct((padded, WIDE), bf16),
            jax.ShapeDtypeStruct((heads, rows, NOPE + ROPE), bf16),
            jax.ShapeDtypeStruct((heads * count, WIDE), bf16),
            jax.ShapeDtypeStruct((pages.shape[0], slots, tokens, WIDE), bf16),
        ),
        scratch_shapes=[
            pltpu.VMEM(x.shape, bf16),
            pltpu.VMEM(dec.shape, bf16),
            pltpu.VMEM(lat_proj_t.shape, bf16),
            pltpu.VMEM(query_proj.shape, bf16),
            pltpu.VMEM(key_expand.shape, bf16),
            pltpu.VMEM((rows + padded, width), bf16),
            pltpu.VMEM((2, rows + padded, ROPE), f32),
            pltpu.SemaphoreType.DMA((8,)),
        ],
        compiler_params=params(40),
    )(place, lengths, fine, coarse, x, dec, lat_proj_t, query_proj, key_expand, pages)


def pack_shares(summed, sum_ref):
    shares = sum_ref.shape[0]
    rows, width = summed.shape
    share = width // shares
    for g in range(shares):
        part = summed[:, g * share : (g + 1) * share]
        sum_ref[g, :rows] = part[:, :128].astype(bf16)
        sum_ref[g, rows : 2 * rows] = part[:, 128:256].astype(bf16)
        rest = part[:, 256:]
        count = 128 // rest.shape[1]
        piece = rows // count
        sum_ref[g, 2 * rows :] = jnp.concatenate(
            [rest[i * piece : (i + 1) * piece] for i in range(count)], axis=1
        ).astype(bf16)


def flash_kernel(
    heads, place_ref, q_ref, mine_ref, other_ref, ke_ref, vet_ref, out_hbm, sum_ref,
    peak, acc, out_ref, sem,
):
    step = pl.program_id(0)
    rows = q_ref.shape[1]
    half = rows // 2
    first, core = place_ref[0] * rows, lax.rem(place_ref[1], 2)
    side = mine_ref.shape[0]
    block = 2 * side
    load = pltpu.make_async_copy(out_hbm, out_ref, sem)

    @pl.when(step == 0)
    def _():
        load.start()
        peak[...] = jnp.full_like(peak, masked_score)
        acc[...] = jnp.zeros_like(acc)

    def work(masked):
        lat = jnp.concatenate([mine_ref[...], other_ref[...]], axis=0)
        low, rope = lat[:, :LAT], lat[:, LAT:]
        ones = jnp.ones((16, block), bf16)
        keys = dot_nn(low, ke_ref[...]).astype(bf16)
        values = dot_nt(vet_ref[...], low).astype(bf16)
        scores = []
        for head in range(heads):
            whole_keys = jnp.concatenate(
                [keys[:, head * NOPE : (head + 1) * NOPE], rope], axis=-1
            )
            scores.append(dot_nt(whole_keys, q_ref[head]))
        if masked:
            row = lax.broadcasted_iota(jnp.int32, (block, rows), 0)
            from_other = row >= side
            row = jnp.where(from_other, row - side, row)
            which = jnp.where(from_other, 1 - core, core)
            key_pos = step * block + (row // half) * rows + which * half + lax.rem(row, half)
            live = key_pos <= first + lax.broadcasted_iota(jnp.int32, (block, rows), 1)
            scores = [jnp.where(live, s, masked_score) for s in scores]
        for head in range(heads):
            old = peak[head]
            new = jnp.maximum(old, jnp.max(scores[head], axis=0, keepdims=True))
            fade = jnp.exp2(old - new)
            weights = jnp.exp2(scores[head] - new).astype(bf16)
            peak[head] = new
            carried = jnp.concatenate([values[head * VH : (head + 1) * VH], ones], axis=0)
            acc[head] = acc[head] * fade + dot_nn(carried, weights)

    @pl.when((step + 1) * block <= first + 1)
    def _():
        work(False)

    @pl.when(((step + 1) * block > first + 1) & (step * block < first + rows))
    def _():
        work(True)

    @pl.when(step == pl.num_programs(0) - 1)
    def _():
        mixed = jnp.concatenate(
            [(acc[h, :VH] / acc[h, VH : VH + 1]).T for h in range(heads)], axis=-1
        ).astype(bf16)
        load.wait()
        pack_shares(dot_nn(mixed, out_ref[...]), sum_ref)


def prefill_attend(place, q, mine, other, key_expand, value_expand_t, mla_output, shares):
    heads, rows, _ = q.shape
    keys = mine.shape[0]
    side = min(512, keys)
    width = mla_output.shape[1]
    dense = rows * width // shares // 128
    whole = lambda shape: pl.BlockSpec(shape, lambda i, s: (0,) * len(shape))
    return pl.pallas_call(
        functools.partial(flash_kernel, heads),
        grid_spec=pltpu.PrefetchScalarGridSpec(
            num_scalar_prefetch=1,
            grid=(keys // side,),
            in_specs=[
                whole(q.shape),
                pl.BlockSpec((side, WIDE), lambda i, s: (i, 0)),
                pl.BlockSpec((side, WIDE), lambda i, s: (i, 0)),
                whole(key_expand.shape),
                whole(value_expand_t.shape),
                pl.BlockSpec(memory_space=pltpu.HBM),
            ],
            out_specs=whole((shares, dense, 128)),
            scratch_shapes=[
                pltpu.VMEM((heads, 1, rows), f32),
                pltpu.VMEM((heads, VH + 16, rows), f32),
                pltpu.VMEM(mla_output.shape, bf16),
                pltpu.SemaphoreType.DMA,
            ],
        ),
        out_shape=jax.ShapeDtypeStruct((shares, dense, 128), bf16),
        compiler_params=params(56),
    )(place, q, mine, other, key_expand, value_expand_t, mla_output)


def gather_share_kernel(parts_ref, x_ref, out_ref):
    rows, share = x_ref.shape
    x = x_ref[...].astype(f32)
    total = jnp.sum(parts_ref[...].astype(f32), axis=0)
    left = total[:rows] + x[:, :128]
    right = total[rows : 2 * rows] + x[:, 128:256]
    rest = total[2 * rows :]
    wide = share - 256
    rest = jnp.concatenate(
        [rest[:, i * wide : (i + 1) * wide] for i in range(128 // wide)], axis=0
    )
    rest = rest + x[:, 256:]
    out_ref[...] = jnp.concatenate([left.T, right.T, rest.T], axis=0).astype(bf16)


def gather_share(parts, x):
    rows, share = x.shape
    return pl.pallas_call(
        gather_share_kernel,
        out_shape=jax.ShapeDtypeStruct((share, rows), bf16),
        compiler_params=params(32),
    )(parts, x)


def pages_kernel(group, requests, first_ref, q_ref, keys_ref, fresh_ref, owner_ref, sent_ref):
    rows = q_ref.shape[0]
    parts = 4
    block = rows // parts
    keys = keys_ref[...]
    fresh = fresh_ref[...]
    within = lax.rem(lax.broadcasted_iota(jnp.int32, (block, 1), 0), group)
    request = lax.rem(within, requests)
    step = within // requests
    live_old = owner_ref[...] == request
    column = lax.broadcasted_iota(jnp.int32, (1, fresh.shape[0]), 1)
    fresh_step = column // requests + first_ref[1] * group
    live_new = (lax.rem(column, requests) == request) & (fresh_step <= step)
    lane = lax.broadcasted_iota(jnp.int32, (block, SENT - LAT), 1)
    scores = []
    for i in range(parts):
        q = q_ref[i * block : (i + 1) * block]
        scores.append(
            (
                jnp.where(live_old, dot_nt(q, keys), masked_score),
                jnp.where(live_new, dot_nt(q, fresh), masked_score),
            )
        )
    for i in range(parts):
        old, new = scores[i]
        highest = jnp.maximum(
            jnp.max(old, axis=-1, keepdims=True), jnp.max(new, axis=-1, keepdims=True)
        )
        highest = jnp.maximum(highest, 0.1 * masked_score)
        w_old = jnp.exp2(old - highest)
        w_new = jnp.exp2(new - highest)
        total = jnp.sum(w_old, axis=-1, keepdims=True) + jnp.sum(w_new, axis=-1, keepdims=True)
        some = total > 0.0
        safe = jnp.where(some, total, 1.0)
        mixed = dot_nn(w_old.astype(bf16), keys[:, :LAT]) + dot_nn(
            w_new.astype(bf16), fresh[:, :LAT]
        )
        mixed = mixed / safe
        level = jnp.where(some, highest + jnp.log2(safe), masked_score)
        high = level.astype(bf16).astype(f32)
        middle = (level - high).astype(bf16).astype(f32)
        low = level - high - middle
        tail = jnp.where(
            lane == 0, high, jnp.where(lane == 1, middle, jnp.where(lane == 2, low, 0.0))
        )
        sent_ref[i * block : (i + 1) * block] = jnp.concatenate([mixed, tail], axis=-1).astype(
            bf16
        )


def pages_attend(place, q_all, keys, fresh, owner, group, requests):
    smem = pl.BlockSpec(memory_space=pltpu.SMEM)
    vmem = pl.BlockSpec(memory_space=pltpu.VMEM)
    return pl.pallas_call(
        functools.partial(pages_kernel, group, requests),
        in_specs=[smem, vmem, vmem, vmem, vmem],
        out_specs=vmem,
        out_shape=jax.ShapeDtypeStruct((q_all.shape[0], SENT), bf16),
        compiler_params=params(40),
    )(place, q_all, keys, fresh, owner)


def combine_kernel(heads, parts_ref, ve_ref, out_ref, sum_ref):
    tails = parts_ref[:, :, LAT:].astype(f32)
    lane = lax.broadcasted_iota(jnp.int32, tails.shape, 2)
    level = jnp.sum(jnp.where(lane < 3, tails, 0.0), axis=-1, keepdims=True)
    weights = jnp.exp2(level - jnp.max(level, axis=0, keepdims=True))
    total = jnp.sum(weights, axis=0)
    mixed = jnp.sum(parts_ref[:, :, :LAT].astype(f32) * weights, axis=0) / total
    count = mixed.shape[0] // heads
    head_values = [
        dot_nn(
            mixed[h * count : (h + 1) * count].astype(bf16), ve_ref[:, h * VH : (h + 1) * VH]
        )
        for h in range(heads)
    ]
    joined = jnp.concatenate(head_values, axis=-1).astype(bf16)
    sum_ref[...] = dot_nn(joined, out_ref[...]).astype(bf16)


def combine(parts, value_expand, mla_output):
    heads = value_expand.shape[1] // VH
    return pl.pallas_call(
        functools.partial(combine_kernel, heads),
        out_shape=jax.ShapeDtypeStruct((parts.shape[1] // heads, mla_output.shape[1]), bf16),
        compiler_params=params(40),
    )(parts, value_expand, mla_output)


def kda_kernel(
    heads,
    requests,
    parts_ref,
    dec_ref,
    inputs_ref,
    beta_ref,
    decay_down_ref,
    decay_up_ref,
    gate_down_ref,
    gate_up_ref,
    rate_ref,
    states_ref,
    output_ref,
    hidden_ref,
    sum_ref,
    kin,
    projected,
):
    part = pl.program_id(0)
    shares, rows, share = hidden_ref.shape

    @pl.when(part == 0)
    def _():
        hidden = dec_ref[...].astype(f32) + jnp.sum(parts_ref[...].astype(f32), axis=0)
        for g in range(shares):
            hidden_ref[g] = hidden[:, g * share : (g + 1) * share]
        kin[...] = norm_rows(hidden).astype(bf16)

    projected[part] = dot_nn(kin[...], inputs_ref[0])

    @pl.when(part == pl.num_programs(0) - 1)
    def _():
        read_in = kin[...]
        beta = jax.nn.sigmoid(dot_nt(read_in, beta_ref[...]))
        decay_low = dot_nn(read_in, decay_down_ref[...]).astype(bf16)
        decays = jnp.exp(
            -rate_ref[...] * jax.nn.softplus(dot_nn(decay_low, decay_up_ref[...]))
        )
        gate_low = dot_nn(read_in, gate_down_ref[...]).astype(bf16)
        gates = jax.nn.sigmoid(dot_nn(gate_low, gate_up_ref[...]))
        steps = rows // requests
        at = lambda values, t: values[t * requests : (t + 1) * requests]
        along = lambda a, b: jnp.sum(a * b, axis=-1, keepdims=True)
        blended = []
        for head in range(heads):
            lanes = slice(head * DK, (head + 1) * DK)
            q = unit_rows(projected[0, :, lanes]) * DK ** (-0.5)
            k = unit_rows(projected[1, :, lanes])
            v = projected[2, :, lanes]
            a = decays[:, lanes]
            b = beta[:, head : head + 1]
            vectors = []
            held = None
            for t in range(steps):
                held = at(a, t) if held is None else held * at(a, t)
                vectors += [held * at(k, t), held * at(q, t)]
            vectors = jnp.concatenate(vectors, axis=0)
            high = vectors.astype(bf16)
            both = jnp.concatenate([high.astype(f32), vectors - high.astype(f32)], axis=0)
            owner = lax.rem(lax.broadcasted_iota(jnp.int32, (both.shape[0], 1), 0), requests)
            spread = jnp.concatenate(
                [jnp.where(owner == r, both, 0.0) for r in range(requests)], axis=-1
            ).astype(bf16)
            held_states = jnp.concatenate(
                [
                    states_ref[:, r, head].astype(f32).reshape(DV, DK)
                    for r in range(requests)
                ],
                axis=-1,
            ).astype(bf16)
            met = dot_nt(spread, held_states)
            met = met[: vectors.shape[0]] + met[vectors.shape[0] :]
            carried = []
            reads = []
            for t in range(steps):
                seen = at(met, 2 * t)
                read = at(met, 2 * t + 1)
                carried = [(u, w * at(a, t)) for u, w in carried]
                for u, w in carried:
                    seen = seen + u * along(w, at(k, t))
                u = at(b, t) * (at(v, t) - seen)
                carried.append((u, at(k, t)))
                for u, w in carried:
                    read = read + u * along(w, at(q, t))
                reads.append(read)
            read = jnp.concatenate(reads, axis=0)
            blended.append(norm_rows(read) * gates[:, lanes])
        mixed = jnp.concatenate(blended, axis=-1).astype(bf16)
        summed = dot_nn(mixed, output_ref[...])
        for g in range(shares):
            sum_ref[g] = summed[:, g * share : (g + 1) * share].astype(bf16)


def kda(parts, dec, inputs, beta_t, decay_down, decay_up, gate_down, gate_up, rate, states, output):
    shares, rows, width = parts.shape
    heads = beta_t.shape[0]
    requests = states.shape[1]
    columns = inputs.shape[2]
    whole = lambda a: pl.BlockSpec(a.shape, lambda i: (0,) * len(a.shape))
    share_spec = pl.BlockSpec((shares, rows, width // shares), lambda i: (0, 0, 0))
    return pl.pallas_call(
        functools.partial(kda_kernel, heads, requests),
        grid=(3,),
        in_specs=[
            whole(parts),
            whole(dec),
            pl.BlockSpec((1, width, columns), lambda i: (i, 0, 0)),
            whole(beta_t),
            whole(decay_down),
            whole(decay_up),
            whole(gate_down),
            whole(gate_up),
            whole(rate),
            whole(states),
            whole(output),
        ],
        out_specs=(share_spec, share_spec),
        out_shape=(
            jax.ShapeDtypeStruct((shares, rows, width // shares), f32),
            jax.ShapeDtypeStruct((shares, rows, width // shares), bf16),
        ),
        scratch_shapes=[pltpu.VMEM((rows, width), bf16), pltpu.VMEM((3, rows, columns), f32)],
        compiler_params=params(48),
    )(parts, dec, inputs, beta_t, decay_down, decay_up, gate_down, gate_up, rate, states, output)


def shards(
    x_group,
    decode_input,
    prompt_len,
    latent_pages,
    slot_target,
    page_counts,
    kda_state,
    query_proj,
    latent_proj,
    key_expand,
    value_expand,
    mla_output,
    kda_inputs,
    kda_beta,
    decay_down,
    decay_up,
    gate_down,
    gate_up,
    decay_log,
    kda_output,
):
    seq_index = lax.axis_index("seq")
    grp_index = lax.axis_index("grp")
    seq_size = lax.axis_size("seq")
    grp_size = lax.axis_size("grp")
    rows, width = x_group.shape
    steps, requests, _ = decode_input.shape
    decode_rows = steps * requests
    share = width // grp_size
    dec = decode_input.reshape(decode_rows, width)
    place = jnp.stack([seq_index, grp_index]).astype(jnp.int32)

    own_latent, fresh, q_prefill, q_decode, own_tokens = front(
        place,
        prompt_len,
        x_group,
        dec,
        latent_proj.T,
        query_proj,
        key_expand,
        latent_pages[0],
        seq_size,
        grp_size,
    )
    mine = lax.all_gather(own_latent, "seq", axis=0, tiled=True)
    other = lax.ppermute(mine, "grp", [(g, g ^ 1) for g in range(grp_size)])

    arrived = lax.all_to_all(own_tokens, "seq", split_axis=0, concat_axis=0, tiled=True)
    _, slots, tokens, _ = own_tokens.shape
    page_keys = arrived.reshape(seq_size * slots * tokens, WIDE)
    core = grp_index % 2
    target = lax.dynamic_slice_in_dim(slot_target[:, 0, :], core * slots, slots, 1)
    owner = target // MAXP
    lengths = jnp.sum(
        jnp.where(owner[..., None] == jnp.arange(requests), prompt_len, 0), axis=-1
    )
    held = core * slots + jnp.arange(slots)[None, :] < page_counts
    token_pos = (
        ((target % MAXP) * PAGE + (grp_index // 2) * tokens)[..., None] + jnp.arange(tokens)
    )
    key_owner = jnp.where(
        held[..., None] & (token_pos < lengths[..., None]), owner[..., None], -1
    ).reshape(1, -1)

    states = lax.all_to_all(
        kda_state.astype(bf16), "seq", split_axis=0, concat_axis=0, tiled=True
    ).reshape((seq_size, requests) + kda_state.shape[1:])

    q_all = lax.all_gather(q_decode, "grp", axis=0, tiled=True)
    partial = pages_attend(place, q_all, page_keys, fresh, key_owner, decode_rows, requests)
    partial = lax.all_to_all(
        partial.reshape(grp_size, -1, SENT), "grp", split_axis=0, concat_axis=0, tiled=True
    )
    mla_part = combine(partial, value_expand, mla_output)
    mla_parts = lax.all_gather(mla_part, "grp", axis=0, tiled=False)
    hidden, kda_part = kda(
        mla_parts,
        dec,
        kda_inputs.transpose(1, 0, 2),
        kda_beta.T,
        decay_down,
        decay_up,
        gate_down,
        gate_up,
        jnp.repeat(jnp.exp(decay_log), DK)[None, :],
        states,
        kda_output,
    )
    kda_parts = lax.all_to_all(kda_part, "grp", split_axis=0, concat_axis=0, tiled=True)
    hidden_share = lax.dynamic_index_in_dim(hidden, grp_index, 0, keepdims=False)
    decode_out = (hidden_share + jnp.sum(kda_parts.astype(f32), axis=0)).astype(bf16)

    prefill_part = prefill_attend(
        place, q_prefill, mine, other, key_expand, value_expand.T, mla_output, grp_size
    )
    prefill_parts = lax.all_to_all(
        prefill_part, "grp", split_axis=0, concat_axis=0, tiled=True
    )
    own_columns = lax.dynamic_slice_in_dim(x_group, grp_index * share, share, 1)
    prefill_out = gather_share(prefill_parts, own_columns).T
    return (prefill_out, decode_out.reshape(steps, requests, share))


def solution(mesh):
    in_specs = (
        P("seq", None),
        P(None, "seq", None),
        P("seq"),
        P("seq", None, None, None, None),
        P(None, "seq", None),
        P(None, "seq"),
        P(None, "grp", "seq", None),
        P(None, "grp"),
        P(),
        P(None, "grp"),
        P(None, "grp"),
        P("grp", None),
        P(None, None, "grp"),
        P(None, "grp"),
        P(),
        P(None, "grp"),
        P(),
        P(None, "grp"),
        P("grp"),
        P("grp", None),
    )
    out_specs = (P("seq", "grp"), P(None, "seq", "grp"))
    return jax.shard_map(shards, mesh=mesh, in_specs=in_specs, out_specs=out_specs, check_vma=False)
```

```python
import functools

import jax
import jax.numpy as jnp
import numpy as np
from jax import lax
from jax.experimental import pallas as pl
from jax.experimental.pallas import tpu as pltpu
from jax.sharding import PartitionSpec as P

LAT = 512
ROPE = 64
NOPE = 128
VH = 128
DK = 128
DV = 128
PAGE = 64
MAXP = 12
WIDE = LAT + ROPE
SENT = LAT + 128

epsilon = 1e-06
masked_score = -1e30
scale = (NOPE + ROPE) ** (-0.5)
log2e = 1.4426950408889634

f32 = jnp.float32
bf16 = jnp.bfloat16
MIB = 1024 * 1024


def params(mib=58):
    return pltpu.CompilerParams(vmem_limit_bytes=mib * MIB)


def dot_nt(a, b):
    return lax.dot_general(a, b, (((1,), (1,)), ((), ())), preferred_element_type=f32)


def dot_nn(a, b):
    return lax.dot_general(a, b, (((1,), (0,)), ((), ())), preferred_element_type=f32)


def norm_rows(values):
    return values * lax.rsqrt(jnp.mean(values * values, axis=-1, keepdims=True) + epsilon)


def unit_rows(values):
    return values * lax.rsqrt(jnp.sum(values * values, axis=-1, keepdims=True) + epsilon)


def turn(values, cos, sin):
    half = ROPE // 2
    swapped = jnp.concatenate([values[:, half:], values[:, :half]], axis=-1)
    return values * cos + swapped * sin


def rope_tables(positions):
    half = ROPE // 2
    frequency = np.exp(-np.log(10000.0) * np.arange(half) / half)
    angles = np.asarray(positions, np.float64)[:, None] * frequency
    cos, sin = np.cos(angles), np.sin(angles)
    both = np.stack([np.concatenate([cos, cos], -1), np.concatenate([-sin, sin], -1)])
    return jnp.asarray(both, f32)


def slice_kernel(pages_hbm, own_hbm, held, in_sems, out_sems):
    grp = lax.axis_index("grp")
    owners, slots, tokens, _ = own_hbm.shape
    parts = in_sems.shape[0]
    each = owners // parts
    first = lax.rem(grp, 2) * slots
    row = pl.multiple_of((grp // 2) * tokens, tokens)
    loads = [
        pltpu.make_async_copy(
            pages_hbm.at[pl.ds(i * each, each), pl.ds(first, slots), pl.ds(row, tokens), :],
            held.at[pl.ds(i * each, each)],
            in_sems.at[i],
        )
        for i in range(parts)
    ]
    stores = [
        pltpu.make_async_copy(
            held.at[pl.ds(i * each, each)], own_hbm.at[pl.ds(i * each, each)], out_sems.at[i]
        )
        for i in range(parts)
    ]
    for load in loads:
        load.start()
    for load, store in zip(loads, stores):
        load.wait()
        store.start()
    for store in stores:
        store.wait()


def slice_pages(pages, grp_size):
    owners, cap, page, wide = pages.shape
    shape = (owners, cap // 2, page // (grp_size // 2), wide)
    parts = 4
    hbm = pl.BlockSpec(memory_space=pltpu.HBM)
    return pl.pallas_call(
        slice_kernel,
        in_specs=[hbm],
        out_specs=hbm,
        out_shape=jax.ShapeDtypeStruct(shape, bf16),
        scratch_shapes=[
            pltpu.VMEM(shape, bf16),
            pltpu.SemaphoreType.DMA((parts,)),
            pltpu.SemaphoreType.DMA((parts,)),
        ],
        compiler_params=params(),
    )(pages)


def front_kernel(
    lengths_ref,
    fine_ref,
    coarse_ref,
    x_hbm,
    dec_hbm,
    lat_proj_hbm,
    query_proj_hbm,
    expand_hbm,
    lat_hbm,
    fresh_ref,
    qp_ref,
    qd_ref,
    x_ref,
    dec_ref,
    lat_proj_ref,
    query_proj_ref,
    expand_ref,
    normed,
    turns,
    lat_ref,
    sems,
    out_sems,
):
    seq, grp = lax.axis_index("seq"), lax.axis_index("grp")
    rows, width = x_ref.shape
    count = dec_ref.shape[0]
    half_rows = lat_ref.shape[0]
    core = lax.rem(grp, 2)
    heads = qp_ref.shape[0]
    requests = lengths_ref.shape[0]
    chunks = 3
    depth = width // chunks
    loads = [
        pltpu.make_async_copy(x_hbm, x_ref, sems.at[0]),
        pltpu.make_async_copy(dec_hbm, dec_ref, sems.at[1]),
        pltpu.make_async_copy(lat_proj_hbm, lat_proj_ref, sems.at[2]),
        pltpu.make_async_copy(expand_hbm, expand_ref, sems.at[3]),
    ]
    loads += [
        pltpu.make_async_copy(
            query_proj_hbm.at[pl.ds(i * depth, depth)],
            query_proj_ref.at[pl.ds(i * depth, depth)],
            sems.at[4 + i],
        )
        for i in range(chunks)
    ]
    for load in loads:
        load.start()
    for r in range(requests):
        for t in range(count // requests):
            at = rows + t * requests + r
            row = lengths_ref[r] + t
            turns[0, at : at + 1] = fine_ref[0, pl.ds(row, 1)]
            turns[1, at : at + 1] = fine_ref[1, pl.ds(row, 1)]
    turns[:, rows + count :] = jnp.zeros((2, turns.shape[1] - rows - count, ROPE), f32)
    base_cos, base_sin = coarse_ref[0, pl.ds(seq, 1)], coarse_ref[1, pl.ds(seq, 1)]
    fine_cos, fine_sin = fine_ref[0, :rows], fine_ref[1, :rows]
    turns[0, :rows] = base_cos * fine_cos - base_sin * fine_sin
    turns[1, :rows] = base_sin * fine_cos + base_cos * fine_sin
    loads[0].wait()
    normed[:rows] = norm_rows(x_ref[...].astype(f32)).astype(bf16)
    loads[1].wait()
    tail = normed.shape[0] - rows - count
    normed[rows:] = jnp.concatenate(
        [norm_rows(dec_ref[...].astype(f32)), jnp.zeros((tail, width), f32)], axis=0
    ).astype(bf16)
    loads[2].wait()

    def latents(inputs, cos, sin):
        projected = dot_nt(inputs, lat_proj_ref[...])
        return jnp.concatenate(
            [norm_rows(projected[:, :LAT]), turn(projected[:, LAT:], cos, sin)], axis=-1
        ).astype(bf16)

    own = pl.ds(pl.multiple_of(core * half_rows, half_rows), half_rows)
    gap = jnp.zeros((half_rows, SENT - WIDE), bf16)
    lat_ref[...] = jnp.concatenate(
        [latents(normed[own], turns[0, own], turns[1, own]), gap], axis=-1
    )
    stores = [
        pltpu.make_async_copy(lat_ref, lat_hbm.at[i], out_sems.at[i])
        for i in range(lat_hbm.shape[0])
    ]
    for store in stores:
        store.start()
    fresh_ref[...] = latents(normed[rows:], turns[0, rows:], turns[1, rows:])
    total = None
    for i in range(chunks):
        loads[4 + i].wait()
        lanes = slice(i * depth, (i + 1) * depth)
        term = dot_nn(normed[:, lanes], query_proj_ref[lanes])
        total = term if total is None else total + term
    loads[3].wait()
    fold = scale * log2e
    decode = []
    cos, sin = turns[0], turns[1]
    for head in range(heads):
        at = head * (NOPE + ROPE)
        nope = total[:, at : at + NOPE]
        turned = turn(total[:, at + NOPE : at + NOPE + ROPE], cos, sin)
        qp_ref[head] = (
            jnp.concatenate([nope[:rows], turned[:rows]], axis=-1) * fold
        ).astype(bf16)
        absorbed = dot_nt(
            nope[rows:].astype(bf16), expand_ref[:, head * NOPE : (head + 1) * NOPE]
        )
        blank = jnp.zeros((absorbed.shape[0], SENT - WIDE), f32)
        decode.append(jnp.concatenate([absorbed, turned[rows:], blank], axis=-1)[:count])
    qd_ref[...] = (jnp.concatenate(decode, axis=0) * fold).astype(bf16)
    for store in stores:
        store.wait()


def front(lengths, x, dec, lat_proj_t, query_proj, key_expand, seq_size):
    rows, width = x.shape
    count = dec.shape[0]
    heads = key_expand.shape[1] // NOPE
    padded = count + 8
    requests = lengths.shape[0]
    fine = rope_tables(range(max(rows, MAXP * PAGE + count // requests)))
    coarse = rope_tables([rows * i for i in range(seq_size)])
    smem = pl.BlockSpec(memory_space=pltpu.SMEM)
    vmem = pl.BlockSpec(memory_space=pltpu.VMEM)
    hbm = pl.BlockSpec(memory_space=pltpu.HBM)
    return pl.pallas_call(
        front_kernel,
        in_specs=[smem, vmem, vmem] + [hbm] * 5,
        out_specs=(hbm, vmem, vmem, vmem),
        out_shape=(
            jax.ShapeDtypeStruct((seq_size, rows // 2, SENT), bf16),
            jax.ShapeDtypeStruct((padded, WIDE), bf16),
            jax.ShapeDtypeStruct((heads, rows, NOPE + ROPE), bf16),
            jax.ShapeDtypeStruct((heads * count, SENT), bf16),
        ),
        scratch_shapes=[
            pltpu.VMEM(x.shape, bf16),
            pltpu.VMEM(dec.shape, bf16),
            pltpu.VMEM(lat_proj_t.shape, bf16),
            pltpu.VMEM(query_proj.shape, bf16),
            pltpu.VMEM(key_expand.shape, bf16),
            pltpu.VMEM((rows + padded, width), bf16),
            pltpu.VMEM((2, rows + padded, ROPE), f32),
            pltpu.VMEM((rows // 2, SENT), bf16),
            pltpu.SemaphoreType.DMA((7,)),
            pltpu.SemaphoreType.DMA((seq_size,)),
        ],
        compiler_params=params(),
    )(lengths, fine, coarse, x, dec, lat_proj_t, query_proj, key_expand)


def pack_shares(summed, sum_ref):
    shares = sum_ref.shape[0]
    rows, width = summed.shape
    share = width // shares
    for g in range(shares):
        part = summed[:, g * share : (g + 1) * share]
        sum_ref[g, :rows] = part[:, :128].astype(bf16)
        sum_ref[g, rows : 2 * rows] = part[:, 128:256].astype(bf16)
        rest = part[:, 256:]
        count = 128 // rest.shape[1]
        piece = rows // count
        sum_ref[g, 2 * rows :] = jnp.concatenate(
            [rest[i * piece : (i + 1) * piece] for i in range(count)], axis=1
        ).astype(bf16)


def flash_kernel(
    heads, q_ref, mine_ref, other_ref, ke_ref, ve_ref, out_hbm, sum_ref,
    peak, acc, vet_ref, out_ref, sem,
):
    step = pl.program_id(0)
    rows = q_ref.shape[1]
    half = rows // 2
    first, core = lax.axis_index("seq") * rows, lax.rem(lax.axis_index("grp"), 2)
    side = mine_ref.shape[0]
    block = 2 * side
    load = pltpu.make_async_copy(out_hbm, out_ref, sem)

    @pl.when(step == 0)
    def _():
        load.start()
        vet_ref[...] = ve_ref[...].astype(f32).T.astype(bf16)
        peak[...] = jnp.full_like(peak, masked_score)
        acc[...] = jnp.zeros_like(acc)

    def work(masked):
        lat = jnp.concatenate([mine_ref[...], other_ref[...]], axis=0)
        low, rope = lat[:, :LAT], lat[:, LAT:WIDE]
        ones = jnp.ones((16, block), bf16)
        keys = dot_nn(low, ke_ref[...]).astype(bf16)
        values = dot_nt(vet_ref[...], low).astype(bf16)
        scores = []
        for head in range(heads):
            whole_keys = jnp.concatenate(
                [keys[:, head * NOPE : (head + 1) * NOPE], rope], axis=-1
            )
            scores.append(dot_nt(whole_keys, q_ref[head]))
        if masked:
            row = lax.broadcasted_iota(jnp.int32, (block, rows), 0)
            from_other = row >= side
            row = jnp.where(from_other, row - side, row)
            which = jnp.where(from_other, 1 - core, core)
            key_pos = step * block + (row // half) * rows + which * half + lax.rem(row, half)
            live = key_pos <= first + lax.broadcasted_iota(jnp.int32, (block, rows), 1)
            scores = [jnp.where(live, s, masked_score) for s in scores]
        for head in range(heads):
            old = peak[head]
            new = jnp.maximum(old, jnp.max(scores[head], axis=0, keepdims=True))
            fade = jnp.exp2(old - new)
            weights = jnp.exp2(scores[head] - new).astype(bf16)
            peak[head] = new
            carried = jnp.concatenate([values[head * VH : (head + 1) * VH], ones], axis=0)
            acc[head] = acc[head] * fade + dot_nn(carried, weights)

    @pl.when((step + 1) * block <= first + 1)
    def _():
        work(False)

    @pl.when(((step + 1) * block > first + 1) & (step * block < first + rows))
    def _():
        work(True)

    @pl.when(step == pl.num_programs(0) - 1)
    def _():
        mixed = jnp.concatenate(
            [(acc[h, :VH] / acc[h, VH : VH + 1]).T for h in range(heads)], axis=-1
        ).astype(bf16)
        load.wait()
        pack_shares(dot_nn(mixed, out_ref[...]), sum_ref)


def prefill_attend(q, mine, other, key_expand, value_expand, mla_output, shares):
    heads, rows, _ = q.shape
    keys = mine.shape[0]
    side = min(512, keys)
    width = mla_output.shape[1]
    dense = rows * width // shares // 128
    whole = lambda shape: pl.BlockSpec(shape, lambda i: (0,) * len(shape))
    return pl.pallas_call(
        functools.partial(flash_kernel, heads),
        grid=(keys // side,),
        in_specs=[
            whole(q.shape),
            pl.BlockSpec((side, SENT), lambda i: (i, 0)),
            pl.BlockSpec((side, SENT), lambda i: (i, 0)),
            whole(key_expand.shape),
            whole(value_expand.shape),
            pl.BlockSpec(memory_space=pltpu.HBM),
        ],
        out_specs=whole((shares, dense, 128)),
        scratch_shapes=[
            pltpu.VMEM((heads, 1, rows), f32),
            pltpu.VMEM((heads, VH + 16, rows), f32),
            pltpu.VMEM((value_expand.shape[1], value_expand.shape[0]), bf16),
            pltpu.VMEM(mla_output.shape, bf16),
            pltpu.SemaphoreType.DMA,
        ],
        out_shape=jax.ShapeDtypeStruct((shares, dense, 128), bf16),
        compiler_params=params(),
    )(q, mine, other, key_expand, value_expand, mla_output)


def gather_share_kernel(parts_ref, x_ref, out_ref):
    rows, share = x_ref.shape
    x = x_ref[...].astype(f32)
    total = jnp.sum(parts_ref[...].astype(f32), axis=0)
    left = total[:rows] + x[:, :128]
    right = total[rows : 2 * rows] + x[:, 128:256]
    rest = total[2 * rows :]
    wide = share - 256
    rest = jnp.concatenate(
        [rest[:, i * wide : (i + 1) * wide] for i in range(128 // wide)], axis=0
    )
    rest = rest + x[:, 256:]
    out_ref[...] = jnp.concatenate([left.T, right.T, rest.T], axis=0).astype(bf16)


def gather_share(parts, x):
    rows, share = x.shape
    return pl.pallas_call(
        gather_share_kernel,
        out_shape=jax.ShapeDtypeStruct((share, rows), bf16),
        compiler_params=params(),
    )(parts, x)


def split_level(level, rows):
    lane = lax.broadcasted_iota(jnp.int32, (rows, SENT - LAT), 1)
    high = level.astype(bf16).astype(f32)
    middle = (level - high).astype(bf16).astype(f32)
    low = level - high - middle
    return jnp.where(
        lane == 0, high, jnp.where(lane == 1, middle, jnp.where(lane == 2, low, 0.0))
    )


def join_level(part):
    tail = part[:, LAT:].astype(f32)
    lane = lax.broadcasted_iota(jnp.int32, tail.shape, 1)
    return jnp.sum(jnp.where(lane < 3, tail, 0.0), axis=-1, keepdims=True)


def merge_parts(parts):
    levels = [join_level(p) for p in parts]
    highest = functools.reduce(jnp.maximum, levels)
    weights = [jnp.exp2(v - highest) for v in levels]
    total = sum(weights)
    mixed = sum(p[:, :LAT].astype(f32) * w for p, w in zip(parts, weights)) / total
    return mixed, highest + jnp.log2(total)


def pages_kernel(group, requests, count, *refs):
    q_refs = refs[: 2 * count]
    keys_ref, fresh_ref, owner_ref, keep_ref, send_ref = refs[2 * count :]
    each = q_refs[0].shape[0]
    block = 2 * each
    keys = keys_ref[...]
    fresh = fresh_ref[...]
    within = lax.rem(lax.broadcasted_iota(jnp.int32, (block, 1), 0), group)
    request = lax.rem(within, requests)
    step = within // requests
    live_old = owner_ref[...] == request
    column = lax.broadcasted_iota(jnp.int32, (1, fresh.shape[0]), 1)
    fresh_step = column // requests + lax.axis_index("grp") * group
    live_new = (lax.rem(column, requests) == request) & (fresh_step <= step)
    scores = []
    for i in range(0, 2 * count, 2):
        q = jnp.concatenate([q_refs[i][:, :WIDE], q_refs[i + 1][:, :WIDE]], axis=0)
        scores.append(
            (
                jnp.where(live_old, dot_nt(q, keys), masked_score),
                jnp.where(live_new, dot_nt(q, fresh), masked_score),
            )
        )
    for i, (old, new) in enumerate(scores):
        highest = jnp.maximum(
            jnp.max(old, axis=-1, keepdims=True), jnp.max(new, axis=-1, keepdims=True)
        )
        highest = jnp.maximum(highest, 0.1 * masked_score)
        w_old = jnp.exp2(old - highest)
        w_new = jnp.exp2(new - highest)
        total = jnp.sum(w_old, axis=-1, keepdims=True) + jnp.sum(w_new, axis=-1, keepdims=True)
        some = total > 0.0
        safe = jnp.where(some, total, 1.0)
        mixed = dot_nn(w_old.astype(bf16), keys[:, :LAT]) + dot_nn(
            w_new.astype(bf16), fresh[:, :LAT]
        )
        level = jnp.where(some, highest + jnp.log2(safe), masked_score)
        out_ref = keep_ref if 2 * i < count else send_ref
        both = jnp.concatenate([mixed / safe, split_level(level, block)], axis=-1).astype(bf16)
        out_ref[2 * i % count] = both[:each]
        out_ref[2 * i % count + 1] = both[each:]


def pages_attend(queries, keys, fresh, owner, group, requests):
    count = len(queries) // 2
    vmem = pl.BlockSpec(memory_space=pltpu.VMEM)
    shape = jax.ShapeDtypeStruct((count, queries[0].shape[0], SENT), bf16)
    return pl.pallas_call(
        functools.partial(pages_kernel, group, requests, count),
        in_specs=[vmem] * (2 * count + 3),
        out_specs=(vmem, vmem),
        out_shape=(shape, shape),
        compiler_params=params(),
    )(*queries, keys, fresh, owner)


def merge_kernel(keep_ref, got_ref, *out_refs):
    for i, out_ref in enumerate(out_refs):
        mixed, level = merge_parts([keep_ref[i], got_ref[i]])
        out_ref[...] = jnp.concatenate(
            [mixed, split_level(level, mixed.shape[0])], axis=-1
        ).astype(bf16)


def merge_pair(keep, got):
    shape = jax.ShapeDtypeStruct(keep.shape[1:], bf16)
    return pl.pallas_call(
        merge_kernel,
        out_shape=(shape,) * keep.shape[0],
        compiler_params=params(),
    )(keep, got)


def combine_kernel(heads, count, *refs):
    ve_ref, out_ref, sum_ref = refs[count:]
    mixed, _ = merge_parts([ref[...] for ref in refs[:count]])
    each = mixed.shape[0] // heads
    head_values = [
        dot_nn(mixed[h * each : (h + 1) * each].astype(bf16), ve_ref[:, h * VH : (h + 1) * VH])
        for h in range(heads)
    ]
    joined = jnp.concatenate(head_values, axis=-1).astype(bf16)
    sum_ref[...] = dot_nn(joined, out_ref[...]).astype(bf16)


def combine(parts, value_expand, mla_output):
    heads = value_expand.shape[1] // VH
    return pl.pallas_call(
        functools.partial(combine_kernel, heads, len(parts)),
        out_shape=jax.ShapeDtypeStruct((parts[0].shape[0] // heads, mla_output.shape[1]), bf16),
        compiler_params=params(20),
    )(*parts, value_expand, mla_output)


def kda_kernel(
    heads,
    requests,
    one_ref,
    two_ref,
    dec_ref,
    inputs_ref,
    beta_ref,
    decay_down_ref,
    decay_up_ref,
    gate_down_ref,
    gate_up_ref,
    rate_ref,
    states_ref,
    output_ref,
    hidden_ref,
    keep_ref,
    send_ref,
    kin,
    projected,
    by_share,
    summed_ref,
):
    part = pl.program_id(0)
    shares, rows, share = by_share.shape
    grp = lax.axis_index("grp")

    @pl.when(part == 0)
    def _():
        hidden = dec_ref[...].astype(f32) + one_ref[...] + two_ref[...]
        for g in range(shares):
            by_share[g] = hidden[:, g * share : (g + 1) * share]
        hidden_ref[...] = by_share[grp]
        kin[...] = norm_rows(hidden).astype(bf16)

    projected[part] = dot_nn(kin[...], inputs_ref[0])

    @pl.when(part == pl.num_programs(0) - 1)
    def _():
        read_in = kin[...]
        beta = jax.nn.sigmoid(dot_nt(read_in, beta_ref[...]))
        decay_low = dot_nn(read_in, decay_down_ref[...]).astype(bf16)
        decays = jnp.exp(
            -rate_ref[...] * jax.nn.softplus(dot_nn(decay_low, decay_up_ref[...]))
        )
        gate_low = dot_nn(read_in, gate_down_ref[...]).astype(bf16)
        gates = jax.nn.sigmoid(dot_nn(gate_low, gate_up_ref[...]))
        steps = rows // requests
        at = lambda values, t: values[t * requests : (t + 1) * requests]
        along = lambda a, b: jnp.sum(a * b, axis=-1, keepdims=True)
        blended = []
        for head in range(heads):
            lanes = slice(head * DK, (head + 1) * DK)
            q = unit_rows(projected[0, :, lanes]) * DK ** (-0.5)
            k = unit_rows(projected[1, :, lanes])
            v = projected[2, :, lanes]
            a = decays[:, lanes]
            b = beta[:, head : head + 1]
            vectors = []
            held = None
            for t in range(steps):
                held = at(a, t) if held is None else held * at(a, t)
                vectors += [held * at(k, t), held * at(q, t)]
            vectors = jnp.concatenate(vectors, axis=0)
            high = vectors.astype(bf16)
            both = jnp.concatenate([high.astype(f32), vectors - high.astype(f32)], axis=0)
            owner = lax.rem(lax.broadcasted_iota(jnp.int32, (both.shape[0], 1), 0), requests)
            spread = jnp.concatenate(
                [jnp.where(owner == r, both, 0.0) for r in range(requests)], axis=-1
            ).astype(bf16)
            held_states = jnp.concatenate(
                [
                    states_ref[:, r, head].astype(f32).reshape(DV, DK)
                    for r in range(requests)
                ],
                axis=-1,
            ).astype(bf16)
            met = dot_nt(spread, held_states)
            met = met[: vectors.shape[0]] + met[vectors.shape[0] :]
            carried = []
            reads = []
            for t in range(steps):
                seen = at(met, 2 * t)
                read = at(met, 2 * t + 1)
                carried = [(u, w * at(a, t)) for u, w in carried]
                for u, w in carried:
                    seen = seen + u * along(w, at(k, t))
                u = at(b, t) * (at(v, t) - seen)
                carried.append((u, at(k, t)))
                for u, w in carried:
                    read = read + u * along(w, at(q, t))
                reads.append(read)
            read = jnp.concatenate(reads, axis=0)
            blended.append(norm_rows(read) * gates[:, lanes])
        mixed = jnp.concatenate(blended, axis=-1).astype(bf16)
        summed = dot_nn(mixed, output_ref[...])
        for g in range(shares):
            summed_ref[g] = summed[:, g * share : (g + 1) * share]
        core = lax.rem(grp, 2)
        for by in range(shares // 2):
            pair = 2 * lax.rem(grp // 2 + by, shares // 2)
            keep_ref[by] = summed_ref[pair + core]
            send_ref[by] = summed_ref[pair + 1 - core].astype(bf16)


def kda(shares, one, two, dec, inputs, beta_t, decay_down, decay_up, gate_down, gate_up, rate, states, output):
    rows, width = dec.shape
    heads = beta_t.shape[0]
    requests = states.shape[1]
    columns = inputs.shape[2]
    whole = lambda a: pl.BlockSpec(a.shape, lambda i: (0,) * len(a.shape))
    share = width // shares
    sides = shares // 2
    held = lambda shape: pl.BlockSpec(shape, lambda i: (0,) * len(shape))
    return pl.pallas_call(
        functools.partial(kda_kernel, heads, requests),
        grid=(3,),
        in_specs=[
            whole(one),
            whole(two),
            whole(dec),
            pl.BlockSpec((1, width, columns), lambda i: (i, 0, 0)),
            whole(beta_t),
            whole(decay_down),
            whole(decay_up),
            whole(gate_down),
            whole(gate_up),
            whole(rate),
            whole(states),
            whole(output),
        ],
        out_specs=(held((rows, share)), held((sides, rows, share)), held((sides, rows, share))),
        out_shape=(
            jax.ShapeDtypeStruct((rows, share), f32),
            jax.ShapeDtypeStruct((sides, rows, share), f32),
            jax.ShapeDtypeStruct((sides, rows, share), bf16),
        ),
        scratch_shapes=[
            pltpu.VMEM((rows, width), bf16),
            pltpu.VMEM((3, rows, columns), f32),
            pltpu.VMEM((shares, rows, share), f32),
            pltpu.VMEM((shares, rows, share), f32),
        ],
        compiler_params=params(),
    )(one, two, dec, inputs, beta_t, decay_down, decay_up, gate_down, gate_up, rate, states, output)


def shards(
    x_group,
    decode_input,
    prompt_len,
    latent_pages,
    slot_target,
    page_counts,
    kda_state,
    query_proj,
    latent_proj,
    key_expand,
    value_expand,
    mla_output,
    kda_inputs,
    kda_beta,
    decay_down,
    decay_up,
    gate_down,
    gate_up,
    decay_log,
    kda_output,
):
    seq_index = lax.axis_index("seq")
    grp_index = lax.axis_index("grp")
    seq_size = lax.axis_size("seq")
    grp_size = lax.axis_size("grp")
    rows, width = x_group.shape
    steps, requests, _ = decode_input.shape
    decode_rows = steps * requests
    share = width // grp_size
    dec = decode_input.reshape(decode_rows, width)

    own_tokens = slice_pages(latent_pages[0], grp_size)
    x_rows, own_tokens = lax.optimization_barrier((x_group, own_tokens))
    own_latent, fresh, q_prefill, q_decode = front(
        prompt_len, x_rows, dec, latent_proj.T, query_proj, key_expand, seq_size
    )
    sides = grp_size // 2

    def shift(value, by):
        return lax.ppermute(
            value, "grp", [(g, (g + 2 * by) % grp_size) for g in range(grp_size)]
        )

    def swap(value):
        return lax.ppermute(value, "grp", [(g, g ^ 1) for g in range(grp_size)])

    arrived = lax.all_to_all(own_tokens, "seq", split_axis=0, concat_axis=0, tiled=True)
    own_latent, arrived = lax.optimization_barrier((own_latent, arrived))
    mine = lax.all_to_all(own_latent, "seq", split_axis=0, concat_axis=0, tiled=True)
    mine = mine.reshape(-1, SENT)
    _, slots, tokens, _ = own_tokens.shape
    page_keys = arrived.reshape(seq_size * slots * tokens, WIDE)
    core = grp_index % 2
    target = lax.dynamic_slice_in_dim(slot_target[:, 0, :], core * slots, slots, 1)
    owner = target // MAXP
    lengths = jnp.sum(
        jnp.where(owner[..., None] == jnp.arange(requests), prompt_len, 0), axis=-1
    )
    held = core * slots + jnp.arange(slots)[None, :] < page_counts
    token_pos = (
        ((target % MAXP) * PAGE + (grp_index // 2) * tokens)[..., None] + jnp.arange(tokens)
    )
    key_owner = jnp.where(
        held[..., None] & (token_pos < lengths[..., None]), owner[..., None], -1
    ).reshape(1, -1)

    queries = [q_decode] + [shift(q_decode, by) for by in range(1, sides)]
    queries += [swap(q) for q in queries]
    keep, send = pages_attend(
        queries, page_keys, fresh, key_owner, decode_rows, requests
    )
    merged = merge_pair(keep, swap(send))
    state_rows, mine = lax.optimization_barrier((kda_state, mine))
    states = lax.all_to_all(
        state_rows.astype(bf16), "seq", split_axis=0, concat_axis=0, tiled=True
    ).reshape((seq_size, requests) + kda_state.shape[1:])
    partial = [merged[0]] + [shift(merged[by], -by) for by in range(1, sides)]
    mla_part = combine(partial, value_expand, mla_output)
    mine, mla_part = lax.optimization_barrier((mine, mla_part))
    mla_half = mla_part.astype(f32)
    for by in range(1, sides):
        mla_half = mla_half + shift(mla_part, by).astype(f32)
    mla_rest = swap(mla_half)

    prefill_part = prefill_attend(
        q_prefill, mine, swap(mine), key_expand, value_expand, mla_output, grp_size
    )
    mla_half, mla_rest, prefill_part = lax.optimization_barrier(
        (mla_half, mla_rest, prefill_part)
    )
    prefill_parts = lax.all_to_all(
        prefill_part, "grp", split_axis=0, concat_axis=0, tiled=True
    )
    own_columns = lax.dynamic_slice_in_dim(x_group, grp_index * share, share, 1)
    prefill_out = gather_share(prefill_parts, own_columns).T

    hidden_share, keep, send = kda(
        grp_size,
        mla_half,
        mla_rest,
        dec,
        kda_inputs.transpose(1, 0, 2),
        kda_beta.T,
        decay_down,
        decay_up,
        gate_down,
        gate_up,
        jnp.repeat(jnp.exp(decay_log), DK)[None, :],
        states,
        kda_output,
    )
    crossing = swap(send)
    kda_total = keep[0] + crossing[0].astype(f32)
    for by in range(1, sides):
        pair = keep[by] + crossing[by].astype(f32)
        kda_total = kda_total + shift(pair.astype(bf16), by).astype(f32)
    decode_out = (hidden_share + kda_total).astype(bf16)
    return (prefill_out, decode_out.reshape(steps, requests, share))


def solution(mesh):
    in_specs = (
        P("seq", None),
        P(None, "seq", None),
        P("seq"),
        P("seq", None, None, None, None),
        P(None, "seq", None),
        P(None, "seq"),
        P(None, "grp", "seq", None),
        P(None, "grp"),
        P(),
        P(None, "grp"),
        P(None, "grp"),
        P("grp", None),
        P(None, None, "grp"),
        P(None, "grp"),
        P(),
        P(None, "grp"),
        P(),
        P(None, "grp"),
        P("grp"),
        P("grp", None),
    )
    out_specs = (P("seq", "grp"), P(None, "seq", "grp"))
    return jax.shard_map(shards, mesh=mesh, in_specs=in_specs, out_specs=out_specs, check_vma=False)
```

```python
import functools

import jax
import jax.numpy as jnp
import numpy as np
from jax import lax
from jax.experimental import pallas as pl
from jax.experimental.pallas import tpu as pltpu
from jax.sharding import PartitionSpec as P

LAT = 512
ROPE = 64
NOPE = 128
VH = 128
DK = 128
DV = 128
PAGE = 64
MAXP = 12
WIDE = LAT + ROPE
SENT = LAT + 128

epsilon = 1e-06
masked_score = -1e30
scale = (NOPE + ROPE) ** (-0.5)
log2e = 1.4426950408889634

f32 = jnp.float32
bf16 = jnp.bfloat16
MIB = 1024 * 1024


def params(mib=58):
    return pltpu.CompilerParams(vmem_limit_bytes=mib * MIB)


def dot_nt(a, b):
    return lax.dot_general(a, b, (((1,), (1,)), ((), ())), preferred_element_type=f32)


def dot_nn(a, b):
    return lax.dot_general(a, b, (((1,), (0,)), ((), ())), preferred_element_type=f32)


def norm_rows(values):
    return values * lax.rsqrt(jnp.mean(values * values, axis=-1, keepdims=True) + epsilon)


def unit_rows(values):
    return values * lax.rsqrt(jnp.sum(values * values, axis=-1, keepdims=True) + epsilon)


def turn(values, cos, sin):
    half = ROPE // 2
    swapped = jnp.concatenate([values[:, half:], values[:, :half]], axis=-1)
    return values * cos + swapped * sin


def rope_tables(positions):
    half = ROPE // 2
    frequency = np.exp(-np.log(10000.0) * np.arange(half) / half)
    angles = np.asarray(positions, np.float64)[:, None] * frequency
    cos, sin = np.cos(angles), np.sin(angles)
    both = np.concatenate([cos, cos, -sin, sin], -1)
    return jnp.asarray(both, f32)


def slice_kernel(pages_hbm, own_hbm, held, in_sems, out_sems):
    grp = lax.axis_index("grp")
    owners, slots, tokens, _ = own_hbm.shape
    parts = in_sems.shape[0]
    each = owners // parts
    first = lax.rem(grp, 2) * slots
    row = pl.multiple_of((grp // 2) * tokens, tokens)
    loads = [
        pltpu.make_async_copy(
            pages_hbm.at[pl.ds(i * each, each), pl.ds(first, slots), pl.ds(row, tokens), :],
            held.at[pl.ds(i * each, each)],
            in_sems.at[i],
        )
        for i in range(parts)
    ]
    stores = [
        pltpu.make_async_copy(
            held.at[pl.ds(i * each, each)], own_hbm.at[pl.ds(i * each, each)], out_sems.at[i]
        )
        for i in range(parts)
    ]
    for load in loads:
        load.start()
    for load, store in zip(loads, stores):
        load.wait()
        store.start()
    for store in stores:
        store.wait()


def slice_pages(pages, grp_size):
    owners, cap, page, wide = pages.shape
    shape = (owners, cap // 2, page // (grp_size // 2), wide)
    parts = 4
    hbm = pl.BlockSpec(memory_space=pltpu.HBM)
    return pl.pallas_call(
        slice_kernel,
        in_specs=[hbm],
        out_specs=hbm,
        out_shape=jax.ShapeDtypeStruct(shape, bf16),
        scratch_shapes=[
            pltpu.VMEM(shape, bf16),
            pltpu.SemaphoreType.DMA((parts,)),
            pltpu.SemaphoreType.DMA((parts,)),
        ],
        compiler_params=params(),
    )(pages)


def pack_rope(values):
    count = LAT // ROPE
    piece = values.shape[0] // count
    return jnp.concatenate(
        [values[i * piece : (i + 1) * piece] for i in range(count)], axis=1
    )


def unpack_rope(packed):
    return jnp.concatenate(
        [packed[:, i * ROPE : (i + 1) * ROPE] for i in range(LAT // ROPE)], axis=0
    )


def front_kernel(
    lengths_ref,
    fine_hbm,
    coarse_hbm,
    x_hbm,
    dec_hbm,
    lat_proj_hbm,
    query_proj_hbm,
    expand_hbm,
    state_hbm,
    lat_hbm,
    fresh_ref,
    qp_ref,
    qd_ref,
    state_out_ref,
    fine_ref,
    coarse_ref,
    x_ref,
    dec_ref,
    lat_proj_ref,
    query_proj_ref,
    expand_ref,
    state_ref,
    normed,
    turns,
    lat_ref,
    sems,
    out_sems,
):
    seq, grp = lax.axis_index("seq"), lax.axis_index("grp")
    rows, width = x_ref.shape
    count = dec_ref.shape[0]
    half_rows = rows // 2
    core = lax.rem(grp, 2)
    heads = qp_ref.shape[0]
    requests = lengths_ref.shape[0]
    chunks = 3
    depth = width // chunks
    loads = [
        pltpu.make_async_copy(x_hbm, x_ref, sems.at[0]),
        pltpu.make_async_copy(dec_hbm, dec_ref, sems.at[1]),
        pltpu.make_async_copy(lat_proj_hbm, lat_proj_ref, sems.at[2]),
        pltpu.make_async_copy(expand_hbm, expand_ref, sems.at[3]),
    ]
    loads += [
        pltpu.make_async_copy(
            query_proj_hbm.at[pl.ds(i * depth, depth)],
            query_proj_ref.at[pl.ds(i * depth, depth)],
            sems.at[4 + i],
        )
        for i in range(chunks)
    ]
    loads.append(pltpu.make_async_copy(state_hbm, state_ref, sems.at[4 + chunks]))
    loads.append(pltpu.make_async_copy(fine_hbm, fine_ref, sems.at[5 + chunks]))
    loads.append(pltpu.make_async_copy(coarse_hbm, coarse_ref, sems.at[6 + chunks]))
    for i in (0, 1, 2, 5 + chunks, 6 + chunks):
        loads[i].start()
    loads[0].wait()
    for i in range(4, 4 + chunks):
        loads[i].start()
    loads[3].start()
    normed[:rows] = norm_rows(x_ref[...].astype(f32)).astype(bf16)
    loads[1].wait()
    tail = normed.shape[0] - rows - count
    normed[rows:] = jnp.concatenate(
        [norm_rows(dec_ref[...].astype(f32)), jnp.zeros((tail, width), f32)], axis=0
    ).astype(bf16)
    loads[4 + chunks].start()
    loads[5 + chunks].wait()
    loads[6 + chunks].wait()
    for r in range(requests):
        for t in range(count // requests):
            at = rows + t * requests + r
            row = lengths_ref[r] + t
            turns[at : at + 1] = fine_ref[pl.ds(row, 1)]
    turns[rows + count :] = jnp.zeros((turns.shape[0] - rows - count, 2 * ROPE), f32)
    base, near = coarse_ref[pl.ds(seq, 1)], fine_ref[:rows]
    base_cos, base_sin = base[:, :ROPE], base[:, ROPE:]
    near_cos, near_sin = near[:, :ROPE], near[:, ROPE:]
    turns[:rows] = jnp.concatenate(
        [base_cos * near_cos - base_sin * near_sin, base_sin * near_cos + base_cos * near_sin],
        axis=-1,
    )
    loads[2].wait()

    own = pl.ds(pl.multiple_of(core * half_rows, half_rows), half_rows)
    projected = dot_nt(
        jnp.concatenate([normed[own], normed[rows:]], axis=0), lat_proj_ref[...]
    )
    around = jnp.concatenate([turns[own], turns[rows:]], axis=0)
    cos, sin = around[:, :ROPE], around[:, ROPE:]
    latent = jnp.concatenate(
        [norm_rows(projected[:, :LAT]), turn(projected[:, LAT:], cos, sin)], axis=-1
    )
    lat_ref[:half_rows] = latent[:half_rows, :LAT].astype(bf16)
    lat_ref[half_rows:] = pack_rope(latent[:half_rows, LAT:]).astype(bf16)
    stores = [
        pltpu.make_async_copy(lat_ref, lat_hbm.at[i], out_sems.at[i])
        for i in range(lat_hbm.shape[0])
    ]
    for store in stores:
        store.start()
    fresh_ref[...] = latent[half_rows:].astype(bf16)
    total = None
    for i in range(chunks):
        loads[4 + i].wait()
        lanes = slice(i * depth, (i + 1) * depth)
        term = dot_nn(normed[:, lanes], query_proj_ref[lanes])
        total = term if total is None else total + term
    loads[3].wait()
    fold = scale * log2e
    decode = []
    cos, sin = turns[:, :ROPE], turns[:, ROPE:]
    for head in range(heads):
        at = head * (NOPE + ROPE)
        nope = total[:, at : at + NOPE]
        turned = turn(total[:, at + NOPE : at + NOPE + ROPE], cos, sin)
        qp_ref[head] = (
            jnp.concatenate([nope[:rows], turned[:rows]], axis=-1) * fold
        ).astype(bf16)
        absorbed = dot_nt(
            nope[rows:].astype(bf16), expand_ref[:, head * NOPE : (head + 1) * NOPE]
        )
        blank = jnp.zeros((absorbed.shape[0], SENT - WIDE), f32)
        decode.append(jnp.concatenate([absorbed, turned[rows:], blank], axis=-1)[:count])
    qd_ref[...] = (jnp.concatenate(decode, axis=0) * fold).astype(bf16)
    loads[4 + chunks].wait()
    state_out_ref[...] = state_ref[...].astype(bf16)
    for store in stores:
        store.wait()


def front(lengths, x, dec, lat_proj_t, query_proj, key_expand, states, seq_size):
    rows, width = x.shape
    count = dec.shape[0]
    heads = key_expand.shape[1] // NOPE
    padded = count + 8
    requests = lengths.shape[0]
    reach = max(rows, MAXP * PAGE + count // requests)
    fine = rope_tables(range(-(-reach // 8) * 8))
    coarse = rope_tables([rows * i for i in range(seq_size)])
    smem = pl.BlockSpec(memory_space=pltpu.SMEM)
    vmem = pl.BlockSpec(memory_space=pltpu.VMEM)
    hbm = pl.BlockSpec(memory_space=pltpu.HBM)
    return pl.pallas_call(
        front_kernel,
        in_specs=[smem] + [hbm] * 8,
        out_specs=(hbm, vmem, vmem, vmem, vmem),
        out_shape=(
            jax.ShapeDtypeStruct((seq_size, rows // 2 + rows * ROPE // (2 * LAT), LAT), bf16),
            jax.ShapeDtypeStruct((padded, WIDE), bf16),
            jax.ShapeDtypeStruct((heads, rows, NOPE + ROPE), bf16),
            jax.ShapeDtypeStruct((heads * count, SENT), bf16),
            jax.ShapeDtypeStruct(states.shape, bf16),
        ),
        scratch_shapes=[
            pltpu.VMEM(fine.shape, f32),
            pltpu.VMEM(coarse.shape, f32),
            pltpu.VMEM(x.shape, bf16),
            pltpu.VMEM(dec.shape, bf16),
            pltpu.VMEM(lat_proj_t.shape, bf16),
            pltpu.VMEM(query_proj.shape, bf16),
            pltpu.VMEM(key_expand.shape, bf16),
            pltpu.VMEM(states.shape, f32),
            pltpu.VMEM((rows + padded, width), bf16),
            pltpu.VMEM((rows + padded, 2 * ROPE), f32),
            pltpu.VMEM((rows // 2 + rows * ROPE // (2 * LAT), LAT), bf16),
            pltpu.SemaphoreType.DMA((10,)),
            pltpu.SemaphoreType.DMA((seq_size,)),
        ],
        compiler_params=params(),
    )(lengths, fine, coarse, x, dec, lat_proj_t, query_proj, key_expand, states)


def pack_shares(summed, sum_ref):
    shares = sum_ref.shape[0]
    rows, width = summed.shape
    share = width // shares
    for g in range(shares):
        part = summed[:, g * share : (g + 1) * share]
        sum_ref[g, :rows] = part[:, :128].astype(bf16)
        sum_ref[g, rows : 2 * rows] = part[:, 128:256].astype(bf16)
        rest = part[:, 256:]
        count = 128 // rest.shape[1]
        piece = rows // count
        sum_ref[g, 2 * rows :] = jnp.concatenate(
            [rest[i * piece : (i + 1) * piece] for i in range(count)], axis=1
        ).astype(bf16)


def flash_kernel(
    heads, q_ref, mine_ref, other_ref, ke_ref, ve_ref, out_hbm, sum_ref,
    peak, acc, vet_ref, out_ref, sem,
):
    step = pl.program_id(0)
    rows = q_ref.shape[1]
    half = rows // 2
    first, core = lax.axis_index("seq") * rows, lax.rem(lax.axis_index("grp"), 2)
    side = mine_ref.shape[0] * half
    block = 2 * side
    load = pltpu.make_async_copy(out_hbm, out_ref, sem)

    @pl.when(step == 0)
    def _():
        load.start()
        vet_ref[...] = ve_ref[...].astype(f32).T.astype(bf16)
        peak[...] = jnp.full_like(peak, masked_score)
        acc[...] = jnp.zeros_like(acc)

    def work(masked):
        sources = [(ref, i) for ref in (mine_ref, other_ref) for i in range(ref.shape[0])]
        low = jnp.concatenate([ref[i, :half] for ref, i in sources], axis=0)
        rope = jnp.concatenate([unpack_rope(ref[i, half:]) for ref, i in sources], axis=0)
        ones = jnp.ones((16, block), bf16)
        keys = dot_nn(low, ke_ref[...]).astype(bf16)
        values = dot_nt(vet_ref[...], low).astype(bf16)
        scores = []
        for head in range(heads):
            whole_keys = jnp.concatenate(
                [keys[:, head * NOPE : (head + 1) * NOPE], rope], axis=-1
            )
            scores.append(dot_nt(whole_keys, q_ref[head]))
        if masked:
            row = lax.broadcasted_iota(jnp.int32, (block, rows), 0)
            from_other = row >= side
            row = jnp.where(from_other, row - side, row)
            which = jnp.where(from_other, 1 - core, core)
            key_pos = step * block + (row // half) * rows + which * half + lax.rem(row, half)
            live = key_pos <= first + lax.broadcasted_iota(jnp.int32, (block, rows), 1)
            scores = [jnp.where(live, s, masked_score) for s in scores]
        for head in range(heads):
            old = peak[head]
            new = jnp.maximum(old, jnp.max(scores[head], axis=0, keepdims=True))
            fade = jnp.exp2(old - new)
            weights = jnp.exp2(scores[head] - new).astype(bf16)
            peak[head] = new
            carried = jnp.concatenate([values[head * VH : (head + 1) * VH], ones], axis=0)
            acc[head] = acc[head] * fade + dot_nn(carried, weights)

    @pl.when((step + 1) * block <= first + 1)
    def _():
        work(False)

    @pl.when(((step + 1) * block > first + 1) & (step * block < first + rows))
    def _():
        work(True)

    @pl.when(step == pl.num_programs(0) - 1)
    def _():
        mixed = jnp.concatenate(
            [(acc[h, :VH] / acc[h, VH : VH + 1]).T for h in range(heads)], axis=-1
        ).astype(bf16)
        load.wait()
        pack_shares(dot_nn(mixed, out_ref[...]), sum_ref)


def prefill_attend(q, mine, other, key_expand, value_expand, mla_output, shares):
    heads, rows, _ = q.shape
    sources, packed, _ = mine.shape
    side = max(1, min(sources, 1024 // rows))
    width = mla_output.shape[1]
    dense = rows * width // shares // 128
    whole = lambda shape: pl.BlockSpec(shape, lambda i: (0,) * len(shape))
    return pl.pallas_call(
        functools.partial(flash_kernel, heads),
        grid=(sources // side,),
        in_specs=[
            whole(q.shape),
            pl.BlockSpec((side, packed, LAT), lambda i: (i, 0, 0)),
            pl.BlockSpec((side, packed, LAT), lambda i: (i, 0, 0)),
            whole(key_expand.shape),
            whole(value_expand.shape),
            pl.BlockSpec(memory_space=pltpu.HBM),
        ],
        out_specs=whole((shares, dense, 128)),
        scratch_shapes=[
            pltpu.VMEM((heads, 1, rows), f32),
            pltpu.VMEM((heads, VH + 16, rows), f32),
            pltpu.VMEM((value_expand.shape[1], value_expand.shape[0]), bf16),
            pltpu.VMEM(mla_output.shape, bf16),
            pltpu.SemaphoreType.DMA,
        ],
        out_shape=jax.ShapeDtypeStruct((shares, dense, 128), bf16),
        compiler_params=params(),
    )(q, mine, other, key_expand, value_expand, mla_output)


def gather_share_kernel(parts_ref, x_ref, out_ref):
    rows, share = x_ref.shape
    x = x_ref[...].astype(f32)
    total = jnp.sum(parts_ref[...].astype(f32), axis=0)
    left = total[:rows] + x[:, :128]
    right = total[rows : 2 * rows] + x[:, 128:256]
    rest = total[2 * rows :]
    wide = share - 256
    rest = jnp.concatenate(
        [rest[:, i * wide : (i + 1) * wide] for i in range(128 // wide)], axis=0
    )
    rest = rest + x[:, 256:]
    out_ref[...] = jnp.concatenate([left.T, right.T, rest.T], axis=0).astype(bf16)


def gather_share(parts, x):
    rows, share = x.shape
    return pl.pallas_call(
        gather_share_kernel,
        out_shape=jax.ShapeDtypeStruct((share, rows), bf16),
        compiler_params=params(20),
    )(parts, x)


def split_level(level, rows):
    lane = lax.broadcasted_iota(jnp.int32, (rows, SENT - LAT), 1)
    high = level.astype(bf16).astype(f32)
    middle = (level - high).astype(bf16).astype(f32)
    low = level - high - middle
    return jnp.where(
        lane == 0, high, jnp.where(lane == 1, middle, jnp.where(lane == 2, low, 0.0))
    )


def join_level(part):
    tail = part[:, LAT:].astype(f32)
    lane = lax.broadcasted_iota(jnp.int32, tail.shape, 1)
    return jnp.sum(jnp.where(lane < 3, tail, 0.0), axis=-1, keepdims=True)


def merge_parts(parts):
    levels = [join_level(p) for p in parts]
    highest = functools.reduce(jnp.maximum, levels)
    weights = [jnp.exp2(v - highest) for v in levels]
    total = sum(weights)
    mixed = sum(p[:, :LAT].astype(f32) * w for p, w in zip(parts, weights)) / total
    return mixed, highest + jnp.log2(total)


def pages_kernel(group, requests, count, *refs):
    q_refs = refs[: 2 * count]
    keys_ref, fresh_ref, owner_ref, keep_ref, send_ref = refs[2 * count :]
    each = q_refs[0].shape[0]
    block = 2 * each
    keys = keys_ref[...]
    fresh = fresh_ref[...]
    within = lax.rem(lax.broadcasted_iota(jnp.int32, (block, 1), 0), group)
    request = lax.rem(within, requests)
    step = within // requests
    live_old = owner_ref[...] == request
    column = lax.broadcasted_iota(jnp.int32, (1, fresh.shape[0]), 1)
    fresh_step = column // requests + lax.axis_index("grp") * group
    live_new = (lax.rem(column, requests) == request) & (fresh_step <= step)
    scores = []
    for i in range(0, 2 * count, 2):
        q = jnp.concatenate([q_refs[i][:, :WIDE], q_refs[i + 1][:, :WIDE]], axis=0)
        scores.append(
            (
                jnp.where(live_old, dot_nt(q, keys), masked_score),
                jnp.where(live_new, dot_nt(q, fresh), masked_score),
            )
        )
    for i, (old, new) in enumerate(scores):
        highest = jnp.maximum(
            jnp.max(old, axis=-1, keepdims=True), jnp.max(new, axis=-1, keepdims=True)
        )
        highest = jnp.maximum(highest, 0.1 * masked_score)
        w_old = jnp.exp2(old - highest)
        w_new = jnp.exp2(new - highest)
        total = jnp.sum(w_old, axis=-1, keepdims=True) + jnp.sum(w_new, axis=-1, keepdims=True)
        some = total > 0.0
        safe = jnp.where(some, total, 1.0)
        mixed = dot_nn(w_old.astype(bf16), keys[:, :LAT]) + dot_nn(
            w_new.astype(bf16), fresh[:, :LAT]
        )
        level = jnp.where(some, highest + jnp.log2(safe), masked_score)
        out_ref = keep_ref if 2 * i < count else send_ref
        both = jnp.concatenate([mixed / safe, split_level(level, block)], axis=-1).astype(bf16)
        out_ref[2 * i % count] = both[:each]
        out_ref[2 * i % count + 1] = both[each:]


def pages_attend(queries, keys, fresh, owner, group, requests):
    count = len(queries) // 2
    vmem = pl.BlockSpec(memory_space=pltpu.VMEM)
    shape = jax.ShapeDtypeStruct((count, queries[0].shape[0], SENT), bf16)
    return pl.pallas_call(
        functools.partial(pages_kernel, group, requests, count),
        in_specs=[vmem] * (2 * count + 3),
        out_specs=(vmem, vmem),
        out_shape=(shape, shape),
        compiler_params=params(24),
    )(*queries, keys, fresh, owner)


def merge_kernel(keep_ref, got_ref, *out_refs):
    for i, out_ref in enumerate(out_refs):
        mixed, level = merge_parts([keep_ref[i], got_ref[i]])
        out_ref[...] = jnp.concatenate(
            [mixed, split_level(level, mixed.shape[0])], axis=-1
        ).astype(bf16)


def merge_pair(keep, got):
    shape = jax.ShapeDtypeStruct(keep.shape[1:], bf16)
    return pl.pallas_call(
        merge_kernel,
        out_shape=(shape,) * keep.shape[0],
        compiler_params=params(24),
    )(keep, got)


def combine_kernel(heads, count, *refs):
    ve_ref, out_ref, sum_ref = refs[count:]
    mixed, _ = merge_parts([ref[...] for ref in refs[:count]])
    each = mixed.shape[0] // heads
    head_values = [
        dot_nn(mixed[h * each : (h + 1) * each].astype(bf16), ve_ref[:, h * VH : (h + 1) * VH])
        for h in range(heads)
    ]
    joined = jnp.concatenate(head_values, axis=-1).astype(bf16)
    sum_ref[...] = dot_nn(joined, out_ref[...]).astype(bf16)


def combine(parts, value_expand, mla_output):
    heads = value_expand.shape[1] // VH
    return pl.pallas_call(
        functools.partial(combine_kernel, heads, len(parts)),
        out_shape=jax.ShapeDtypeStruct((parts[0].shape[0] // heads, mla_output.shape[1]), bf16),
        compiler_params=params(20),
    )(*parts, value_expand, mla_output)


def kda_kernel(
    heads,
    requests,
    rate_ref,
    one_hbm,
    two_hbm,
    dec_hbm,
    inputs_hbm,
    beta_hbm,
    decay_down_hbm,
    gate_down_hbm,
    decay_up_hbm,
    gate_up_hbm,
    states_hbm,
    output_hbm,
    hidden_ref,
    keep_ref,
    send_ref,
    one_ref,
    two_ref,
    dec_ref,
    inputs_ref,
    beta_ref,
    decay_down_ref,
    gate_down_ref,
    decay_up_ref,
    gate_up_ref,
    states_ref,
    output_ref,
    by_share,
    summed_ref,
    sems,
):
    shares, rows, share = by_share.shape
    grp = lax.axis_index("grp")
    pairs = [
        (one_hbm, one_ref),
        (two_hbm, two_ref),
        (dec_hbm, dec_ref),
        (inputs_hbm.at[1], inputs_ref.at[1]),
        (beta_hbm, beta_ref),
        (decay_down_hbm, decay_down_ref),
        (gate_down_hbm, gate_down_ref),
        (decay_up_hbm, decay_up_ref),
        (gate_up_hbm, gate_up_ref),
        (inputs_hbm.at[0], inputs_ref.at[0]),
        (states_hbm, states_ref),
        (inputs_hbm.at[2], inputs_ref.at[2]),
        (output_hbm, output_ref),
    ]
    loads = [pltpu.make_async_copy(a, b, sems.at[i]) for i, (a, b) in enumerate(pairs)]
    for load in loads:
        load.start()
    for load in loads[:3]:
        load.wait()
    hidden = dec_ref[...].astype(f32) + one_ref[...] + two_ref[...]
    for g in range(shares):
        by_share[g] = hidden[:, g * share : (g + 1) * share]
    hidden_ref[...] = by_share[grp]
    kin = norm_rows(hidden).astype(bf16)
    loads[3].wait()
    all_keys = dot_nn(kin, inputs_ref[1])
    for load in loads[4:9]:
        load.wait()
    beta = jax.nn.sigmoid(dot_nt(kin, beta_ref[...]))
    decay_low = dot_nn(kin, decay_down_ref[...]).astype(bf16)
    rises = jax.nn.softplus(dot_nn(decay_low, decay_up_ref[...]))
    gate_low = dot_nn(kin, gate_down_ref[...]).astype(bf16)
    gates = jax.nn.sigmoid(dot_nn(gate_low, gate_up_ref[...]))
    loads[9].wait()
    all_queries = dot_nn(kin, inputs_ref[0])
    loads[10].wait()
    held_states = [states_ref[:, r].astype(f32) for r in range(requests)]
    steps = rows // requests
    piece = held_states[0].shape[1] // heads
    at = lambda values, t: values[t * requests : (t + 1) * requests]
    along = lambda a, b: jnp.sum(a * b, axis=-1, keepdims=True)
    ready = []
    for head in range(heads):
        lanes = slice(head * DK, (head + 1) * DK)
        q = unit_rows(all_queries[:, lanes]) * DK ** (-0.5)
        k = unit_rows(all_keys[:, lanes])
        rate = jnp.exp(jnp.full((1, DK), rate_ref[head], f32))
        a = jnp.exp(-rate * rises[:, lanes])
        vectors = []
        kept = None
        for t in range(steps):
            kept = at(a, t) if kept is None else kept * at(a, t)
            vectors += [kept * at(k, t), kept * at(q, t)]
        vectors = jnp.concatenate(vectors, axis=0)
        high = vectors.astype(bf16).astype(f32)
        both = jnp.concatenate([high, vectors - high], axis=0)
        owner = lax.rem(lax.broadcasted_iota(jnp.int32, (both.shape[0], 1), 0), requests)
        spread = jnp.concatenate(
            [jnp.where(owner == r, both, 0.0) for r in range(requests)], axis=-1
        ).astype(bf16)
        facing = jnp.concatenate(
            [
                held_states[r][:, head * piece : (head + 1) * piece].reshape(DV, DK)
                for r in range(requests)
            ],
            axis=-1,
        ).astype(bf16)
        met = dot_nt(spread, facing)
        ready.append((q, k, a, met[: vectors.shape[0]] + met[vectors.shape[0] :]))
    loads[11].wait()
    all_values = dot_nn(kin, inputs_ref[2])
    blended = []
    for head in range(heads):
        lanes = slice(head * DK, (head + 1) * DK)
        q, k, a, met = ready[head]
        v = all_values[:, lanes]
        b = beta[:, head : head + 1]
        carried = []
        reads = []
        for t in range(steps):
            seen = at(met, 2 * t)
            read = at(met, 2 * t + 1)
            carried = [(u, w * at(a, t)) for u, w in carried]
            for u, w in carried:
                seen = seen + u * along(w, at(k, t))
            u = at(b, t) * (at(v, t) - seen)
            carried.append((u, at(k, t)))
            for u, w in carried:
                read = read + u * along(w, at(q, t))
            reads.append(read)
        read = jnp.concatenate(reads, axis=0)
        blended.append(norm_rows(read) * gates[:, lanes])
    mixed = jnp.concatenate(blended, axis=-1).astype(bf16)
    loads[12].wait()
    summed = dot_nn(mixed, output_ref[...])
    for g in range(shares):
        summed_ref[g] = summed[:, g * share : (g + 1) * share]
    core = lax.rem(grp, 2)
    for by in range(shares // 2):
        pair = 2 * lax.rem(grp // 2 + by, shares // 2)
        keep_ref[by] = summed_ref[pair + core]
        send_ref[by] = summed_ref[pair + 1 - core].astype(bf16)


def kda(shares, rate, *operands):
    dec, beta_t, states = operands[2], operands[4], operands[9]
    rows, width = dec.shape
    heads = beta_t.shape[0]
    requests = states.shape[1]
    share = width // shares
    sides = shares // 2
    vmem = pl.BlockSpec(memory_space=pltpu.VMEM)
    return pl.pallas_call(
        functools.partial(kda_kernel, heads, requests),
        in_specs=[pl.BlockSpec(memory_space=pltpu.SMEM)]
        + [pl.BlockSpec(memory_space=pltpu.HBM)] * len(operands),
        out_specs=(vmem, vmem, vmem),
        out_shape=(
            jax.ShapeDtypeStruct((rows, share), f32),
            jax.ShapeDtypeStruct((sides, rows, share), f32),
            jax.ShapeDtypeStruct((sides, rows, share), bf16),
        ),
        scratch_shapes=[pltpu.VMEM(a.shape, a.dtype) for a in operands]
        + [
            pltpu.VMEM((shares, rows, share), f32),
            pltpu.VMEM((shares, rows, share), f32),
            pltpu.SemaphoreType.DMA((len(operands) + 2,)),
        ],
        compiler_params=params(),
    )(rate, *operands)


def shards(
    x_group,
    decode_input,
    prompt_len,
    latent_pages,
    slot_target,
    page_counts,
    kda_state,
    query_proj,
    latent_proj,
    key_expand,
    value_expand,
    mla_output,
    kda_inputs,
    kda_beta,
    decay_down,
    decay_up,
    gate_down,
    gate_up,
    decay_log,
    kda_output,
):
    seq_index = lax.axis_index("seq")
    grp_index = lax.axis_index("grp")
    seq_size = lax.axis_size("seq")
    grp_size = lax.axis_size("grp")
    rows, width = x_group.shape
    steps, requests, _ = decode_input.shape
    decode_rows = steps * requests
    share = width // grp_size
    dec = decode_input.reshape(decode_rows, width)

    own_tokens = slice_pages(latent_pages[0], grp_size)
    _, slots, tokens, _ = own_tokens.shape
    core = grp_index % 2
    target = lax.dynamic_slice_in_dim(slot_target[:, 0, :], core * slots, slots, 1)
    owner = target // MAXP
    lengths = jnp.sum(
        jnp.where(owner[..., None] == jnp.arange(requests), prompt_len, 0), axis=-1
    )
    held = core * slots + jnp.arange(slots)[None, :] < page_counts
    token_pos = (
        ((target % MAXP) * PAGE + (grp_index // 2) * tokens)[..., None] + jnp.arange(tokens)
    )
    key_owner = jnp.where(
        held[..., None] & (token_pos < lengths[..., None]), owner[..., None], -1
    ).reshape(1, -1)

    x_rows, _, key_owner = lax.optimization_barrier((x_group, own_tokens, key_owner))
    own_latent, fresh, q_prefill, q_decode, state_rows = front(
        prompt_len,
        x_rows,
        dec,
        latent_proj.T,
        query_proj,
        key_expand,
        kda_state.reshape(kda_state.shape[0], -1, DK),
        seq_size,
    )
    sides = grp_size // 2

    def shift(value, by):
        return lax.ppermute(
            value, "grp", [(g, (g + 2 * by) % grp_size) for g in range(grp_size)]
        )

    def swap(value):
        return lax.ppermute(value, "grp", [(g, g ^ 1) for g in range(grp_size)])

    arrived = lax.all_to_all(own_tokens, "seq", split_axis=0, concat_axis=0, tiled=True)
    queries = [q_decode] + [shift(q_decode, by) for by in range(1, sides)]
    own_latent, _, _ = lax.optimization_barrier((own_latent, arrived, queries[1]))
    mine = lax.all_to_all(own_latent, "seq", split_axis=0, concat_axis=0, tiled=True)
    page_keys = arrived.reshape(-1, WIDE)
    queries = queries + [swap(q) for q in queries]
    keep, send = pages_attend(
        queries, page_keys, fresh, key_owner, decode_rows, requests
    )
    merged = merge_pair(keep, swap(send))
    state_rows, _ = lax.optimization_barrier((state_rows, mine))
    states = lax.all_to_all(
        state_rows, "seq", split_axis=0, concat_axis=0, tiled=True
    ).reshape((seq_size, requests) + state_rows.shape[1:])
    partial = [merged[0]] + [shift(merged[by], -by) for by in range(1, sides)]
    mla_part = combine(partial, value_expand, mla_output)
    mine, _ = lax.optimization_barrier((mine, mla_part))
    mla_half = mla_part.astype(f32)
    for by in range(1, sides):
        mla_half = mla_half + shift(mla_part, by).astype(f32)
    mla_rest = swap(mla_half)

    prefill_part = prefill_attend(
        q_prefill, mine, swap(mine), key_expand, value_expand, mla_output, grp_size
    )
    mla_half, mla_rest, prefill_part = lax.optimization_barrier(
        (mla_half, mla_rest, prefill_part)
    )
    prefill_parts = lax.all_to_all(
        prefill_part, "grp", split_axis=0, concat_axis=0, tiled=True
    )
    own_columns = lax.dynamic_slice_in_dim(x_group, grp_index * share, share, 1)
    prefill_out = gather_share(prefill_parts, own_columns).T

    hidden_share, keep, send = kda(
        grp_size,
        decay_log,
        mla_half,
        mla_rest,
        dec,
        kda_inputs.transpose(1, 0, 2),
        kda_beta.T,
        decay_down,
        gate_down,
        decay_up,
        gate_up,
        states,
        kda_output,
    )
    crossing = swap(send)
    kda_total = keep[0] + crossing[0].astype(f32)
    for by in range(1, sides):
        pair = keep[by] + crossing[by].astype(f32)
        kda_total = kda_total + shift(pair.astype(bf16), by).astype(f32)
    decode_out = (hidden_share + kda_total).astype(bf16)
    return (prefill_out, decode_out.reshape(steps, requests, share))


def solution(mesh):
    in_specs = (
        P("seq", None),
        P(None, "seq", None),
        P("seq"),
        P("seq", None, None, None, None),
        P(None, "seq", None),
        P(None, "seq"),
        P(None, "grp", "seq", None),
        P(None, "grp"),
        P(),
        P(None, "grp"),
        P(None, "grp"),
        P("grp", None),
        P(None, None, "grp"),
        P(None, "grp"),
        P(),
        P(None, "grp"),
        P(),
        P(None, "grp"),
        P("grp"),
        P("grp", None),
    )
    out_specs = (P("seq", "grp"), P(None, "seq", "grp"))
    return jax.shard_map(shards, mesh=mesh, in_specs=in_specs, out_specs=out_specs, check_vma=False)
```

```python
import functools

import jax
import jax.numpy as jnp
import numpy as np
from jax import lax
from jax.experimental import pallas as pl
from jax.experimental.pallas import tpu as pltpu
from jax.sharding import PartitionSpec as P

LAT = 512
ROPE = 64
NOPE = 128
VH = 128
DK = 128
DV = 128
PAGE = 64
MAXP = 12
WIDE = LAT + ROPE
SENT = LAT + 128

epsilon = 1e-06
masked_score = -1e30
scale = (NOPE + ROPE) ** (-0.5)
log2e = 1.4426950408889634

f32 = jnp.float32
bf16 = jnp.bfloat16
MIB = 1024 * 1024


def params(mib=58):
    return pltpu.CompilerParams(vmem_limit_bytes=mib * MIB)


def dot_nt(a, b):
    return lax.dot_general(a, b, (((1,), (1,)), ((), ())), preferred_element_type=f32)


def dot_nn(a, b):
    return lax.dot_general(a, b, (((1,), (0,)), ((), ())), preferred_element_type=f32)


def norm_rows(values):
    return values * lax.rsqrt(jnp.mean(values * values, axis=-1, keepdims=True) + epsilon)


def unit_rows(values):
    return values * lax.rsqrt(jnp.sum(values * values, axis=-1, keepdims=True) + epsilon)


def turn(values, cos, sin):
    half = ROPE // 2
    swapped = jnp.concatenate([values[:, half:], values[:, :half]], axis=-1)
    return values * cos + swapped * sin


def rope_tables(positions):
    half = ROPE // 2
    frequency = np.exp(-np.log(10000.0) * np.arange(half) / half)
    angles = np.asarray(positions, np.float64)[:, None] * frequency
    cos, sin = np.cos(angles), np.sin(angles)
    both = np.concatenate([cos, cos, -sin, sin], -1)
    return jnp.asarray(both, f32)


def slice_kernel(pages_hbm, own_hbm, held, in_sems, out_sems):
    grp = lax.axis_index("grp")
    owners, slots, tokens, _ = own_hbm.shape
    parts = in_sems.shape[0]
    each = owners // parts
    first = lax.rem(grp, 2) * slots
    row = pl.multiple_of((grp // 2) * tokens, tokens)
    loads = [
        pltpu.make_async_copy(
            pages_hbm.at[pl.ds(i * each, each), pl.ds(first, slots), pl.ds(row, tokens), :],
            held.at[pl.ds(i * each, each)],
            in_sems.at[i],
        )
        for i in range(parts)
    ]
    stores = [
        pltpu.make_async_copy(
            held.at[pl.ds(i * each, each)], own_hbm.at[pl.ds(i * each, each)], out_sems.at[i]
        )
        for i in range(parts)
    ]
    for load in loads:
        load.start()
    for load, store in zip(loads, stores):
        load.wait()
        store.start()
    for store in stores:
        store.wait()


def slice_pages(pages, grp_size):
    owners, cap, page, wide = pages.shape
    shape = (owners, cap // 2, page // (grp_size // 2), wide)
    parts = 4
    hbm = pl.BlockSpec(memory_space=pltpu.HBM)
    return pl.pallas_call(
        slice_kernel,
        in_specs=[hbm],
        out_specs=hbm,
        out_shape=jax.ShapeDtypeStruct(shape, bf16),
        scratch_shapes=[
            pltpu.VMEM(shape, bf16),
            pltpu.SemaphoreType.DMA((parts,)),
            pltpu.SemaphoreType.DMA((parts,)),
        ],
        compiler_params=params(),
    )(pages)


def pack_rope(values):
    count = LAT // ROPE
    piece = values.shape[0] // count
    return jnp.concatenate(
        [values[i * piece : (i + 1) * piece] for i in range(count)], axis=1
    )


def unpack_rope(packed):
    return jnp.concatenate(
        [packed[:, i * ROPE : (i + 1) * ROPE] for i in range(LAT // ROPE)], axis=0
    )


def turned_tables(base, near):
    base_cos, base_sin = base[:, :ROPE], base[:, ROPE:]
    near_cos, near_sin = near[:, :ROPE], near[:, ROPE:]
    return jnp.concatenate(
        [base_cos * near_cos - base_sin * near_sin, base_sin * near_cos + base_cos * near_sin],
        axis=-1,
    )


def front_kernel(
    count,
    lengths_ref,
    fine_hbm,
    coarse_hbm,
    x_hbm,
    dec_hbm,
    lat_proj_hbm,
    query_proj_hbm,
    expand_hbm,
    lat_hbm,
    fresh_ref,
    qd_ref,
    fine_ref,
    coarse_ref,
    x_ref,
    dec_ref,
    lat_proj_ref,
    query_proj_ref,
    expand_ref,
    normed,
    turns,
    lat_ref,
    sems,
    out_sems,
):
    seq, grp = lax.axis_index("seq"), lax.axis_index("grp")
    rows, width = x_ref.shape
    core = lax.rem(grp, 2)
    heads = expand_ref.shape[1] // NOPE
    requests = lengths_ref.shape[0]
    chunks = 3
    depth = width // chunks
    own = pl.ds(pl.multiple_of(core * rows, rows), rows)
    first = [
        pltpu.make_async_copy(x_hbm.at[own], x_ref, sems.at[0]),
        pltpu.make_async_copy(dec_hbm, dec_ref, sems.at[1]),
        pltpu.make_async_copy(lat_proj_hbm, lat_proj_ref, sems.at[2]),
        pltpu.make_async_copy(fine_hbm, fine_ref, sems.at[3]),
        pltpu.make_async_copy(coarse_hbm, coarse_ref, sems.at[4]),
    ]
    later = [
        pltpu.make_async_copy(
            query_proj_hbm.at[pl.ds(i * depth, depth)],
            query_proj_ref.at[pl.ds(i * depth, depth)],
            sems.at[5 + i],
        )
        for i in range(chunks)
    ]
    later.append(pltpu.make_async_copy(expand_hbm, expand_ref, sems.at[5 + chunks]))
    for load in first + later:
        load.start()
    first[0].wait()
    normed[:rows] = norm_rows(x_ref[...].astype(f32)).astype(bf16)
    first[1].wait()
    tail = normed.shape[0] - rows - count
    normed[rows:] = jnp.concatenate(
        [norm_rows(dec_ref[...].astype(f32)), jnp.zeros((tail, width), f32)], axis=0
    ).astype(bf16)
    first[3].wait()
    first[4].wait()
    for r in range(requests):
        for t in range(count // requests):
            at = rows + t * requests + r
            turns[at : at + 1] = fine_ref[pl.ds(lengths_ref[r] + t, 1)]
    turns[rows + count :] = jnp.zeros((tail, 2 * ROPE), f32)
    turns[:rows] = turned_tables(coarse_ref[pl.ds(seq, 1)], fine_ref[own])
    first[2].wait()
    projected = dot_nt(normed[...], lat_proj_ref[...])
    cos, sin = turns[:, :ROPE], turns[:, ROPE:]
    latent = jnp.concatenate(
        [norm_rows(projected[:, :LAT]), turn(projected[:, LAT:], cos, sin)], axis=-1
    )
    lat_ref[:rows] = latent[:rows, :LAT].astype(bf16)
    lat_ref[rows:] = pack_rope(latent[:rows, LAT:]).astype(bf16)
    stores = [
        pltpu.make_async_copy(lat_ref, lat_hbm.at[i], out_sems.at[i])
        for i in range(lat_hbm.shape[0])
    ]
    for store in stores:
        store.start()
    fresh_ref[...] = latent[rows:].astype(bf16)
    total = None
    for i in range(chunks):
        later[i].wait()
        lanes = slice(i * depth, (i + 1) * depth)
        term = dot_nn(normed[rows:, lanes], query_proj_ref[lanes])
        total = term if total is None else total + term
    later[chunks].wait()
    decode = []
    for head in range(heads):
        at = head * (NOPE + ROPE)
        turned = turn(total[:, at + NOPE : at + NOPE + ROPE], cos[rows:], sin[rows:])
        absorbed = dot_nt(
            total[:, at : at + NOPE].astype(bf16),
            expand_ref[:, head * NOPE : (head + 1) * NOPE],
        )
        blank = jnp.zeros((absorbed.shape[0], SENT - WIDE), f32)
        decode.append(jnp.concatenate([absorbed, turned, blank], axis=-1)[:count])
    qd_ref[...] = (jnp.concatenate(decode, axis=0) * (scale * log2e)).astype(bf16)
    for store in stores:
        store.wait()


def front(lengths, fine, coarse, x, dec, lat_proj_t, query_proj, key_expand):
    rows, width = x.shape
    half = rows // 2
    count = dec.shape[0]
    heads = key_expand.shape[1] // NOPE
    padded = count + 8
    packed = half + half * ROPE // LAT
    seq_size = coarse.shape[0]
    smem = pl.BlockSpec(memory_space=pltpu.SMEM)
    vmem = pl.BlockSpec(memory_space=pltpu.VMEM)
    hbm = pl.BlockSpec(memory_space=pltpu.HBM)
    return pl.pallas_call(
        functools.partial(front_kernel, count),
        in_specs=[smem] + [hbm] * 7,
        out_specs=(hbm, vmem, vmem),
        out_shape=(
            jax.ShapeDtypeStruct((seq_size, packed, LAT), bf16),
            jax.ShapeDtypeStruct((padded, WIDE), bf16),
            jax.ShapeDtypeStruct((heads * count, SENT), bf16),
        ),
        scratch_shapes=[
            pltpu.VMEM(fine.shape, f32),
            pltpu.VMEM(coarse.shape, f32),
            pltpu.VMEM((half, width), bf16),
            pltpu.VMEM(dec.shape, bf16),
            pltpu.VMEM(lat_proj_t.shape, bf16),
            pltpu.VMEM(query_proj.shape, bf16),
            pltpu.VMEM(key_expand.shape, bf16),
            pltpu.VMEM((half + padded, width), bf16),
            pltpu.VMEM((half + padded, 2 * ROPE), f32),
            pltpu.VMEM((packed, LAT), bf16),
            pltpu.SemaphoreType.DMA((9,)),
            pltpu.SemaphoreType.DMA((seq_size,)),
        ],
        compiler_params=params(),
    )(lengths, fine, coarse, x, dec, lat_proj_t, query_proj, key_expand)


def prefill_query_kernel(
    fine_hbm,
    coarse_hbm,
    x_hbm,
    query_proj_hbm,
    state_hbm,
    qp_ref,
    state_out_ref,
    fine_ref,
    coarse_ref,
    x_ref,
    query_proj_ref,
    state_ref,
    sems,
):
    rows, width = x_ref.shape
    heads = qp_ref.shape[0]
    chunks = 3
    depth = width // chunks
    loads = [
        pltpu.make_async_copy(x_hbm, x_ref, sems.at[0]),
        pltpu.make_async_copy(fine_hbm.at[pl.ds(0, rows)], fine_ref, sems.at[1]),
        pltpu.make_async_copy(coarse_hbm, coarse_ref, sems.at[2]),
        pltpu.make_async_copy(state_hbm, state_ref, sems.at[3]),
    ]
    loads += [
        pltpu.make_async_copy(
            query_proj_hbm.at[pl.ds(i * depth, depth)],
            query_proj_ref.at[pl.ds(i * depth, depth)],
            sems.at[4 + i],
        )
        for i in range(chunks)
    ]
    for load in loads:
        load.start()
    loads[0].wait()
    normed = norm_rows(x_ref[...].astype(f32)).astype(bf16)
    loads[1].wait()
    loads[2].wait()
    turns = turned_tables(coarse_ref[pl.ds(lax.axis_index("seq"), 1)], fine_ref[...])
    cos, sin = turns[:, :ROPE], turns[:, ROPE:]
    loads[3].wait()
    state_out_ref[...] = state_ref[...].astype(bf16)
    total = None
    for i in range(chunks):
        loads[4 + i].wait()
        lanes = slice(i * depth, (i + 1) * depth)
        term = dot_nn(normed[:, lanes], query_proj_ref[lanes])
        total = term if total is None else total + term
    for head in range(heads):
        at = head * (NOPE + ROPE)
        turned = turn(total[:, at + NOPE : at + NOPE + ROPE], cos, sin)
        qp_ref[head] = (
            jnp.concatenate([total[:, at : at + NOPE], turned], axis=-1) * (scale * log2e)
        ).astype(bf16)


def prefill_queries(fine, coarse, x, query_proj, states):
    rows = x.shape[0]
    heads = query_proj.shape[1] // (NOPE + ROPE)
    vmem = pl.BlockSpec(memory_space=pltpu.VMEM)
    return pl.pallas_call(
        prefill_query_kernel,
        in_specs=[pl.BlockSpec(memory_space=pltpu.HBM)] * 5,
        out_specs=(vmem, vmem),
        out_shape=(
            jax.ShapeDtypeStruct((heads, rows, NOPE + ROPE), bf16),
            jax.ShapeDtypeStruct(states.shape, bf16),
        ),
        scratch_shapes=[
            pltpu.VMEM((rows, fine.shape[1]), f32),
            pltpu.VMEM(coarse.shape, f32),
            pltpu.VMEM(x.shape, bf16),
            pltpu.VMEM(query_proj.shape, bf16),
            pltpu.VMEM(states.shape, f32),
            pltpu.SemaphoreType.DMA((7,)),
        ],
        compiler_params=params(),
    )(fine, coarse, x, query_proj, states)


def pack_shares(summed, sum_ref):
    shares = sum_ref.shape[0]
    rows, width = summed.shape
    share = width // shares
    for g in range(shares):
        part = summed[:, g * share : (g + 1) * share]
        sum_ref[g, :rows] = part[:, :128].astype(bf16)
        sum_ref[g, rows : 2 * rows] = part[:, 128:256].astype(bf16)
        rest = part[:, 256:]
        count = 128 // rest.shape[1]
        piece = rows // count
        sum_ref[g, 2 * rows :] = jnp.concatenate(
            [rest[i * piece : (i + 1) * piece] for i in range(count)], axis=1
        ).astype(bf16)


def flash_kernel(
    heads, q_ref, mine_ref, other_ref, ke_ref, ve_ref, out_hbm, sum_ref,
    peak, acc, vet_ref, out_ref, sem,
):
    step = pl.program_id(0)
    rows = q_ref.shape[1]
    half = rows // 2
    first, core = lax.axis_index("seq") * rows, lax.rem(lax.axis_index("grp"), 2)
    side = mine_ref.shape[0] * half
    block = 2 * side
    load = pltpu.make_async_copy(out_hbm, out_ref, sem)

    @pl.when(step == 0)
    def _():
        load.start()
        vet_ref[...] = ve_ref[...].astype(f32).T.astype(bf16)
        peak[...] = jnp.full_like(peak, masked_score)
        acc[...] = jnp.zeros_like(acc)

    def work(masked):
        sources = [(ref, i) for ref in (mine_ref, other_ref) for i in range(ref.shape[0])]
        low = jnp.concatenate([ref[i, :half] for ref, i in sources], axis=0)
        rope = jnp.concatenate([unpack_rope(ref[i, half:]) for ref, i in sources], axis=0)
        ones = jnp.ones((16, block), bf16)
        keys = dot_nn(low, ke_ref[...]).astype(bf16)
        values = dot_nt(vet_ref[...], low).astype(bf16)
        scores = []
        for head in range(heads):
            whole_keys = jnp.concatenate(
                [keys[:, head * NOPE : (head + 1) * NOPE], rope], axis=-1
            )
            scores.append(dot_nt(whole_keys, q_ref[head]))
        if masked:
            row = lax.broadcasted_iota(jnp.int32, (block, rows), 0)
            from_other = row >= side
            row = jnp.where(from_other, row - side, row)
            which = jnp.where(from_other, 1 - core, core)
            key_pos = step * block + (row // half) * rows + which * half + lax.rem(row, half)
            live = key_pos <= first + lax.broadcasted_iota(jnp.int32, (block, rows), 1)
            scores = [jnp.where(live, s, masked_score) for s in scores]
        for head in range(heads):
            old = peak[head]
            new = jnp.maximum(old, jnp.max(scores[head], axis=0, keepdims=True))
            fade = jnp.exp2(old - new)
            weights = jnp.exp2(scores[head] - new).astype(bf16)
            peak[head] = new
            carried = jnp.concatenate([values[head * VH : (head + 1) * VH], ones], axis=0)
            acc[head] = acc[head] * fade + dot_nn(carried, weights)

    @pl.when((step + 1) * block <= first + 1)
    def _():
        work(False)

    @pl.when(((step + 1) * block > first + 1) & (step * block < first + rows))
    def _():
        work(True)

    @pl.when(step == pl.num_programs(0) - 1)
    def _():
        mixed = jnp.concatenate(
            [(acc[h, :VH] / acc[h, VH : VH + 1]).T for h in range(heads)], axis=-1
        ).astype(bf16)
        load.wait()
        pack_shares(dot_nn(mixed, out_ref[...]), sum_ref)


def prefill_attend(q, mine, other, key_expand, value_expand, mla_output, shares):
    heads, rows, _ = q.shape
    sources, packed, _ = mine.shape
    side = max(1, min(sources, 1024 // rows))
    width = mla_output.shape[1]
    dense = rows * width // shares // 128
    whole = lambda shape: pl.BlockSpec(shape, lambda i: (0,) * len(shape))
    return pl.pallas_call(
        functools.partial(flash_kernel, heads),
        grid=(sources // side,),
        in_specs=[
            whole(q.shape),
            pl.BlockSpec((side, packed, LAT), lambda i: (i, 0, 0)),
            pl.BlockSpec((side, packed, LAT), lambda i: (i, 0, 0)),
            whole(key_expand.shape),
            whole(value_expand.shape),
            pl.BlockSpec(memory_space=pltpu.HBM),
        ],
        out_specs=whole((shares, dense, 128)),
        scratch_shapes=[
            pltpu.VMEM((heads, 1, rows), f32),
            pltpu.VMEM((heads, VH + 16, rows), f32),
            pltpu.VMEM((value_expand.shape[1], value_expand.shape[0]), bf16),
            pltpu.VMEM(mla_output.shape, bf16),
            pltpu.SemaphoreType.DMA,
        ],
        out_shape=jax.ShapeDtypeStruct((shares, dense, 128), bf16),
        compiler_params=params(),
    )(q, mine, other, key_expand, value_expand, mla_output)


def gather_share_kernel(parts_ref, x_ref, *refs):
    sides, (out_ref, decode_ref) = refs[:-2], refs[-2:]
    decode_ref[...] = sum(side[...].astype(f32) for side in sides).astype(bf16)
    rows, share = x_ref.shape
    x = x_ref[...].astype(f32)
    total = jnp.sum(parts_ref[...].astype(f32), axis=0)
    left = total[:rows] + x[:, :128]
    right = total[rows : 2 * rows] + x[:, 128:256]
    rest = total[2 * rows :]
    wide = share - 256
    rest = jnp.concatenate(
        [rest[:, i * wide : (i + 1) * wide] for i in range(128 // wide)], axis=0
    )
    rest = rest + x[:, 256:]
    out_ref[...] = jnp.concatenate([left.T, right.T, rest.T], axis=0).astype(bf16)


def gather_share(parts, x, *sides):
    rows, share = x.shape
    return pl.pallas_call(
        gather_share_kernel,
        out_shape=(
            jax.ShapeDtypeStruct((share, rows), bf16),
            jax.ShapeDtypeStruct(sides[0].shape, bf16),
        ),
        compiler_params=params(20),
    )(parts, x, *sides)


def split_level(level, rows):
    lane = lax.broadcasted_iota(jnp.int32, (rows, SENT - LAT), 1)
    high = level.astype(bf16).astype(f32)
    middle = (level - high).astype(bf16).astype(f32)
    low = level - high - middle
    return jnp.where(
        lane == 0, high, jnp.where(lane == 1, middle, jnp.where(lane == 2, low, 0.0))
    )


def join_level(part):
    tail = part[:, LAT:].astype(f32)
    lane = lax.broadcasted_iota(jnp.int32, tail.shape, 1)
    return jnp.sum(jnp.where(lane < 3, tail, 0.0), axis=-1, keepdims=True)


def merge_parts(parts):
    levels = [join_level(p) for p in parts]
    highest = functools.reduce(jnp.maximum, levels)
    weights = [jnp.exp2(v - highest) for v in levels]
    total = sum(weights)
    mixed = sum(p[:, :LAT].astype(f32) * w for p, w in zip(parts, weights)) / total
    return mixed, highest + jnp.log2(total)


def pages_kernel(group, requests, count, *refs):
    q_refs = refs[: 2 * count]
    keys_ref, fresh_ref, owner_ref, keep_ref, send_ref = refs[2 * count :]
    each = q_refs[0].shape[0]
    block = 2 * each
    keys = keys_ref[...]
    fresh = fresh_ref[...]
    within = lax.rem(lax.broadcasted_iota(jnp.int32, (block, 1), 0), group)
    request = lax.rem(within, requests)
    step = within // requests
    live_old = owner_ref[...] == request
    column = lax.broadcasted_iota(jnp.int32, (1, fresh.shape[0]), 1)
    fresh_step = column // requests + lax.axis_index("grp") * group
    live_new = (lax.rem(column, requests) == request) & (fresh_step <= step)
    scores = []
    for i in range(0, 2 * count, 2):
        q = jnp.concatenate([q_refs[i][:, :WIDE], q_refs[i + 1][:, :WIDE]], axis=0)
        scores.append(
            (
                jnp.where(live_old, dot_nt(q, keys), masked_score),
                jnp.where(live_new, dot_nt(q, fresh), masked_score),
            )
        )
    for i, (old, new) in enumerate(scores):
        highest = jnp.maximum(
            jnp.max(old, axis=-1, keepdims=True), jnp.max(new, axis=-1, keepdims=True)
        )
        highest = jnp.maximum(highest, 0.1 * masked_score)
        w_old = jnp.exp2(old - highest)
        w_new = jnp.exp2(new - highest)
        total = jnp.sum(w_old, axis=-1, keepdims=True) + jnp.sum(w_new, axis=-1, keepdims=True)
        some = total > 0.0
        safe = jnp.where(some, total, 1.0)
        mixed = dot_nn(w_old.astype(bf16), keys[:, :LAT]) + dot_nn(
            w_new.astype(bf16), fresh[:, :LAT]
        )
        level = jnp.where(some, highest + jnp.log2(safe), masked_score)
        out_ref = keep_ref if 2 * i < count else send_ref
        both = jnp.concatenate([mixed / safe, split_level(level, block)], axis=-1).astype(bf16)
        out_ref[2 * i % count] = both[:each]
        out_ref[2 * i % count + 1] = both[each:]


def pages_attend(queries, keys, fresh, owner, group, requests):
    count = len(queries) // 2
    vmem = pl.BlockSpec(memory_space=pltpu.VMEM)
    shape = jax.ShapeDtypeStruct((count, queries[0].shape[0], SENT), bf16)
    return pl.pallas_call(
        functools.partial(pages_kernel, group, requests, count),
        in_specs=[vmem] * (2 * count + 3),
        out_specs=(vmem, vmem),
        out_shape=(shape, shape),
        compiler_params=params(24),
    )(*queries, keys, fresh, owner)


def merge_kernel(keep_ref, got_ref, *out_refs):
    for i, out_ref in enumerate(out_refs):
        mixed, level = merge_parts([keep_ref[i], got_ref[i]])
        out_ref[...] = jnp.concatenate(
            [mixed, split_level(level, mixed.shape[0])], axis=-1
        ).astype(bf16)


def merge_pair(keep, got):
    shape = jax.ShapeDtypeStruct(keep.shape[1:], bf16)
    return pl.pallas_call(
        merge_kernel,
        out_shape=(shape,) * keep.shape[0],
        compiler_params=params(24),
    )(keep, got)


def combine_kernel(heads, count, *refs):
    ve_ref, out_ref, sum_ref = refs[count:]
    mixed, _ = merge_parts([ref[...] for ref in refs[:count]])
    each = mixed.shape[0] // heads
    head_values = [
        dot_nn(mixed[h * each : (h + 1) * each].astype(bf16), ve_ref[:, h * VH : (h + 1) * VH])
        for h in range(heads)
    ]
    joined = jnp.concatenate(head_values, axis=-1).astype(bf16)
    sum_ref[...] = dot_nn(joined, out_ref[...]).astype(bf16)


def combine(parts, value_expand, mla_output):
    heads = value_expand.shape[1] // VH
    return pl.pallas_call(
        functools.partial(combine_kernel, heads, len(parts)),
        out_shape=jax.ShapeDtypeStruct((parts[0].shape[0] // heads, mla_output.shape[1]), bf16),
        compiler_params=params(20),
    )(*parts, value_expand, mla_output)


def kda_kernel(
    heads,
    requests,
    rate_ref,
    one_hbm,
    two_hbm,
    dec_hbm,
    inputs_hbm,
    beta_hbm,
    decay_down_hbm,
    gate_down_hbm,
    decay_up_hbm,
    gate_up_hbm,
    states_hbm,
    output_hbm,
    hidden_ref,
    keep_ref,
    send_ref,
    one_ref,
    two_ref,
    dec_ref,
    inputs_ref,
    beta_ref,
    decay_down_ref,
    gate_down_ref,
    decay_up_ref,
    gate_up_ref,
    states_ref,
    output_ref,
    by_share,
    summed_ref,
    sems,
):
    shares, rows, share = by_share.shape
    grp = lax.axis_index("grp")
    pairs = [
        (one_hbm, one_ref),
        (two_hbm, two_ref),
        (dec_hbm, dec_ref),
        (inputs_hbm.at[1], inputs_ref.at[1]),
        (beta_hbm, beta_ref),
        (decay_down_hbm, decay_down_ref),
        (gate_down_hbm, gate_down_ref),
        (decay_up_hbm, decay_up_ref),
        (gate_up_hbm, gate_up_ref),
        (inputs_hbm.at[0], inputs_ref.at[0]),
        (states_hbm, states_ref),
        (inputs_hbm.at[2], inputs_ref.at[2]),
        (output_hbm, output_ref),
    ]
    loads = [pltpu.make_async_copy(a, b, sems.at[i]) for i, (a, b) in enumerate(pairs)]
    for load in loads:
        load.start()
    for load in loads[:3]:
        load.wait()
    hidden = dec_ref[...].astype(f32) + (
        one_ref[...].astype(f32) + two_ref[...].astype(f32)
    )
    for g in range(shares):
        by_share[g] = hidden[:, g * share : (g + 1) * share]
    hidden_ref[...] = by_share[grp]
    kin = norm_rows(hidden).astype(bf16)
    loads[3].wait()
    all_keys = dot_nn(kin, inputs_ref[1])
    for load in loads[4:9]:
        load.wait()
    beta = jax.nn.sigmoid(dot_nt(kin, beta_ref[...]))
    decay_low = dot_nn(kin, decay_down_ref[...]).astype(bf16)
    rises = jax.nn.softplus(dot_nn(decay_low, decay_up_ref[...]))
    gate_low = dot_nn(kin, gate_down_ref[...]).astype(bf16)
    gates = jax.nn.sigmoid(dot_nn(gate_low, gate_up_ref[...]))
    loads[9].wait()
    all_queries = dot_nn(kin, inputs_ref[0])
    loads[10].wait()
    held_states = [states_ref[:, r].astype(f32) for r in range(requests)]
    steps = rows // requests
    piece = held_states[0].shape[1] // heads
    at = lambda values, t: values[t * requests : (t + 1) * requests]
    along = lambda a, b: jnp.sum(a * b, axis=-1, keepdims=True)
    ready = []
    for head in range(heads):
        lanes = slice(head * DK, (head + 1) * DK)
        q = unit_rows(all_queries[:, lanes]) * DK ** (-0.5)
        k = unit_rows(all_keys[:, lanes])
        rate = jnp.exp(jnp.full((1, DK), rate_ref[head], f32))
        a = jnp.exp(-rate * rises[:, lanes])
        vectors = []
        kept = None
        for t in range(steps):
            kept = at(a, t) if kept is None else kept * at(a, t)
            vectors += [kept * at(k, t), kept * at(q, t)]
        vectors = jnp.concatenate(vectors, axis=0)
        high = vectors.astype(bf16).astype(f32)
        both = jnp.concatenate([high, vectors - high], axis=0)
        owner = lax.rem(lax.broadcasted_iota(jnp.int32, (both.shape[0], 1), 0), requests)
        spread = jnp.concatenate(
            [jnp.where(owner == r, both, 0.0) for r in range(requests)], axis=-1
        ).astype(bf16)
        facing = jnp.concatenate(
            [
                held_states[r][:, head * piece : (head + 1) * piece].reshape(DV, DK)
                for r in range(requests)
            ],
            axis=-1,
        ).astype(bf16)
        met = dot_nt(spread, facing)
        ready.append((q, k, a, met[: vectors.shape[0]] + met[vectors.shape[0] :]))
    loads[11].wait()
    all_values = dot_nn(kin, inputs_ref[2])
    blended = []
    for head in range(heads):
        lanes = slice(head * DK, (head + 1) * DK)
        q, k, a, met = ready[head]
        v = all_values[:, lanes]
        b = beta[:, head : head + 1]
        carried = []
        reads = []
        for t in range(steps):
            seen = at(met, 2 * t)
            read = at(met, 2 * t + 1)
            carried = [(u, w * at(a, t)) for u, w in carried]
            for u, w in carried:
                seen = seen + u * along(w, at(k, t))
            u = at(b, t) * (at(v, t) - seen)
            carried.append((u, at(k, t)))
            for u, w in carried:
                read = read + u * along(w, at(q, t))
            reads.append(read)
        read = jnp.concatenate(reads, axis=0)
        blended.append(norm_rows(read) * gates[:, lanes])
    mixed = jnp.concatenate(blended, axis=-1).astype(bf16)
    loads[12].wait()
    summed = dot_nn(mixed, output_ref[...])
    for g in range(shares):
        summed_ref[g] = summed[:, g * share : (g + 1) * share]
    core = lax.rem(grp, 2)
    for by in range(shares // 2):
        pair = 2 * lax.rem(grp // 2 + by, shares // 2)
        keep_ref[by] = summed_ref[pair + core]
        send_ref[by] = summed_ref[pair + 1 - core].astype(bf16)


def kda(shares, rate, *operands):
    dec, beta_t, states = operands[2], operands[4], operands[9]
    rows, width = dec.shape
    heads = beta_t.shape[0]
    requests = states.shape[1]
    share = width // shares
    sides = shares // 2
    vmem = pl.BlockSpec(memory_space=pltpu.VMEM)
    return pl.pallas_call(
        functools.partial(kda_kernel, heads, requests),
        in_specs=[pl.BlockSpec(memory_space=pltpu.SMEM)]
        + [pl.BlockSpec(memory_space=pltpu.HBM)] * len(operands),
        out_specs=(vmem, vmem, vmem),
        out_shape=(
            jax.ShapeDtypeStruct((rows, share), f32),
            jax.ShapeDtypeStruct((sides, rows, share), f32),
            jax.ShapeDtypeStruct((sides, rows, share), bf16),
        ),
        scratch_shapes=[pltpu.VMEM(a.shape, a.dtype) for a in operands]
        + [
            pltpu.VMEM((shares, rows, share), f32),
            pltpu.VMEM((shares, rows, share), f32),
            pltpu.SemaphoreType.DMA((len(operands) + 2,)),
        ],
        compiler_params=params(),
    )(rate, *operands)


def shards(
    x_group,
    decode_input,
    prompt_len,
    latent_pages,
    slot_target,
    page_counts,
    kda_state,
    query_proj,
    latent_proj,
    key_expand,
    value_expand,
    mla_output,
    kda_inputs,
    kda_beta,
    decay_down,
    decay_up,
    gate_down,
    gate_up,
    decay_log,
    kda_output,
):
    seq_index = lax.axis_index("seq")
    grp_index = lax.axis_index("grp")
    seq_size = lax.axis_size("seq")
    grp_size = lax.axis_size("grp")
    rows, width = x_group.shape
    steps, requests, _ = decode_input.shape
    decode_rows = steps * requests
    share = width // grp_size
    dec = decode_input.reshape(decode_rows, width)

    own_tokens = slice_pages(latent_pages[0], grp_size)
    _, slots, tokens, _ = own_tokens.shape
    core = grp_index % 2
    target = lax.dynamic_slice_in_dim(slot_target[:, 0, :], core * slots, slots, 1)
    owner = target // MAXP
    lengths = jnp.sum(
        jnp.where(owner[..., None] == jnp.arange(requests), prompt_len, 0), axis=-1
    )
    held = core * slots + jnp.arange(slots)[None, :] < page_counts
    token_pos = (
        ((target % MAXP) * PAGE + (grp_index // 2) * tokens)[..., None] + jnp.arange(tokens)
    )
    key_owner = jnp.where(
        held[..., None] & (token_pos < lengths[..., None]), owner[..., None], -1
    ).reshape(1, -1)

    x_rows, _ = lax.optimization_barrier((x_group, own_tokens))
    reach = max(rows, MAXP * PAGE + steps)
    fine = rope_tables(range(-(-reach // 8) * 8))
    coarse = rope_tables([rows * i for i in range(seq_size)])
    own_latent, fresh, q_decode = front(
        prompt_len, fine, coarse, x_rows, dec, latent_proj.T, query_proj, key_expand
    )
    sides = grp_size // 2

    def shift(value, by):
        return lax.ppermute(
            value, "grp", [(g, (g + 2 * by) % grp_size) for g in range(grp_size)]
        )

    def swap(value):
        return lax.ppermute(value, "grp", [(g, g ^ 1) for g in range(grp_size)])

    arrived = lax.all_to_all(own_tokens, "seq", split_axis=0, concat_axis=0, tiled=True)
    queries = [q_decode] + [shift(q_decode, by) for by in range(1, sides)]
    own_latent, _, _, key_owner = lax.optimization_barrier(
        (own_latent, arrived, queries[1], key_owner)
    )
    mine = lax.all_to_all(own_latent, "seq", split_axis=0, concat_axis=0, tiled=True)
    page_keys = arrived.reshape(-1, WIDE)
    queries = queries + [swap(q) for q in queries]
    keep, send = pages_attend(
        queries, page_keys, fresh, key_owner, decode_rows, requests
    )
    merged = merge_pair(keep, swap(send))
    x_again, _ = lax.optimization_barrier((x_group, merged[1]))
    q_prefill, state_rows = prefill_queries(
        fine, coarse, x_again, query_proj, kda_state.reshape(kda_state.shape[0], -1, DK)
    )
    partial = [merged[0]] + [shift(merged[by], -by) for by in range(1, sides)]
    partial[0], _ = lax.optimization_barrier((partial[0], q_prefill))
    mla_part = combine(partial, value_expand, mla_output)
    add = lambda one, two: one.astype(f32) + two.astype(f32)
    trade = lambda value, bits: lax.ppermute(
        value, "grp", [(g, g ^ bits) for g in range(grp_size)]
    )
    mla_pair = add(mla_part, swap(mla_part)).astype(bf16)
    mla_near = trade(mla_pair, 2)
    mine, _ = lax.optimization_barrier((mine, mla_pair))
    state_rows, _ = lax.optimization_barrier((state_rows, mine))
    states = lax.all_to_all(
        state_rows, "seq", split_axis=0, concat_axis=0, tiled=True
    ).reshape((seq_size, requests) + state_rows.shape[1:])
    mla_half = add(mla_pair, mla_near).astype(bf16)
    mla_rest = trade(mla_half, 6)

    prefill_part = prefill_attend(
        q_prefill, mine, swap(mine), key_expand, value_expand, mla_output, grp_size
    )
    mla_half, mla_rest, prefill_part = lax.optimization_barrier(
        (mla_half, mla_rest, prefill_part)
    )
    prefill_parts = lax.all_to_all(
        prefill_part, "grp", split_axis=0, concat_axis=0, tiled=True
    )
    own_columns = lax.dynamic_slice_in_dim(x_group, grp_index * share, share, 1)

    hidden_share, keep, send = kda(
        grp_size,
        decay_log,
        mla_half,
        mla_rest,
        dec,
        kda_inputs.transpose(1, 0, 2),
        kda_beta.T,
        decay_down,
        gate_down,
        decay_up,
        gate_up,
        states,
        kda_output,
    )
    crossing = swap(send)
    kda_sides = [keep[by] + crossing[by].astype(f32) for by in range(sides)]
    kda_sides[0] = kda_sides[0] + hidden_share
    for by in range(1, sides):
        kda_sides[by] = shift(kda_sides[by].astype(bf16), by)
    prefill_out, decode_out = gather_share(prefill_parts, own_columns, *kda_sides)
    return (prefill_out.T, decode_out.reshape(steps, requests, share))


def solution(mesh):
    in_specs = (
        P("seq", None),
        P(None, "seq", None),
        P("seq"),
        P("seq", None, None, None, None),
        P(None, "seq", None),
        P(None, "seq"),
        P(None, "grp", "seq", None),
        P(None, "grp"),
        P(),
        P(None, "grp"),
        P(None, "grp"),
        P("grp", None),
        P(None, None, "grp"),
        P(None, "grp"),
        P(),
        P(None, "grp"),
        P(),
        P(None, "grp"),
        P("grp"),
        P("grp", None),
    )
    out_specs = (P("seq", "grp"), P(None, "seq", "grp"))
    return jax.shard_map(shards, mesh=mesh, in_specs=in_specs, out_specs=out_specs, check_vma=False)
```

```python
import functools

import jax
import jax.numpy as jnp
import numpy as np
from jax import lax
from jax.experimental import pallas as pl
from jax.experimental.pallas import tpu as pltpu
from jax.sharding import PartitionSpec as P

LAT = 512
ROPE = 64
NOPE = 128
VH = 128
DK = 128
DV = 128
PAGE = 64
MAXP = 12
WIDE = LAT + ROPE
SENT = LAT + 128

epsilon = 1e-06
masked_score = -1e30
scale = (NOPE + ROPE) ** (-0.5)
log2e = 1.4426950408889634

f32 = jnp.float32
bf16 = jnp.bfloat16
MIB = 1024 * 1024


def params(mib=58):
    return pltpu.CompilerParams(vmem_limit_bytes=mib * MIB)


def dot_nt(a, b):
    return lax.dot_general(a, b, (((1,), (1,)), ((), ())), preferred_element_type=f32)


def dot_nn(a, b):
    return lax.dot_general(a, b, (((1,), (0,)), ((), ())), preferred_element_type=f32)


def norm_rows(values):
    return values * lax.rsqrt(jnp.mean(values * values, axis=-1, keepdims=True) + epsilon)


def unit_rows(values):
    return values * lax.rsqrt(jnp.sum(values * values, axis=-1, keepdims=True) + epsilon)


def turn(values, cos, sin):
    half = ROPE // 2
    swapped = jnp.concatenate([values[:, half:], values[:, :half]], axis=-1)
    return values * cos + swapped * sin


def rope_tables(positions):
    half = ROPE // 2
    frequency = np.exp(-np.log(10000.0) * np.arange(half) / half)
    angles = np.asarray(positions, np.float64)[:, None] * frequency
    cos, sin = np.cos(angles), np.sin(angles)
    both = np.concatenate([cos, cos, -sin, sin], -1)
    return jnp.asarray(both, f32)


def slice_kernel(pages_hbm, own_hbm, held, in_sems, out_sems):
    grp = lax.axis_index("grp")
    owners, slots, tokens, _ = own_hbm.shape
    parts = in_sems.shape[0]
    each = owners // parts
    first = lax.rem(grp, 2) * slots
    row = pl.multiple_of((grp // 2) * tokens, tokens)
    loads = [
        pltpu.make_async_copy(
            pages_hbm.at[pl.ds(i * each, each), pl.ds(first, slots), pl.ds(row, tokens), :],
            held.at[pl.ds(i * each, each)],
            in_sems.at[i],
        )
        for i in range(parts)
    ]
    stores = [
        pltpu.make_async_copy(
            held.at[pl.ds(i * each, each)], own_hbm.at[pl.ds(i * each, each)], out_sems.at[i]
        )
        for i in range(parts)
    ]
    for load in loads:
        load.start()
    for load, store in zip(loads, stores):
        load.wait()
        store.start()
    for store in stores:
        store.wait()


def slice_pages(pages, grp_size):
    owners, cap, page, wide = pages.shape
    shape = (owners, cap // 2, page // (grp_size // 2), wide)
    parts = 4
    hbm = pl.BlockSpec(memory_space=pltpu.HBM)
    return pl.pallas_call(
        slice_kernel,
        in_specs=[hbm],
        out_specs=hbm,
        out_shape=jax.ShapeDtypeStruct(shape, bf16),
        scratch_shapes=[
            pltpu.VMEM(shape, bf16),
            pltpu.SemaphoreType.DMA((parts,)),
            pltpu.SemaphoreType.DMA((parts,)),
        ],
        compiler_params=params(),
    )(pages)


def pack_rope(values):
    count = LAT // ROPE
    piece = values.shape[0] // count
    return jnp.concatenate(
        [values[i * piece : (i + 1) * piece] for i in range(count)], axis=1
    )


def unpack_rope(packed):
    return jnp.concatenate(
        [packed[:, i * ROPE : (i + 1) * ROPE] for i in range(LAT // ROPE)], axis=0
    )


def turned_tables(base, near):
    base_cos, base_sin = base[:, :ROPE], base[:, ROPE:]
    near_cos, near_sin = near[:, :ROPE], near[:, ROPE:]
    return jnp.concatenate(
        [base_cos * near_cos - base_sin * near_sin, base_sin * near_cos + base_cos * near_sin],
        axis=-1,
    )


def front_kernel(
    count,
    lengths_ref,
    fine_hbm,
    coarse_hbm,
    x_hbm,
    dec_hbm,
    lat_proj_hbm,
    query_proj_hbm,
    expand_hbm,
    lat_hbm,
    fresh_ref,
    qd_ref,
    fine_ref,
    coarse_ref,
    x_ref,
    dec_ref,
    lat_proj_ref,
    query_proj_ref,
    expand_ref,
    normed,
    turns,
    lat_ref,
    sems,
    out_sems,
):
    seq, grp = lax.axis_index("seq"), lax.axis_index("grp")
    rows, width = x_ref.shape
    core = lax.rem(grp, 2)
    heads = expand_ref.shape[1] // NOPE
    requests = lengths_ref.shape[0]
    chunks = 3
    depth = width // chunks
    own = pl.ds(pl.multiple_of(core * rows, rows), rows)
    first = [
        pltpu.make_async_copy(x_hbm.at[own], x_ref, sems.at[0]),
        pltpu.make_async_copy(dec_hbm, dec_ref, sems.at[1]),
        pltpu.make_async_copy(lat_proj_hbm, lat_proj_ref, sems.at[2]),
        pltpu.make_async_copy(fine_hbm, fine_ref, sems.at[3]),
        pltpu.make_async_copy(coarse_hbm, coarse_ref, sems.at[4]),
    ]
    later = [
        pltpu.make_async_copy(
            query_proj_hbm.at[pl.ds(i * depth, depth)],
            query_proj_ref.at[pl.ds(i * depth, depth)],
            sems.at[5 + i],
        )
        for i in range(chunks)
    ]
    later.append(pltpu.make_async_copy(expand_hbm, expand_ref, sems.at[5 + chunks]))
    for load in first + later:
        load.start()
    first[0].wait()
    normed[:rows] = norm_rows(x_ref[...].astype(f32)).astype(bf16)
    first[1].wait()
    tail = normed.shape[0] - rows - count
    normed[rows:] = jnp.concatenate(
        [norm_rows(dec_ref[...].astype(f32)), jnp.zeros((tail, width), f32)], axis=0
    ).astype(bf16)
    first[3].wait()
    first[4].wait()
    for r in range(requests):
        for t in range(count // requests):
            at = rows + t * requests + r
            turns[at : at + 1] = fine_ref[pl.ds(lengths_ref[r] + t, 1)]
    turns[rows + count :] = jnp.zeros((tail, 2 * ROPE), f32)
    turns[:rows] = turned_tables(coarse_ref[pl.ds(seq, 1)], fine_ref[own])
    first[2].wait()
    projected = dot_nt(normed[...], lat_proj_ref[...])
    cos, sin = turns[:, :ROPE], turns[:, ROPE:]
    latent = jnp.concatenate(
        [norm_rows(projected[:, :LAT]), turn(projected[:, LAT:], cos, sin)], axis=-1
    )
    lat_ref[:rows] = latent[:rows, :LAT].astype(bf16)
    lat_ref[rows:] = pack_rope(latent[:rows, LAT:]).astype(bf16)
    stores = [
        pltpu.make_async_copy(lat_ref, lat_hbm.at[i], out_sems.at[i])
        for i in range(lat_hbm.shape[0])
    ]
    for store in stores:
        store.start()
    fresh_ref[...] = latent[rows:].astype(bf16)
    total = None
    for i in range(chunks):
        later[i].wait()
        lanes = slice(i * depth, (i + 1) * depth)
        term = dot_nn(normed[rows:, lanes], query_proj_ref[lanes])
        total = term if total is None else total + term
    later[chunks].wait()
    decode = []
    for head in range(heads):
        at = head * (NOPE + ROPE)
        turned = turn(total[:, at + NOPE : at + NOPE + ROPE], cos[rows:], sin[rows:])
        absorbed = dot_nt(
            total[:, at : at + NOPE].astype(bf16),
            expand_ref[:, head * NOPE : (head + 1) * NOPE],
        )
        blank = jnp.zeros((absorbed.shape[0], SENT - WIDE), f32)
        decode.append(jnp.concatenate([absorbed, turned, blank], axis=-1)[:count])
    qd_ref[...] = (jnp.concatenate(decode, axis=0) * (scale * log2e)).astype(bf16)
    for store in stores:
        store.wait()


def front(lengths, fine, coarse, x, dec, lat_proj_t, query_proj, key_expand):
    rows, width = x.shape
    half = rows // 2
    count = dec.shape[0]
    heads = key_expand.shape[1] // NOPE
    padded = count + 8
    packed = half + half * ROPE // LAT
    seq_size = coarse.shape[0]
    smem = pl.BlockSpec(memory_space=pltpu.SMEM)
    vmem = pl.BlockSpec(memory_space=pltpu.VMEM)
    hbm = pl.BlockSpec(memory_space=pltpu.HBM)
    return pl.pallas_call(
        functools.partial(front_kernel, count),
        in_specs=[smem] + [hbm] * 7,
        out_specs=(hbm, vmem, vmem),
        out_shape=(
            jax.ShapeDtypeStruct((seq_size, packed, LAT), bf16),
            jax.ShapeDtypeStruct((padded, WIDE), bf16),
            jax.ShapeDtypeStruct((heads * count, SENT), bf16),
        ),
        scratch_shapes=[
            pltpu.VMEM(fine.shape, f32),
            pltpu.VMEM(coarse.shape, f32),
            pltpu.VMEM((half, width), bf16),
            pltpu.VMEM(dec.shape, bf16),
            pltpu.VMEM(lat_proj_t.shape, bf16),
            pltpu.VMEM(query_proj.shape, bf16),
            pltpu.VMEM(key_expand.shape, bf16),
            pltpu.VMEM((half + padded, width), bf16),
            pltpu.VMEM((half + padded, 2 * ROPE), f32),
            pltpu.VMEM((packed, LAT), bf16),
            pltpu.SemaphoreType.DMA((9,)),
            pltpu.SemaphoreType.DMA((seq_size,)),
        ],
        compiler_params=params(),
    )(lengths, fine, coarse, x, dec, lat_proj_t, query_proj, key_expand)


def prefill_query_kernel(
    fine_hbm,
    coarse_hbm,
    x_hbm,
    query_proj_hbm,
    state_hbm,
    qp_ref,
    state_out_ref,
    fine_ref,
    coarse_ref,
    x_ref,
    query_proj_ref,
    state_ref,
    sems,
):
    rows, width = x_ref.shape
    heads = qp_ref.shape[0]
    chunks = 3
    depth = width // chunks
    loads = [
        pltpu.make_async_copy(x_hbm, x_ref, sems.at[0]),
        pltpu.make_async_copy(fine_hbm.at[pl.ds(0, rows)], fine_ref, sems.at[1]),
        pltpu.make_async_copy(coarse_hbm, coarse_ref, sems.at[2]),
        pltpu.make_async_copy(state_hbm, state_ref, sems.at[3]),
    ]
    loads += [
        pltpu.make_async_copy(
            query_proj_hbm.at[pl.ds(i * depth, depth)],
            query_proj_ref.at[pl.ds(i * depth, depth)],
            sems.at[4 + i],
        )
        for i in range(chunks)
    ]
    for load in loads:
        load.start()
    loads[0].wait()
    normed = norm_rows(x_ref[...].astype(f32)).astype(bf16)
    loads[1].wait()
    loads[2].wait()
    turns = turned_tables(coarse_ref[pl.ds(lax.axis_index("seq"), 1)], fine_ref[...])
    cos, sin = turns[:, :ROPE], turns[:, ROPE:]
    loads[3].wait()
    state_out_ref[...] = state_ref[...].astype(bf16)
    total = None
    for i in range(chunks):
        loads[4 + i].wait()
        lanes = slice(i * depth, (i + 1) * depth)
        term = dot_nn(normed[:, lanes], query_proj_ref[lanes])
        total = term if total is None else total + term
    for head in range(heads):
        at = head * (NOPE + ROPE)
        turned = turn(total[:, at + NOPE : at + NOPE + ROPE], cos, sin)
        qp_ref[head] = (
            jnp.concatenate([total[:, at : at + NOPE], turned], axis=-1) * (scale * log2e)
        ).astype(bf16)


def prefill_queries(fine, coarse, x, query_proj, states):
    rows = x.shape[0]
    heads = query_proj.shape[1] // (NOPE + ROPE)
    vmem = pl.BlockSpec(memory_space=pltpu.VMEM)
    return pl.pallas_call(
        prefill_query_kernel,
        in_specs=[pl.BlockSpec(memory_space=pltpu.HBM)] * 5,
        out_specs=(vmem, vmem),
        out_shape=(
            jax.ShapeDtypeStruct((heads, rows, NOPE + ROPE), bf16),
            jax.ShapeDtypeStruct(states.shape, bf16),
        ),
        scratch_shapes=[
            pltpu.VMEM((rows, fine.shape[1]), f32),
            pltpu.VMEM(coarse.shape, f32),
            pltpu.VMEM(x.shape, bf16),
            pltpu.VMEM(query_proj.shape, bf16),
            pltpu.VMEM(states.shape, f32),
            pltpu.SemaphoreType.DMA((7,)),
        ],
        compiler_params=params(),
    )(fine, coarse, x, query_proj, states)


def pack_shares(summed, sum_ref):
    shares = sum_ref.shape[0]
    rows, width = summed.shape
    share = width // shares
    for g in range(shares):
        part = summed[:, g * share : (g + 1) * share]
        sum_ref[g, :rows] = part[:, :128].astype(bf16)
        sum_ref[g, rows : 2 * rows] = part[:, 128:256].astype(bf16)
        rest = part[:, 256:]
        count = 128 // rest.shape[1]
        piece = rows // count
        sum_ref[g, 2 * rows :] = jnp.concatenate(
            [rest[i * piece : (i + 1) * piece] for i in range(count)], axis=1
        ).astype(bf16)


def flash_kernel(
    heads, q_ref, mine_ref, other_ref, ke_ref, ve_ref, out_hbm, sum_ref,
    peak, acc, vet_ref, out_ref, sem,
):
    step = pl.program_id(0)
    rows = q_ref.shape[1]
    half = rows // 2
    first, core = lax.axis_index("seq") * rows, lax.rem(lax.axis_index("grp"), 2)
    side = mine_ref.shape[0] * half
    block = 2 * side
    load = pltpu.make_async_copy(out_hbm, out_ref, sem)

    @pl.when(step == 0)
    def _():
        load.start()
        vet_ref[...] = ve_ref[...].astype(f32).T.astype(bf16)
        peak[...] = jnp.full_like(peak, masked_score)
        acc[...] = jnp.zeros_like(acc)

    def work(masked):
        sources = [(ref, i) for ref in (mine_ref, other_ref) for i in range(ref.shape[0])]
        low = jnp.concatenate([ref[i, :half] for ref, i in sources], axis=0)
        rope = jnp.concatenate([unpack_rope(ref[i, half:]) for ref, i in sources], axis=0)
        ones = jnp.ones((16, block), bf16)
        keys = dot_nn(low, ke_ref[...]).astype(bf16)
        values = dot_nt(vet_ref[...], low).astype(bf16)
        scores = []
        for head in range(heads):
            whole_keys = jnp.concatenate(
                [keys[:, head * NOPE : (head + 1) * NOPE], rope], axis=-1
            )
            scores.append(dot_nt(whole_keys, q_ref[head]))
        if masked:
            row = lax.broadcasted_iota(jnp.int32, (block, rows), 0)
            from_other = row >= side
            row = jnp.where(from_other, row - side, row)
            which = jnp.where(from_other, 1 - core, core)
            key_pos = step * block + (row // half) * rows + which * half + lax.rem(row, half)
            live = key_pos <= first + lax.broadcasted_iota(jnp.int32, (block, rows), 1)
            scores = [jnp.where(live, s, masked_score) for s in scores]
        for head in range(heads):
            old = peak[head]
            new = jnp.maximum(old, jnp.max(scores[head], axis=0, keepdims=True))
            fade = jnp.exp2(old - new)
            weights = jnp.exp2(scores[head] - new).astype(bf16)
            peak[head] = new
            carried = jnp.concatenate([values[head * VH : (head + 1) * VH], ones], axis=0)
            acc[head] = acc[head] * fade + dot_nn(carried, weights)

    @pl.when((step + 1) * block <= first + 1)
    def _():
        work(False)

    @pl.when(((step + 1) * block > first + 1) & (step * block < first + rows))
    def _():
        work(True)

    @pl.when(step == pl.num_programs(0) - 1)
    def _():
        mixed = jnp.concatenate(
            [(acc[h, :VH] / acc[h, VH : VH + 1]).T for h in range(heads)], axis=-1
        ).astype(bf16)
        load.wait()
        pack_shares(dot_nn(mixed, out_ref[...]), sum_ref)


def prefill_attend(q, mine, other, key_expand, value_expand, mla_output, shares):
    heads, rows, _ = q.shape
    sources, packed, _ = mine.shape
    side = max(1, min(sources, 2048 // rows))
    width = mla_output.shape[1]
    dense = rows * width // shares // 128
    whole = lambda shape: pl.BlockSpec(shape, lambda i: (0,) * len(shape))
    return pl.pallas_call(
        functools.partial(flash_kernel, heads),
        grid=(sources // side,),
        in_specs=[
            whole(q.shape),
            pl.BlockSpec((side, packed, LAT), lambda i: (i, 0, 0)),
            pl.BlockSpec((side, packed, LAT), lambda i: (i, 0, 0)),
            whole(key_expand.shape),
            whole(value_expand.shape),
            pl.BlockSpec(memory_space=pltpu.HBM),
        ],
        out_specs=whole((shares, dense, 128)),
        scratch_shapes=[
            pltpu.VMEM((heads, 1, rows), f32),
            pltpu.VMEM((heads, VH + 16, rows), f32),
            pltpu.VMEM((value_expand.shape[1], value_expand.shape[0]), bf16),
            pltpu.VMEM(mla_output.shape, bf16),
            pltpu.SemaphoreType.DMA,
        ],
        out_shape=jax.ShapeDtypeStruct((shares, dense, 128), bf16),
        compiler_params=params(),
    )(q, mine, other, key_expand, value_expand, mla_output)


def gather_share_kernel(parts_ref, x_ref, *refs):
    sides, (out_ref, decode_ref) = refs[:-2], refs[-2:]
    decode_ref[...] = sum(side[...].astype(f32) for side in sides).astype(bf16)
    rows, share = x_ref.shape
    x = x_ref[...].astype(f32)
    total = jnp.sum(parts_ref[...].astype(f32), axis=0)
    left = total[:rows] + x[:, :128]
    right = total[rows : 2 * rows] + x[:, 128:256]
    rest = total[2 * rows :]
    wide = share - 256
    rest = jnp.concatenate(
        [rest[:, i * wide : (i + 1) * wide] for i in range(128 // wide)], axis=0
    )
    rest = rest + x[:, 256:]
    out_ref[...] = jnp.concatenate([left.T, right.T, rest.T], axis=0).astype(bf16)


def gather_share(parts, x, *sides):
    rows, share = x.shape
    return pl.pallas_call(
        gather_share_kernel,
        out_shape=(
            jax.ShapeDtypeStruct((share, rows), bf16),
            jax.ShapeDtypeStruct(sides[0].shape, bf16),
        ),
        compiler_params=params(20),
    )(parts, x, *sides)


def split_level(level, rows):
    lane = lax.broadcasted_iota(jnp.int32, (rows, SENT - LAT), 1)
    high = level.astype(bf16).astype(f32)
    middle = (level - high).astype(bf16).astype(f32)
    low = level - high - middle
    return jnp.where(
        lane == 0, high, jnp.where(lane == 1, middle, jnp.where(lane == 2, low, 0.0))
    )


def join_level(part):
    tail = part[:, LAT:].astype(f32)
    lane = lax.broadcasted_iota(jnp.int32, tail.shape, 1)
    return jnp.sum(jnp.where(lane < 3, tail, 0.0), axis=-1, keepdims=True)


def merge_parts(parts):
    levels = [join_level(p) for p in parts]
    highest = functools.reduce(jnp.maximum, levels)
    weights = [jnp.exp2(v - highest) for v in levels]
    total = sum(weights)
    mixed = sum(p[:, :LAT].astype(f32) * w for p, w in zip(parts, weights)) / total
    return mixed, highest + jnp.log2(total)


def pages_kernel(group, requests, count, *refs):
    q_refs = refs[: 2 * count]
    keys_ref, fresh_ref, owner_ref, keep_ref, send_ref = refs[2 * count :]
    each = q_refs[0].shape[0]
    block = 2 * each
    keys = keys_ref[...]
    fresh = fresh_ref[...]
    within = lax.rem(lax.broadcasted_iota(jnp.int32, (block, 1), 0), group)
    request = lax.rem(within, requests)
    step = within // requests
    live_old = owner_ref[...] == request
    column = lax.broadcasted_iota(jnp.int32, (1, fresh.shape[0]), 1)
    fresh_step = column // requests + lax.axis_index("grp") * group
    live_new = (lax.rem(column, requests) == request) & (fresh_step <= step)
    scores = []
    for i in range(0, 2 * count, 2):
        q = jnp.concatenate([q_refs[i][:, :WIDE], q_refs[i + 1][:, :WIDE]], axis=0)
        scores.append(
            (
                jnp.where(live_old, dot_nt(q, keys), masked_score),
                jnp.where(live_new, dot_nt(q, fresh), masked_score),
            )
        )
    for i, (old, new) in enumerate(scores):
        highest = jnp.maximum(
            jnp.max(old, axis=-1, keepdims=True), jnp.max(new, axis=-1, keepdims=True)
        )
        highest = jnp.maximum(highest, 0.1 * masked_score)
        w_old = jnp.exp2(old - highest)
        w_new = jnp.exp2(new - highest)
        total = jnp.sum(w_old, axis=-1, keepdims=True) + jnp.sum(w_new, axis=-1, keepdims=True)
        some = total > 0.0
        safe = jnp.where(some, total, 1.0)
        mixed = dot_nn(w_old.astype(bf16), keys[:, :LAT]) + dot_nn(
            w_new.astype(bf16), fresh[:, :LAT]
        )
        level = jnp.where(some, highest + jnp.log2(safe), masked_score)
        out_ref = keep_ref if 2 * i < count else send_ref
        both = jnp.concatenate([mixed / safe, split_level(level, block)], axis=-1).astype(bf16)
        out_ref[2 * i % count] = both[:each]
        out_ref[2 * i % count + 1] = both[each:]


def pages_attend(queries, keys, fresh, owner, group, requests):
    count = len(queries) // 2
    vmem = pl.BlockSpec(memory_space=pltpu.VMEM)
    shape = jax.ShapeDtypeStruct((count, queries[0].shape[0], SENT), bf16)
    return pl.pallas_call(
        functools.partial(pages_kernel, group, requests, count),
        in_specs=[vmem] * (2 * count + 3),
        out_specs=(vmem, vmem),
        out_shape=(shape, shape),
        compiler_params=params(24),
    )(*queries, keys, fresh, owner)


def merge_kernel(keep_ref, got_ref, *out_refs):
    for i, out_ref in enumerate(out_refs):
        mixed, level = merge_parts([keep_ref[i], got_ref[i]])
        out_ref[...] = jnp.concatenate(
            [mixed, split_level(level, mixed.shape[0])], axis=-1
        ).astype(bf16)


def merge_pair(keep, got):
    shape = jax.ShapeDtypeStruct(keep.shape[1:], bf16)
    return pl.pallas_call(
        merge_kernel,
        out_shape=(shape,) * keep.shape[0],
        compiler_params=params(24),
    )(keep, got)


def combine_kernel(heads, count, *refs):
    ve_ref, out_ref, sum_ref = refs[count:]
    mixed, _ = merge_parts([ref[...] for ref in refs[:count]])
    each = mixed.shape[0] // heads
    head_values = [
        dot_nn(mixed[h * each : (h + 1) * each].astype(bf16), ve_ref[:, h * VH : (h + 1) * VH])
        for h in range(heads)
    ]
    joined = jnp.concatenate(head_values, axis=-1).astype(bf16)
    sum_ref[...] = dot_nn(joined, out_ref[...]).astype(bf16)


def combine(parts, value_expand, mla_output):
    heads = value_expand.shape[1] // VH
    return pl.pallas_call(
        functools.partial(combine_kernel, heads, len(parts)),
        out_shape=jax.ShapeDtypeStruct((parts[0].shape[0] // heads, mla_output.shape[1]), bf16),
        compiler_params=params(20),
    )(*parts, value_expand, mla_output)


def kda_kernel(
    heads,
    requests,
    rate_ref,
    one_hbm,
    two_hbm,
    dec_hbm,
    inputs_hbm,
    beta_hbm,
    decay_down_hbm,
    gate_down_hbm,
    decay_up_hbm,
    gate_up_hbm,
    states_hbm,
    output_hbm,
    hidden_ref,
    keep_ref,
    send_ref,
    one_ref,
    two_ref,
    dec_ref,
    inputs_ref,
    beta_ref,
    decay_down_ref,
    gate_down_ref,
    decay_up_ref,
    gate_up_ref,
    states_ref,
    output_ref,
    by_share,
    summed_ref,
    sems,
):
    shares, rows, share = by_share.shape
    grp = lax.axis_index("grp")
    pairs = [
        (one_hbm, one_ref),
        (two_hbm, two_ref),
        (dec_hbm, dec_ref),
        (inputs_hbm.at[1], inputs_ref.at[1]),
        (beta_hbm, beta_ref),
        (decay_down_hbm, decay_down_ref),
        (gate_down_hbm, gate_down_ref),
        (decay_up_hbm, decay_up_ref),
        (gate_up_hbm, gate_up_ref),
        (inputs_hbm.at[0], inputs_ref.at[0]),
        (states_hbm, states_ref),
        (inputs_hbm.at[2], inputs_ref.at[2]),
        (output_hbm, output_ref),
    ]
    loads = [pltpu.make_async_copy(a, b, sems.at[i]) for i, (a, b) in enumerate(pairs)]
    for load in loads:
        load.start()
    for load in loads[:3]:
        load.wait()
    hidden = dec_ref[...].astype(f32) + (
        one_ref[...].astype(f32) + two_ref[...].astype(f32)
    )
    for g in range(shares):
        by_share[g] = hidden[:, g * share : (g + 1) * share]
    hidden_ref[...] = by_share[grp]
    kin = norm_rows(hidden).astype(bf16)
    loads[3].wait()
    all_keys = dot_nn(kin, inputs_ref[1])
    for load in loads[4:9]:
        load.wait()
    beta = jax.nn.sigmoid(dot_nt(kin, beta_ref[...]))
    decay_low = dot_nn(kin, decay_down_ref[...]).astype(bf16)
    rises = jax.nn.softplus(dot_nn(decay_low, decay_up_ref[...]))
    gate_low = dot_nn(kin, gate_down_ref[...]).astype(bf16)
    gates = jax.nn.sigmoid(dot_nn(gate_low, gate_up_ref[...]))
    loads[9].wait()
    all_queries = dot_nn(kin, inputs_ref[0])
    loads[10].wait()
    held_states = [states_ref[:, r].astype(f32) for r in range(requests)]
    steps = rows // requests
    piece = held_states[0].shape[1] // heads
    at = lambda values, t: values[t * requests : (t + 1) * requests]
    along = lambda a, b: jnp.sum(a * b, axis=-1, keepdims=True)
    ready = []
    for head in range(heads):
        lanes = slice(head * DK, (head + 1) * DK)
        q = unit_rows(all_queries[:, lanes]) * DK ** (-0.5)
        k = unit_rows(all_keys[:, lanes])
        rate = jnp.exp(jnp.full((1, DK), rate_ref[head], f32))
        a = jnp.exp(-rate * rises[:, lanes])
        vectors = []
        kept = None
        for t in range(steps):
            kept = at(a, t) if kept is None else kept * at(a, t)
            vectors += [kept * at(k, t), kept * at(q, t)]
        vectors = jnp.concatenate(vectors, axis=0)
        high = vectors.astype(bf16).astype(f32)
        both = jnp.concatenate([high, vectors - high], axis=0)
        owner = lax.rem(lax.broadcasted_iota(jnp.int32, (both.shape[0], 1), 0), requests)
        spread = jnp.concatenate(
            [jnp.where(owner == r, both, 0.0) for r in range(requests)], axis=-1
        ).astype(bf16)
        facing = jnp.concatenate(
            [
                held_states[r][:, head * piece : (head + 1) * piece].reshape(DV, DK)
                for r in range(requests)
            ],
            axis=-1,
        ).astype(bf16)
        met = dot_nt(spread, facing)
        ready.append((q, k, a, met[: vectors.shape[0]] + met[vectors.shape[0] :]))
    loads[11].wait()
    all_values = dot_nn(kin, inputs_ref[2])
    blended = []
    for head in range(heads):
        lanes = slice(head * DK, (head + 1) * DK)
        q, k, a, met = ready[head]
        v = all_values[:, lanes]
        b = beta[:, head : head + 1]
        carried = []
        reads = []
        for t in range(steps):
            seen = at(met, 2 * t)
            read = at(met, 2 * t + 1)
            carried = [(u, w * at(a, t)) for u, w in carried]
            for u, w in carried:
                seen = seen + u * along(w, at(k, t))
            u = at(b, t) * (at(v, t) - seen)
            carried.append((u, at(k, t)))
            for u, w in carried:
                read = read + u * along(w, at(q, t))
            reads.append(read)
        read = jnp.concatenate(reads, axis=0)
        blended.append(norm_rows(read) * gates[:, lanes])
    mixed = jnp.concatenate(blended, axis=-1).astype(bf16)
    loads[12].wait()
    summed = dot_nn(mixed, output_ref[...])
    for g in range(shares):
        summed_ref[g] = summed[:, g * share : (g + 1) * share]
    core = lax.rem(grp, 2)
    for by in range(shares // 2):
        pair = 2 * lax.rem(grp // 2 + by, shares // 2)
        keep_ref[by] = summed_ref[pair + core]
        send_ref[by] = summed_ref[pair + 1 - core].astype(bf16)


def kda(shares, rate, *operands):
    dec, beta_t, states = operands[2], operands[4], operands[9]
    rows, width = dec.shape
    heads = beta_t.shape[0]
    requests = states.shape[1]
    share = width // shares
    sides = shares // 2
    vmem = pl.BlockSpec(memory_space=pltpu.VMEM)
    return pl.pallas_call(
        functools.partial(kda_kernel, heads, requests),
        in_specs=[pl.BlockSpec(memory_space=pltpu.SMEM)]
        + [pl.BlockSpec(memory_space=pltpu.HBM)] * len(operands),
        out_specs=(vmem, vmem, vmem),
        out_shape=(
            jax.ShapeDtypeStruct((rows, share), f32),
            jax.ShapeDtypeStruct((sides, rows, share), f32),
            jax.ShapeDtypeStruct((sides, rows, share), bf16),
        ),
        scratch_shapes=[pltpu.VMEM(a.shape, a.dtype) for a in operands]
        + [
            pltpu.VMEM((shares, rows, share), f32),
            pltpu.VMEM((shares, rows, share), f32),
            pltpu.SemaphoreType.DMA((len(operands) + 2,)),
        ],
        compiler_params=params(),
    )(rate, *operands)


def shards(
    x_group,
    decode_input,
    prompt_len,
    latent_pages,
    slot_target,
    page_counts,
    kda_state,
    query_proj,
    latent_proj,
    key_expand,
    value_expand,
    mla_output,
    kda_inputs,
    kda_beta,
    decay_down,
    decay_up,
    gate_down,
    gate_up,
    decay_log,
    kda_output,
):
    seq_index = lax.axis_index("seq")
    grp_index = lax.axis_index("grp")
    seq_size = lax.axis_size("seq")
    grp_size = lax.axis_size("grp")
    rows, width = x_group.shape
    steps, requests, _ = decode_input.shape
    decode_rows = steps * requests
    share = width // grp_size
    dec = decode_input.reshape(decode_rows, width)

    own_tokens = slice_pages(latent_pages[0], grp_size)
    _, slots, tokens, _ = own_tokens.shape
    core = grp_index % 2
    target = lax.dynamic_slice_in_dim(slot_target[:, 0, :], core * slots, slots, 1)
    owner = target // MAXP
    lengths = jnp.sum(
        jnp.where(owner[..., None] == jnp.arange(requests), prompt_len, 0), axis=-1
    )
    held = core * slots + jnp.arange(slots)[None, :] < page_counts
    token_pos = (
        ((target % MAXP) * PAGE + (grp_index // 2) * tokens)[..., None] + jnp.arange(tokens)
    )
    key_owner = jnp.where(
        held[..., None] & (token_pos < lengths[..., None]), owner[..., None], -1
    ).reshape(1, -1)

    x_rows, _ = lax.optimization_barrier((x_group, own_tokens))
    reach = max(rows, MAXP * PAGE + steps)
    fine = rope_tables(range(-(-reach // 8) * 8))
    coarse = rope_tables([rows * i for i in range(seq_size)])
    own_latent, fresh, q_decode = front(
        prompt_len, fine, coarse, x_rows, dec, latent_proj.T, query_proj, key_expand
    )
    sides = grp_size // 2

    def shift(value, by):
        return lax.ppermute(
            value, "grp", [(g, (g + 2 * by) % grp_size) for g in range(grp_size)]
        )

    def swap(value):
        return lax.ppermute(value, "grp", [(g, g ^ 1) for g in range(grp_size)])

    arrived = lax.all_to_all(own_tokens, "seq", split_axis=0, concat_axis=0, tiled=True)
    queries = [q_decode] + [shift(q_decode, by) for by in range(1, sides)]
    own_latent, _, _, key_owner = lax.optimization_barrier(
        (own_latent, arrived, queries[1], key_owner)
    )
    mine = lax.all_to_all(own_latent, "seq", split_axis=0, concat_axis=0, tiled=True)
    page_keys = arrived.reshape(-1, WIDE)
    queries = queries + [swap(q) for q in queries]
    keep, send = pages_attend(
        queries, page_keys, fresh, key_owner, decode_rows, requests
    )
    merged = merge_pair(keep, swap(send))
    x_again, _ = lax.optimization_barrier((x_group, merged[1]))
    q_prefill, state_rows = prefill_queries(
        fine, coarse, x_again, query_proj, kda_state.reshape(kda_state.shape[0], -1, DK)
    )
    partial = [merged[0]] + [shift(merged[by], -by) for by in range(1, sides)]
    partial[0], _ = lax.optimization_barrier((partial[0], q_prefill))
    mla_part = combine(partial, value_expand, mla_output)
    add = lambda one, two: one.astype(f32) + two.astype(f32)
    trade = lambda value, bits: lax.ppermute(
        value, "grp", [(g, g ^ bits) for g in range(grp_size)]
    )
    mla_pair = add(mla_part, swap(mla_part)).astype(bf16)
    mla_near = trade(mla_pair, 2)
    mine, _ = lax.optimization_barrier((mine, mla_pair))
    state_rows, _ = lax.optimization_barrier((state_rows, mine))
    states = lax.all_to_all(
        state_rows, "seq", split_axis=0, concat_axis=0, tiled=True
    ).reshape((seq_size, requests) + state_rows.shape[1:])
    mla_half = add(mla_pair, mla_near).astype(bf16)
    mla_rest = trade(mla_half, 6)

    prefill_part = prefill_attend(
        q_prefill, mine, swap(mine), key_expand, value_expand, mla_output, grp_size
    )
    mla_half, mla_rest, prefill_part = lax.optimization_barrier(
        (mla_half, mla_rest, prefill_part)
    )
    prefill_parts = lax.all_to_all(
        prefill_part, "grp", split_axis=0, concat_axis=0, tiled=True
    )
    own_columns = lax.dynamic_slice_in_dim(x_group, grp_index * share, share, 1)

    hidden_share, keep, send = kda(
        grp_size,
        decay_log,
        mla_half,
        mla_rest,
        dec,
        kda_inputs.transpose(1, 0, 2),
        kda_beta.T,
        decay_down,
        gate_down,
        decay_up,
        gate_up,
        states,
        kda_output,
    )
    crossing = swap(send)
    kda_sides = [keep[by] + crossing[by].astype(f32) for by in range(sides)]
    kda_sides[0] = kda_sides[0] + hidden_share
    for by in range(1, sides):
        kda_sides[by] = shift(kda_sides[by].astype(bf16), by)
    prefill_out, decode_out = gather_share(prefill_parts, own_columns, *kda_sides)
    return (prefill_out.T, decode_out.reshape(steps, requests, share))


def solution(mesh):
    in_specs = (
        P("seq", None),
        P(None, "seq", None),
        P("seq"),
        P("seq", None, None, None, None),
        P(None, "seq", None),
        P(None, "seq"),
        P(None, "grp", "seq", None),
        P(None, "grp"),
        P(),
        P(None, "grp"),
        P(None, "grp"),
        P("grp", None),
        P(None, None, "grp"),
        P(None, "grp"),
        P(),
        P(None, "grp"),
        P(),
        P(None, "grp"),
        P("grp"),
        P("grp", None),
    )
    out_specs = (P("seq", "grp"), P(None, "seq", "grp"))
    return jax.shard_map(shards, mesh=mesh, in_specs=in_specs, out_specs=out_specs, check_vma=False)
```

```python
import functools

import jax
import jax.numpy as jnp
import numpy as np
from jax import lax
from jax.experimental import pallas as pl
from jax.experimental.pallas import tpu as pltpu
from jax.sharding import PartitionSpec as P

LAT = 512
ROPE = 64
NOPE = 128
VH = 128
DK = 128
DV = 128
PAGE = 64
MAXP = 12
WIDE = LAT + ROPE
SENT = LAT + 128

epsilon = 1e-06
masked_score = -1e30
scale = (NOPE + ROPE) ** (-0.5)
log2e = 1.4426950408889634

f32 = jnp.float32
bf16 = jnp.bfloat16
MIB = 1024 * 1024


def params(mib=58):
    return pltpu.CompilerParams(vmem_limit_bytes=mib * MIB)


def dot_nt(a, b):
    return lax.dot_general(a, b, (((1,), (1,)), ((), ())), preferred_element_type=f32)


def dot_nn(a, b):
    return lax.dot_general(a, b, (((1,), (0,)), ((), ())), preferred_element_type=f32)


def norm_rows(values):
    return values * lax.rsqrt(jnp.mean(values * values, axis=-1, keepdims=True) + epsilon)


def unit_rows(values):
    return values * lax.rsqrt(jnp.sum(values * values, axis=-1, keepdims=True) + epsilon)


def turn(values, cos, sin):
    half = ROPE // 2
    swapped = jnp.concatenate([values[:, half:], values[:, :half]], axis=-1)
    return values * cos + swapped * sin


def rope_tables(positions):
    half = ROPE // 2
    frequency = np.exp(-np.log(10000.0) * np.arange(half) / half)
    angles = np.asarray(positions, np.float64)[:, None] * frequency
    cos, sin = np.cos(angles), np.sin(angles)
    both = np.concatenate([cos, cos, -sin, sin], -1)
    return jnp.asarray(both, f32)


def slice_kernel(pages_hbm, own_hbm, held, in_sems, out_sems):
    grp = lax.axis_index("grp")
    owners, slots, tokens, _ = own_hbm.shape
    parts = in_sems.shape[0]
    each = owners // parts
    first = lax.rem(grp, 2) * slots
    row = pl.multiple_of((grp // 2) * tokens, tokens)
    loads = [
        pltpu.make_async_copy(
            pages_hbm.at[pl.ds(i * each, each), pl.ds(first, slots), pl.ds(row, tokens), :],
            held.at[pl.ds(i * each, each)],
            in_sems.at[i],
        )
        for i in range(parts)
    ]
    stores = [
        pltpu.make_async_copy(
            held.at[pl.ds(i * each, each)], own_hbm.at[pl.ds(i * each, each)], out_sems.at[i]
        )
        for i in range(parts)
    ]
    for load in loads:
        load.start()
    for load, store in zip(loads, stores):
        load.wait()
        store.start()
    for store in stores:
        store.wait()


def slice_pages(pages, grp_size):
    owners, cap, page, wide = pages.shape
    shape = (owners, cap // 2, page // (grp_size // 2), wide)
    parts = 4
    hbm = pl.BlockSpec(memory_space=pltpu.HBM)
    return pl.pallas_call(
        slice_kernel,
        in_specs=[hbm],
        out_specs=hbm,
        out_shape=jax.ShapeDtypeStruct(shape, bf16),
        scratch_shapes=[
            pltpu.VMEM(shape, bf16),
            pltpu.SemaphoreType.DMA((parts,)),
            pltpu.SemaphoreType.DMA((parts,)),
        ],
        compiler_params=params(),
    )(pages)


def pack_rope(values):
    count = LAT // ROPE
    piece = values.shape[0] // count
    return jnp.concatenate(
        [values[i * piece : (i + 1) * piece] for i in range(count)], axis=1
    )


def unpack_rope(packed):
    return jnp.concatenate(
        [packed[:, i * ROPE : (i + 1) * ROPE] for i in range(LAT // ROPE)], axis=0
    )


def turned_tables(base, near):
    base_cos, base_sin = base[:, :ROPE], base[:, ROPE:]
    near_cos, near_sin = near[:, :ROPE], near[:, ROPE:]
    return jnp.concatenate(
        [base_cos * near_cos - base_sin * near_sin, base_sin * near_cos + base_cos * near_sin],
        axis=-1,
    )


def front_kernel(
    count,
    lengths_ref,
    fine_hbm,
    coarse_hbm,
    x_hbm,
    dec_hbm,
    lat_proj_hbm,
    query_proj_hbm,
    expand_hbm,
    lat_hbm,
    fresh_ref,
    qd_ref,
    fine_ref,
    coarse_ref,
    x_ref,
    dec_ref,
    lat_proj_ref,
    query_proj_ref,
    expand_ref,
    normed,
    turns,
    lat_ref,
    sems,
    out_sems,
):
    seq, grp = lax.axis_index("seq"), lax.axis_index("grp")
    rows, width = x_ref.shape
    core = lax.rem(grp, 2)
    heads = expand_ref.shape[1] // NOPE
    requests = lengths_ref.shape[0]
    chunks = 3
    depth = width // chunks
    own = pl.ds(pl.multiple_of(core * rows, rows), rows)
    first = [
        pltpu.make_async_copy(x_hbm.at[own], x_ref, sems.at[0]),
        pltpu.make_async_copy(dec_hbm, dec_ref, sems.at[1]),
        pltpu.make_async_copy(lat_proj_hbm, lat_proj_ref, sems.at[2]),
        pltpu.make_async_copy(fine_hbm, fine_ref, sems.at[3]),
        pltpu.make_async_copy(coarse_hbm, coarse_ref, sems.at[4]),
    ]
    later = [
        pltpu.make_async_copy(
            query_proj_hbm.at[pl.ds(i * depth, depth)],
            query_proj_ref.at[pl.ds(i * depth, depth)],
            sems.at[5 + i],
        )
        for i in range(chunks)
    ]
    later.append(pltpu.make_async_copy(expand_hbm, expand_ref, sems.at[5 + chunks]))
    for load in first + later:
        load.start()
    first[0].wait()
    normed[:rows] = norm_rows(x_ref[...].astype(f32)).astype(bf16)
    first[1].wait()
    tail = normed.shape[0] - rows - count
    normed[rows:] = jnp.concatenate(
        [norm_rows(dec_ref[...].astype(f32)), jnp.zeros((tail, width), f32)], axis=0
    ).astype(bf16)
    first[3].wait()
    first[4].wait()
    for r in range(requests):
        for t in range(count // requests):
            at = rows + t * requests + r
            turns[at : at + 1] = fine_ref[pl.ds(lengths_ref[r] + t, 1)]
    turns[rows + count :] = jnp.zeros((tail, 2 * ROPE), f32)
    turns[:rows] = turned_tables(coarse_ref[pl.ds(seq, 1)], fine_ref[own])
    first[2].wait()
    projected = dot_nt(normed[...], lat_proj_ref[...])
    cos, sin = turns[:, :ROPE], turns[:, ROPE:]
    latent = jnp.concatenate(
        [norm_rows(projected[:, :LAT]), turn(projected[:, LAT:], cos, sin)], axis=-1
    )
    lat_ref[:rows] = latent[:rows, :LAT].astype(bf16)
    lat_ref[rows:] = pack_rope(latent[:rows, LAT:]).astype(bf16)
    stores = [
        pltpu.make_async_copy(lat_ref, lat_hbm.at[i], out_sems.at[i])
        for i in range(lat_hbm.shape[0])
    ]
    for store in stores:
        store.start()
    fresh_ref[...] = latent[rows:].astype(bf16)
    total = None
    for i in range(chunks):
        later[i].wait()
        lanes = slice(i * depth, (i + 1) * depth)
        term = dot_nn(normed[rows:, lanes], query_proj_ref[lanes])
        total = term if total is None else total + term
    later[chunks].wait()
    decode = []
    for head in range(heads):
        at = head * (NOPE + ROPE)
        turned = turn(total[:, at + NOPE : at + NOPE + ROPE], cos[rows:], sin[rows:])
        absorbed = dot_nt(
            total[:, at : at + NOPE].astype(bf16),
            expand_ref[:, head * NOPE : (head + 1) * NOPE],
        )
        blank = jnp.zeros((absorbed.shape[0], SENT - WIDE), f32)
        decode.append(jnp.concatenate([absorbed, turned, blank], axis=-1)[:count])
    qd_ref[...] = (jnp.concatenate(decode, axis=0) * (scale * log2e)).astype(bf16)
    for store in stores:
        store.wait()


def front(lengths, fine, coarse, x, dec, lat_proj_t, query_proj, key_expand):
    rows, width = x.shape
    half = rows // 2
    count = dec.shape[0]
    heads = key_expand.shape[1] // NOPE
    padded = count + 8
    packed = half + half * ROPE // LAT
    seq_size = coarse.shape[0]
    smem = pl.BlockSpec(memory_space=pltpu.SMEM)
    vmem = pl.BlockSpec(memory_space=pltpu.VMEM)
    hbm = pl.BlockSpec(memory_space=pltpu.HBM)
    return pl.pallas_call(
        functools.partial(front_kernel, count),
        in_specs=[smem] + [hbm] * 7,
        out_specs=(hbm, vmem, vmem),
        out_shape=(
            jax.ShapeDtypeStruct((seq_size, packed, LAT), bf16),
            jax.ShapeDtypeStruct((padded, WIDE), bf16),
            jax.ShapeDtypeStruct((heads * count, SENT), bf16),
        ),
        scratch_shapes=[
            pltpu.VMEM(fine.shape, f32),
            pltpu.VMEM(coarse.shape, f32),
            pltpu.VMEM((half, width), bf16),
            pltpu.VMEM(dec.shape, bf16),
            pltpu.VMEM(lat_proj_t.shape, bf16),
            pltpu.VMEM(query_proj.shape, bf16),
            pltpu.VMEM(key_expand.shape, bf16),
            pltpu.VMEM((half + padded, width), bf16),
            pltpu.VMEM((half + padded, 2 * ROPE), f32),
            pltpu.VMEM((packed, LAT), bf16),
            pltpu.SemaphoreType.DMA((9,)),
            pltpu.SemaphoreType.DMA((seq_size,)),
        ],
        compiler_params=params(),
    )(lengths, fine, coarse, x, dec, lat_proj_t, query_proj, key_expand)


def prefill_query_kernel(
    fine_hbm,
    coarse_hbm,
    x_hbm,
    query_proj_hbm,
    state_hbm,
    qp_ref,
    state_out_ref,
    fine_ref,
    coarse_ref,
    x_ref,
    query_proj_ref,
    state_ref,
    sems,
):
    rows, width = x_ref.shape
    heads = qp_ref.shape[0]
    chunks = 3
    depth = width // chunks
    loads = [
        pltpu.make_async_copy(x_hbm, x_ref, sems.at[0]),
        pltpu.make_async_copy(fine_hbm.at[pl.ds(0, rows)], fine_ref, sems.at[1]),
        pltpu.make_async_copy(coarse_hbm, coarse_ref, sems.at[2]),
        pltpu.make_async_copy(state_hbm, state_ref, sems.at[3]),
    ]
    loads += [
        pltpu.make_async_copy(
            query_proj_hbm.at[pl.ds(i * depth, depth)],
            query_proj_ref.at[pl.ds(i * depth, depth)],
            sems.at[4 + i],
        )
        for i in range(chunks)
    ]
    for load in loads:
        load.start()
    loads[0].wait()
    normed = norm_rows(x_ref[...].astype(f32)).astype(bf16)
    loads[1].wait()
    loads[2].wait()
    turns = turned_tables(coarse_ref[pl.ds(lax.axis_index("seq"), 1)], fine_ref[...])
    cos, sin = turns[:, :ROPE], turns[:, ROPE:]
    loads[3].wait()
    state_out_ref[...] = state_ref[...].astype(bf16)
    total = None
    for i in range(chunks):
        loads[4 + i].wait()
        lanes = slice(i * depth, (i + 1) * depth)
        term = dot_nn(normed[:, lanes], query_proj_ref[lanes])
        total = term if total is None else total + term
    for head in range(heads):
        at = head * (NOPE + ROPE)
        turned = turn(total[:, at + NOPE : at + NOPE + ROPE], cos, sin)
        qp_ref[head] = (
            jnp.concatenate([total[:, at : at + NOPE], turned], axis=-1) * (scale * log2e)
        ).astype(bf16)


def prefill_queries(fine, coarse, x, query_proj, states):
    rows = x.shape[0]
    heads = query_proj.shape[1] // (NOPE + ROPE)
    vmem = pl.BlockSpec(memory_space=pltpu.VMEM)
    return pl.pallas_call(
        prefill_query_kernel,
        in_specs=[pl.BlockSpec(memory_space=pltpu.HBM)] * 5,
        out_specs=(vmem, vmem),
        out_shape=(
            jax.ShapeDtypeStruct((heads, rows, NOPE + ROPE), bf16),
            jax.ShapeDtypeStruct(states.shape, bf16),
        ),
        scratch_shapes=[
            pltpu.VMEM((rows, fine.shape[1]), f32),
            pltpu.VMEM(coarse.shape, f32),
            pltpu.VMEM(x.shape, bf16),
            pltpu.VMEM(query_proj.shape, bf16),
            pltpu.VMEM(states.shape, f32),
            pltpu.SemaphoreType.DMA((7,)),
        ],
        compiler_params=params(),
    )(fine, coarse, x, query_proj, states)


def pack_shares(summed, sum_ref):
    shares = sum_ref.shape[0]
    rows, width = summed.shape
    share = width // shares
    for g in range(shares):
        part = summed[:, g * share : (g + 1) * share]
        sum_ref[g, :rows] = part[:, :128].astype(bf16)
        sum_ref[g, rows : 2 * rows] = part[:, 128:256].astype(bf16)
        rest = part[:, 256:]
        count = 128 // rest.shape[1]
        piece = rows // count
        sum_ref[g, 2 * rows :] = jnp.concatenate(
            [rest[i * piece : (i + 1) * piece] for i in range(count)], axis=1
        ).astype(bf16)


def flash_kernel(
    heads, q_ref, mine_ref, other_ref, ke_ref, ve_ref, out_hbm, sum_ref,
    peak, acc, vet_ref, out_ref, sem,
):
    step = pl.program_id(0)
    rows = q_ref.shape[1]
    half = rows // 2
    first, core = lax.axis_index("seq") * rows, lax.rem(lax.axis_index("grp"), 2)
    side = mine_ref.shape[0] * half
    block = 2 * side
    load = pltpu.make_async_copy(out_hbm, out_ref, sem)

    @pl.when(step == 0)
    def _():
        load.start()
        vet_ref[...] = ve_ref[...].astype(f32).T.astype(bf16)
        peak[...] = jnp.full_like(peak, masked_score)
        acc[...] = jnp.zeros_like(acc)

    def work(masked):
        sources = [(ref, i) for ref in (mine_ref, other_ref) for i in range(ref.shape[0])]
        low = jnp.concatenate([ref[i, :half] for ref, i in sources], axis=0)
        rope = jnp.concatenate([unpack_rope(ref[i, half:]) for ref, i in sources], axis=0)
        ones = jnp.ones((16, block), bf16)
        keys = dot_nn(low, ke_ref[...]).astype(bf16)
        values = dot_nt(vet_ref[...], low).astype(bf16)
        scores = []
        for head in range(heads):
            whole_keys = jnp.concatenate(
                [keys[:, head * NOPE : (head + 1) * NOPE], rope], axis=-1
            )
            scores.append(dot_nt(whole_keys, q_ref[head]))
        if masked:
            ahead = lax.broadcasted_iota(jnp.int32, (half, rows), 0) - lax.broadcasted_iota(
                jnp.int32, (half, rows), 1
            )
            count = mine_ref.shape[0]
            limits = [
                first - (step * count + i) * rows - which * half
                for which in (core, 1 - core)
                for i in range(count)
            ]
            scores = [
                jnp.concatenate(
                    [
                        jnp.where(ahead <= limit, s[j * half : (j + 1) * half], masked_score)
                        for j, limit in enumerate(limits)
                    ],
                    axis=0,
                )
                for s in scores
            ]
        for head in range(heads):
            old = peak[head]
            new = jnp.maximum(old, jnp.max(scores[head], axis=0, keepdims=True))
            fade = jnp.exp2(old - new)
            weights = jnp.exp2(scores[head] - new).astype(bf16)
            peak[head] = new
            carried = jnp.concatenate([values[head * VH : (head + 1) * VH], ones], axis=0)
            acc[head] = acc[head] * fade + dot_nn(carried, weights)

    @pl.when((step + 1) * block <= first + 1)
    def _():
        work(False)

    @pl.when(((step + 1) * block > first + 1) & (step * block < first + rows))
    def _():
        work(True)

    @pl.when(step == pl.num_programs(0) - 1)
    def _():
        mixed = jnp.concatenate(
            [(acc[h, :VH] / acc[h, VH : VH + 1]).T for h in range(heads)], axis=-1
        ).astype(bf16)
        load.wait()
        pack_shares(dot_nn(mixed, out_ref[...]), sum_ref)


def prefill_attend(q, mine, other, key_expand, value_expand, mla_output, shares):
    heads, rows, _ = q.shape
    sources, packed, _ = mine.shape
    side = max(1, min(sources, 2048 // rows))
    width = mla_output.shape[1]
    dense = rows * width // shares // 128
    whole = lambda shape: pl.BlockSpec(shape, lambda i: (0,) * len(shape))
    return pl.pallas_call(
        functools.partial(flash_kernel, heads),
        grid=(sources // side,),
        in_specs=[
            whole(q.shape),
            pl.BlockSpec((side, packed, LAT), lambda i: (i, 0, 0)),
            pl.BlockSpec((side, packed, LAT), lambda i: (i, 0, 0)),
            whole(key_expand.shape),
            whole(value_expand.shape),
            pl.BlockSpec(memory_space=pltpu.HBM),
        ],
        out_specs=whole((shares, dense, 128)),
        scratch_shapes=[
            pltpu.VMEM((heads, 1, rows), f32),
            pltpu.VMEM((heads, VH + 16, rows), f32),
            pltpu.VMEM((value_expand.shape[1], value_expand.shape[0]), bf16),
            pltpu.VMEM(mla_output.shape, bf16),
            pltpu.SemaphoreType.DMA,
        ],
        out_shape=jax.ShapeDtypeStruct((shares, dense, 128), bf16),
        compiler_params=params(),
    )(q, mine, other, key_expand, value_expand, mla_output)


def gather_share_kernel(parts_ref, x_ref, *refs):
    sides, (out_ref, decode_ref) = refs[:-2], refs[-2:]
    decode_ref[...] = sum(side[...].astype(f32) for side in sides).astype(bf16)
    rows, share = x_ref.shape
    x = x_ref[...].astype(f32)
    total = jnp.sum(parts_ref[...].astype(f32), axis=0)
    left = total[:rows] + x[:, :128]
    right = total[rows : 2 * rows] + x[:, 128:256]
    rest = total[2 * rows :]
    wide = share - 256
    rest = jnp.concatenate(
        [rest[:, i * wide : (i + 1) * wide] for i in range(128 // wide)], axis=0
    )
    rest = rest + x[:, 256:]
    out_ref[...] = jnp.concatenate([left.T, right.T, rest.T], axis=0).astype(bf16)


def gather_share(parts, x, *sides):
    rows, share = x.shape
    return pl.pallas_call(
        gather_share_kernel,
        out_shape=(
            jax.ShapeDtypeStruct((share, rows), bf16),
            jax.ShapeDtypeStruct(sides[0].shape, bf16),
        ),
        compiler_params=params(20),
    )(parts, x, *sides)


def split_level(level, rows):
    lane = lax.broadcasted_iota(jnp.int32, (rows, SENT - LAT), 1)
    high = level.astype(bf16).astype(f32)
    middle = (level - high).astype(bf16).astype(f32)
    low = level - high - middle
    return jnp.where(
        lane == 0, high, jnp.where(lane == 1, middle, jnp.where(lane == 2, low, 0.0))
    )


def join_level(part):
    tail = part[:, LAT:].astype(f32)
    lane = lax.broadcasted_iota(jnp.int32, tail.shape, 1)
    return jnp.sum(jnp.where(lane < 3, tail, 0.0), axis=-1, keepdims=True)


def merge_parts(parts):
    levels = [join_level(p) for p in parts]
    highest = functools.reduce(jnp.maximum, levels)
    weights = [jnp.exp2(v - highest) for v in levels]
    total = sum(weights)
    mixed = sum(p[:, :LAT].astype(f32) * w for p, w in zip(parts, weights)) / total
    return mixed, highest + jnp.log2(total)


def pages_kernel(group, requests, count, *refs):
    q_refs = refs[: 2 * count]
    keys_ref, fresh_ref, owner_ref, keep_ref, send_ref = refs[2 * count :]
    each = q_refs[0].shape[0]
    block = 2 * each
    keys = keys_ref[...]
    fresh = fresh_ref[...]
    within = lax.rem(lax.broadcasted_iota(jnp.int32, (block, 1), 0), group)
    request = lax.rem(within, requests)
    step = within // requests
    live_old = owner_ref[...] == request
    column = lax.broadcasted_iota(jnp.int32, (1, fresh.shape[0]), 1)
    fresh_step = column // requests + lax.axis_index("grp") * group
    live_new = (lax.rem(column, requests) == request) & (fresh_step <= step)
    scores = []
    for i in range(0, 2 * count, 2):
        q = jnp.concatenate([q_refs[i][:, :WIDE], q_refs[i + 1][:, :WIDE]], axis=0)
        scores.append(
            (
                jnp.where(live_old, dot_nt(q, keys), masked_score),
                jnp.where(live_new, dot_nt(q, fresh), masked_score),
            )
        )
    for i, (old, new) in enumerate(scores):
        highest = jnp.maximum(
            jnp.max(old, axis=-1, keepdims=True), jnp.max(new, axis=-1, keepdims=True)
        )
        highest = jnp.maximum(highest, 0.1 * masked_score)
        w_old = jnp.exp2(old - highest)
        w_new = jnp.exp2(new - highest)
        total = jnp.sum(w_old, axis=-1, keepdims=True) + jnp.sum(w_new, axis=-1, keepdims=True)
        some = total > 0.0
        safe = jnp.where(some, total, 1.0)
        mixed = dot_nn(w_old.astype(bf16), keys[:, :LAT]) + dot_nn(
            w_new.astype(bf16), fresh[:, :LAT]
        )
        level = jnp.where(some, highest + jnp.log2(safe), masked_score)
        out_ref = keep_ref if 2 * i < count else send_ref
        both = jnp.concatenate([mixed / safe, split_level(level, block)], axis=-1).astype(bf16)
        out_ref[2 * i % count] = both[:each]
        out_ref[2 * i % count + 1] = both[each:]


def pages_attend(queries, keys, fresh, owner, group, requests):
    count = len(queries) // 2
    vmem = pl.BlockSpec(memory_space=pltpu.VMEM)
    shape = jax.ShapeDtypeStruct((count, queries[0].shape[0], SENT), bf16)
    return pl.pallas_call(
        functools.partial(pages_kernel, group, requests, count),
        in_specs=[vmem] * (2 * count + 3),
        out_specs=(vmem, vmem),
        out_shape=(shape, shape),
        compiler_params=params(24),
    )(*queries, keys, fresh, owner)


def merge_kernel(keep_ref, got_ref, *out_refs):
    for i, out_ref in enumerate(out_refs):
        mixed, level = merge_parts([keep_ref[i], got_ref[i]])
        out_ref[...] = jnp.concatenate(
            [mixed, split_level(level, mixed.shape[0])], axis=-1
        ).astype(bf16)


def merge_pair(keep, got):
    shape = jax.ShapeDtypeStruct(keep.shape[1:], bf16)
    return pl.pallas_call(
        merge_kernel,
        out_shape=(shape,) * keep.shape[0],
        compiler_params=params(24),
    )(keep, got)


def combine_kernel(heads, count, *refs):
    ve_ref, out_ref, sum_ref = refs[count:]
    mixed, _ = merge_parts([ref[...] for ref in refs[:count]])
    each = mixed.shape[0] // heads
    head_values = [
        dot_nn(mixed[h * each : (h + 1) * each].astype(bf16), ve_ref[:, h * VH : (h + 1) * VH])
        for h in range(heads)
    ]
    joined = jnp.concatenate(head_values, axis=-1).astype(bf16)
    sum_ref[...] = dot_nn(joined, out_ref[...]).astype(bf16)


def combine(parts, value_expand, mla_output):
    heads = value_expand.shape[1] // VH
    return pl.pallas_call(
        functools.partial(combine_kernel, heads, len(parts)),
        out_shape=jax.ShapeDtypeStruct((parts[0].shape[0] // heads, mla_output.shape[1]), bf16),
        compiler_params=params(20),
    )(*parts, value_expand, mla_output)


def kda_kernel(
    heads,
    requests,
    rate_ref,
    one_hbm,
    two_hbm,
    dec_hbm,
    inputs_hbm,
    beta_hbm,
    decay_down_hbm,
    gate_down_hbm,
    decay_up_hbm,
    gate_up_hbm,
    states_hbm,
    output_hbm,
    hidden_ref,
    keep_ref,
    send_ref,
    one_ref,
    two_ref,
    dec_ref,
    inputs_ref,
    beta_ref,
    decay_down_ref,
    gate_down_ref,
    decay_up_ref,
    gate_up_ref,
    states_ref,
    output_ref,
    by_share,
    summed_ref,
    sems,
):
    shares, rows, share = by_share.shape
    grp = lax.axis_index("grp")
    pairs = [
        (one_hbm, one_ref),
        (two_hbm, two_ref),
        (dec_hbm, dec_ref),
        (inputs_hbm.at[1], inputs_ref.at[1]),
        (beta_hbm, beta_ref),
        (decay_down_hbm, decay_down_ref),
        (gate_down_hbm, gate_down_ref),
        (decay_up_hbm, decay_up_ref),
        (gate_up_hbm, gate_up_ref),
        (inputs_hbm.at[0], inputs_ref.at[0]),
        (states_hbm, states_ref),
        (inputs_hbm.at[2], inputs_ref.at[2]),
        (output_hbm, output_ref),
    ]
    loads = [pltpu.make_async_copy(a, b, sems.at[i]) for i, (a, b) in enumerate(pairs)]
    for load in loads:
        load.start()
    for load in loads[:3]:
        load.wait()
    hidden = dec_ref[...].astype(f32) + (
        one_ref[...].astype(f32) + two_ref[...].astype(f32)
    )
    for g in range(shares):
        by_share[g] = hidden[:, g * share : (g + 1) * share]
    hidden_ref[...] = by_share[grp]
    kin = norm_rows(hidden).astype(bf16)
    loads[3].wait()
    all_keys = dot_nn(kin, inputs_ref[1])
    for load in loads[4:9]:
        load.wait()
    beta = jax.nn.sigmoid(dot_nt(kin, beta_ref[...]))
    decay_low = dot_nn(kin, decay_down_ref[...]).astype(bf16)
    rises = jax.nn.softplus(dot_nn(decay_low, decay_up_ref[...]))
    gate_low = dot_nn(kin, gate_down_ref[...]).astype(bf16)
    gates = jax.nn.sigmoid(dot_nn(gate_low, gate_up_ref[...]))
    loads[9].wait()
    all_queries = dot_nn(kin, inputs_ref[0])
    loads[10].wait()
    held_states = [states_ref[:, r].astype(f32) for r in range(requests)]
    steps = rows // requests
    piece = held_states[0].shape[1] // heads
    at = lambda values, t: values[t * requests : (t + 1) * requests]
    along = lambda a, b: jnp.sum(a * b, axis=-1, keepdims=True)
    ready = []
    for head in range(heads):
        lanes = slice(head * DK, (head + 1) * DK)
        q = unit_rows(all_queries[:, lanes]) * DK ** (-0.5)
        k = unit_rows(all_keys[:, lanes])
        rate = jnp.exp(jnp.full((1, DK), rate_ref[head], f32))
        a = jnp.exp(-rate * rises[:, lanes])
        vectors = []
        kept = None
        for t in range(steps):
            kept = at(a, t) if kept is None else kept * at(a, t)
            vectors += [kept * at(k, t), kept * at(q, t)]
        vectors = jnp.concatenate(vectors, axis=0)
        high = vectors.astype(bf16).astype(f32)
        both = jnp.concatenate([high, vectors - high], axis=0)
        owner = lax.rem(lax.broadcasted_iota(jnp.int32, (both.shape[0], 1), 0), requests)
        spread = jnp.concatenate(
            [jnp.where(owner == r, both, 0.0) for r in range(requests)], axis=-1
        ).astype(bf16)
        facing = jnp.concatenate(
            [
                held_states[r][:, head * piece : (head + 1) * piece].reshape(DV, DK)
                for r in range(requests)
            ],
            axis=-1,
        ).astype(bf16)
        met = dot_nt(spread, facing)
        ready.append((q, k, a, met[: vectors.shape[0]] + met[vectors.shape[0] :]))
    loads[11].wait()
    all_values = dot_nn(kin, inputs_ref[2])
    blended = []
    for head in range(heads):
        lanes = slice(head * DK, (head + 1) * DK)
        q, k, a, met = ready[head]
        v = all_values[:, lanes]
        b = beta[:, head : head + 1]
        carried = []
        reads = []
        for t in range(steps):
            seen = at(met, 2 * t)
            read = at(met, 2 * t + 1)
            carried = [(u, w * at(a, t)) for u, w in carried]
            for u, w in carried:
                seen = seen + u * along(w, at(k, t))
            u = at(b, t) * (at(v, t) - seen)
            carried.append((u, at(k, t)))
            for u, w in carried:
                read = read + u * along(w, at(q, t))
            reads.append(read)
        read = jnp.concatenate(reads, axis=0)
        blended.append(norm_rows(read) * gates[:, lanes])
    mixed = jnp.concatenate(blended, axis=-1).astype(bf16)
    loads[12].wait()
    summed = dot_nn(mixed, output_ref[...])
    for g in range(shares):
        summed_ref[g] = summed[:, g * share : (g + 1) * share]
    core = lax.rem(grp, 2)
    for by in range(shares // 2):
        pair = 2 * lax.rem(grp // 2 + by, shares // 2)
        keep_ref[by] = summed_ref[pair + core]
        send_ref[by] = summed_ref[pair + 1 - core].astype(bf16)


def kda(shares, rate, *operands):
    dec, beta_t, states = operands[2], operands[4], operands[9]
    rows, width = dec.shape
    heads = beta_t.shape[0]
    requests = states.shape[1]
    share = width // shares
    sides = shares // 2
    vmem = pl.BlockSpec(memory_space=pltpu.VMEM)
    return pl.pallas_call(
        functools.partial(kda_kernel, heads, requests),
        in_specs=[pl.BlockSpec(memory_space=pltpu.SMEM)]
        + [pl.BlockSpec(memory_space=pltpu.HBM)] * len(operands),
        out_specs=(vmem, vmem, vmem),
        out_shape=(
            jax.ShapeDtypeStruct((rows, share), f32),
            jax.ShapeDtypeStruct((sides, rows, share), f32),
            jax.ShapeDtypeStruct((sides, rows, share), bf16),
        ),
        scratch_shapes=[pltpu.VMEM(a.shape, a.dtype) for a in operands]
        + [
            pltpu.VMEM((shares, rows, share), f32),
            pltpu.VMEM((shares, rows, share), f32),
            pltpu.SemaphoreType.DMA((len(operands) + 2,)),
        ],
        compiler_params=params(),
    )(rate, *operands)


def shards(
    x_group,
    decode_input,
    prompt_len,
    latent_pages,
    slot_target,
    page_counts,
    kda_state,
    query_proj,
    latent_proj,
    key_expand,
    value_expand,
    mla_output,
    kda_inputs,
    kda_beta,
    decay_down,
    decay_up,
    gate_down,
    gate_up,
    decay_log,
    kda_output,
):
    seq_index = lax.axis_index("seq")
    grp_index = lax.axis_index("grp")
    seq_size = lax.axis_size("seq")
    grp_size = lax.axis_size("grp")
    rows, width = x_group.shape
    steps, requests, _ = decode_input.shape
    decode_rows = steps * requests
    share = width // grp_size
    dec = decode_input.reshape(decode_rows, width)

    own_tokens = slice_pages(latent_pages[0], grp_size)
    _, slots, tokens, _ = own_tokens.shape
    core = grp_index % 2
    target = lax.dynamic_slice_in_dim(slot_target[:, 0, :], core * slots, slots, 1)
    owner = target // MAXP
    lengths = jnp.sum(
        jnp.where(owner[..., None] == jnp.arange(requests), prompt_len, 0), axis=-1
    )
    held = core * slots + jnp.arange(slots)[None, :] < page_counts
    token_pos = (
        ((target % MAXP) * PAGE + (grp_index // 2) * tokens)[..., None] + jnp.arange(tokens)
    )
    key_owner = jnp.where(
        held[..., None] & (token_pos < lengths[..., None]), owner[..., None], -1
    ).reshape(1, -1)

    x_rows, _ = lax.optimization_barrier((x_group, own_tokens))
    reach = max(rows, MAXP * PAGE + steps)
    fine = rope_tables(range(-(-reach // 8) * 8))
    coarse = rope_tables([rows * i for i in range(seq_size)])
    own_latent, fresh, q_decode = front(
        prompt_len, fine, coarse, x_rows, dec, latent_proj.T, query_proj, key_expand
    )
    sides = grp_size // 2

    def shift(value, by):
        return lax.ppermute(
            value, "grp", [(g, (g + 2 * by) % grp_size) for g in range(grp_size)]
        )

    def swap(value):
        return lax.ppermute(value, "grp", [(g, g ^ 1) for g in range(grp_size)])

    arrived = lax.all_to_all(own_tokens, "seq", split_axis=0, concat_axis=0, tiled=True)
    queries = [q_decode] + [shift(q_decode, by) for by in range(1, sides)]
    own_latent, _, _, key_owner = lax.optimization_barrier(
        (own_latent, arrived, queries[1], key_owner)
    )
    mine = lax.all_to_all(own_latent, "seq", split_axis=0, concat_axis=0, tiled=True)
    page_keys = arrived.reshape(-1, WIDE)
    queries = queries + [swap(q) for q in queries]
    keep, send = pages_attend(
        queries, page_keys, fresh, key_owner, decode_rows, requests
    )
    merged = merge_pair(keep, swap(send))
    x_again, _ = lax.optimization_barrier((x_group, merged[1]))
    q_prefill, state_rows = prefill_queries(
        fine, coarse, x_again, query_proj, kda_state.reshape(kda_state.shape[0], -1, DK)
    )
    partial = [merged[0]] + [shift(merged[by], -by) for by in range(1, sides)]
    partial[0], _ = lax.optimization_barrier((partial[0], q_prefill))
    mla_part = combine(partial, value_expand, mla_output)
    add = lambda one, two: one.astype(f32) + two.astype(f32)
    trade = lambda value, bits: lax.ppermute(
        value, "grp", [(g, g ^ bits) for g in range(grp_size)]
    )
    mla_pair = add(mla_part, swap(mla_part)).astype(bf16)
    mla_near = trade(mla_pair, 2)
    mine, _ = lax.optimization_barrier((mine, mla_pair))
    state_rows, _ = lax.optimization_barrier((state_rows, mine))
    states = lax.all_to_all(
        state_rows, "seq", split_axis=0, concat_axis=0, tiled=True
    ).reshape((seq_size, requests) + state_rows.shape[1:])
    mla_half = add(mla_pair, mla_near).astype(bf16)
    mla_rest = trade(mla_half, 6)

    prefill_part = prefill_attend(
        q_prefill, mine, swap(mine), key_expand, value_expand, mla_output, grp_size
    )
    mla_half, mla_rest, prefill_part = lax.optimization_barrier(
        (mla_half, mla_rest, prefill_part)
    )
    prefill_parts = lax.all_to_all(
        prefill_part, "grp", split_axis=0, concat_axis=0, tiled=True
    )
    own_columns = lax.dynamic_slice_in_dim(x_group, grp_index * share, share, 1)

    hidden_share, keep, send = kda(
        grp_size,
        decay_log,
        mla_half,
        mla_rest,
        dec,
        kda_inputs.transpose(1, 0, 2),
        kda_beta.T,
        decay_down,
        gate_down,
        decay_up,
        gate_up,
        states,
        kda_output,
    )
    crossing = swap(send)
    kda_sides = [keep[by] + crossing[by].astype(f32) for by in range(sides)]
    kda_sides[0] = kda_sides[0] + hidden_share
    for by in range(1, sides):
        kda_sides[by] = shift(kda_sides[by].astype(bf16), by)
    prefill_out, decode_out = gather_share(prefill_parts, own_columns, *kda_sides)
    return (prefill_out.T, decode_out.reshape(steps, requests, share))


def solution(mesh):
    in_specs = (
        P("seq", None),
        P(None, "seq", None),
        P("seq"),
        P("seq", None, None, None, None),
        P(None, "seq", None),
        P(None, "seq"),
        P(None, "grp", "seq", None),
        P(None, "grp"),
        P(),
        P(None, "grp"),
        P(None, "grp"),
        P("grp", None),
        P(None, None, "grp"),
        P(None, "grp"),
        P(),
        P(None, "grp"),
        P(),
        P(None, "grp"),
        P("grp"),
        P("grp", None),
    )
    out_specs = (P("seq", "grp"), P(None, "seq", "grp"))
    return jax.shard_map(shards, mesh=mesh, in_specs=in_specs, out_specs=out_specs, check_vma=False)
```
